32 devices in a mesh: dp: 8 (over y, x, core), tensor: 4 (over z).
Axes of the slice: x: 2, y: 2, z: 4, core: 2. Of those that a mesh axis runs over, the one named last changes fastest.
Arguments:
- inputs: bfloat16 [2, 8192, 1024], P(None, ('dp', 'tensor')), may hold values from -6 to 6
- query_weight: bfloat16 [1024, 1024], P('dp', 'tensor'), may hold values from -0.1875 to 0.1875
- query_bias: float32 [1024], P('tensor'), may hold values from -3 to 3
- key_weight: bfloat16 [1024, 1024], P('dp', 'tensor'), may hold values from -0.1875 to 0.1875
- value_weight: bfloat16 [1024, 1024], P('dp', 'tensor'), may hold values from -0.1875 to 0.1875
- value_bias: float32 [1024], P('tensor'), may hold values from -3 to 3
- out_weight: bfloat16 [1024, 1024], P('tensor', 'dp'), may hold values from -4 to 4
- out_bias: float32 [1024], replicated, may hold values from -3 to 3
- first_gain: float32 [1024], replicated, may hold values from 0.5 to 1.5
- first_shift: float32 [1024], replicated, may hold values from -2 to 2
- up_weight: bfloat16 [1024, 4096], P('dp', 'tensor'), may hold values from -0.1875 to 0.1875
- up_bias: float32 [4096], P('tensor'), may hold values from -3 to 3
- down_weight: bfloat16 [4096, 1024], P('tensor', 'dp'), may hold values from -0.09375 to 0.09375
- down_bias: float32 [1024], replicated, may hold values from -3 to 3
- second_gain: float32 [1024], replicated, may hold values from 0.5 to 1.5
- second_shift: float32 [1024], replicated, may hold values from -2 to 2
- cotangent: bfloat16 [2, 8192, 1024], P(None, ('dp', 'tensor')), may hold values from -6 to 6
Outputs:
- outputs: bfloat16 [2, 8192, 1024], P(None, ('dp', 'tensor'))
- input_grad: float32 [2, 8192, 1024], P(None, ('dp', 'tensor'))
- query_weight_grad: float32 [1024, 1024], P('dp', 'tensor')
- query_bias_grad: float32 [1024], P('tensor')
- key_weight_grad: float32 [1024, 1024], P('dp', 'tensor')
- value_weight_grad: float32 [1024, 1024], P('dp', 'tensor')
- value_bias_grad: float32 [1024], P('tensor')
- out_weight_grad: float32 [1024, 1024], P('tensor', 'dp')
- out_bias_grad: float32 [1024], replicated
- first_gain_grad: float32 [1024], replicated
- first_shift_grad: float32 [1024], replicated
- up_weight_grad: float32 [1024, 4096], P('dp', 'tensor')
- up_bias_grad: float32 [4096], P('tensor')
- down_weight_grad: float32 [4096, 1024], P('tensor', 'dp')
- down_bias_grad: float32 [1024], replicated
- second_gain_grad: float32 [1024], replicated
- second_shift_grad: float32 [1024], replicated
The draws below stay inside these ranges and needn't reach their ends.
All inputs are finite; a program needn't handle non-finite values.
Results may differ from the reference program's by a relative error of at most 0.017.
Values may be sent and summed in bfloat16 or wider, within the bound.
A program may use at most 192 MiB of HBM per device.

```python
import jax
import jax.numpy as jnp
from jax import lax

D = 1024
HEADS = 16
HD = 64
FF = 4096
LEN = 1024
MICRO = 2
TOKENS_MB = 8192


def with_spikes(values, stream_key, source, target, parts, factor):
    def block_of(dim):
        return (jnp.arange(values.shape[dim]) // (values.shape[dim] // parts)).reshape((-1,) + (1,) * (values.ndim - 1 - dim))

    near = jax.random.permutation(stream_key, parts)[block_of(target)]
    second = (block_of(target) + parts // 2) % parts
    return jnp.where((block_of(source) == near) | (block_of(source) == second), factor * values, values)


def steps_of(stream_key, extent, pieces, low, largest):
    level = 1.0
    for dim, parts in pieces:
        heights = jax.random.uniform(jax.random.fold_in(jax.random.fold_in(stream_key, 6), dim), (parts,), jnp.float32, low / len(pieces), largest / len(pieces))
        level = level * jnp.repeat(jnp.exp(heights), extent[dim] // parts).reshape((-1,) + (1,) * (len(extent) - 1 - dim))
    return level


def scatter_about(key, shape, scale, bound, cuts=(), held_as=jnp.bfloat16):
    values = jax.random.normal(key, shape, jnp.float32) * scale
    if len(cuts) > 0:
        values = steps_of(key, shape, cuts, -0.22, 0.18) * values
    return jnp.clip(values, min=-bound, max=bound).astype(held_as)


def bell_draw_with(key, extent, deviation, limit, cuts, heavy, kind=jnp.bfloat16):
    values = deviation * jax.random.normal(key, extent, jnp.float32)
    if cuts:
        values = values * steps_of(key, extent, cuts, -0.22, 0.18)
    return jnp.clip(with_spikes(values, jax.random.fold_in(key, 3), *heavy), -limit, limit).astype(kind)


def setup_inputs(seed: int = 0) -> dict:
    seeds = jax.random.split(jax.random.key(seed), 18)
    return {
        "inputs": bell_draw_with(seeds[0], (MICRO, TOKENS_MB, D), 1.0, 6.0, ((1, 32),), (1, 2, 32, 2.75)),
        "query_weight": scatter_about(seeds[1], (D, D), D ** -0.5, 0.1875, ((0, 8), (1, 4))),
        "query_bias": scatter_about(seeds[2], (D,), 0.5, 3.0, ((0, 4),), jnp.float32),
        "key_weight": scatter_about(seeds[3], (D, D), D ** -0.5, 0.1875, ((0, 8), (1, 4))),
        "value_weight": scatter_about(seeds[4], (D, D), D ** -0.5, 0.1875, ((0, 8), (1, 4))),
        "value_bias": scatter_about(seeds[5], (D,), 0.5, 3.0, ((0, 4),), jnp.float32),
        "out_weight": scatter_about(seeds[6], (D, D), 2 ** -0.5, 4.0, ((0, 4), (1, 8))),
        "out_bias": scatter_about(seeds[7], (D,), 0.5, 3.0, (), jnp.float32),
        "first_gain": jnp.clip(1.0 + 0.1 * jax.random.normal(seeds[8], (D,), jnp.float32), 0.5, 1.5),
        "first_shift": scatter_about(seeds[9], (D,), 0.3, 2.0, (), jnp.float32),
        "up_weight": scatter_about(seeds[10], (D, FF), D ** -0.5, 0.1875, ((0, 8), (1, 4))),
        "up_bias": scatter_about(seeds[11], (FF,), 0.5, 3.0, ((0, 4),), jnp.float32),
        "down_weight": scatter_about(seeds[12], (FF, D), FF ** -0.5, 0.09375, ((0, 4), (1, 8))),
        "down_bias": scatter_about(seeds[13], (D,), 0.5, 3.0, (), jnp.float32),
        "second_gain": jnp.clip(1.0 + 0.1 * jax.random.normal(seeds[14], (D,), jnp.float32), 0.5, 1.5),
        "second_shift": scatter_about(seeds[15], (D,), 0.3, 2.0, (), jnp.float32),
        "cotangent": bell_draw_with(seeds[16], (MICRO, TOKENS_MB, D), 1.0, 6.0, ((1, 32),), (1, 2, 32, 2.75)),
    }


@jax.custom_vjp
def low(v):
    return lax.optimization_barrier(v.astype(jnp.bfloat16)).astype(jnp.float32)

@jax.custom_vjp
def low_back(v):
    return v

def low_keep(v):
    return (low(v), None)

def low_pass(kept, grad):
    return (grad,)

def back_keep(v):
    return (v, None)

def back_low(kept, grad):
    return (low(grad),)
low.defvjp(low_keep, low_pass)
low_back.defvjp(back_keep, back_low)
EPSILON = 1e-05

def product(left, right):
    return jnp.dot(left, right, precision=lax.Precision.HIGHEST)

def rounded(value):
    return low(low_back(value))

def normalize(hidden, gain, shift):
    average = lax.optimization_barrier(jnp.mean(hidden, axis=-1, keepdims=True))
    center = hidden - average
    spread = lax.optimization_barrier(jnp.mean(center * center, axis=-1, keepdims=True))
    return center * lax.rsqrt(spread + EPSILON) * gain + shift

def attend(block):
    query, keys, values = block
    scores = low_back(jnp.einsum('qhd,khd->hqk', query, keys, precision=lax.Precision.HIGHEST))
    top = lax.optimization_barrier(jnp.max(scores, axis=-1, keepdims=True))
    expo = jnp.exp(scores - top)
    weights = expo / lax.optimization_barrier(jnp.sum(expo, axis=-1, keepdims=True))
    return jnp.einsum('hqk,khd->qhd', low(weights), values, precision=lax.Precision.HIGHEST)

def layer(params, source):
    query_weight, query_bias, key_weight, value_weight, value_bias, out_weight, out_bias, first_gain, first_shift, up_weight, up_bias, down_weight, down_bias, second_gain, second_shift = params
    number = source.shape[0] // LEN
    query = rounded((product(source, query_weight) + query_bias) * HD ** (-0.5))
    keys = rounded(product(source, key_weight))
    values = rounded(product(source, value_weight) + value_bias)
    shape = (number, LEN, HEADS, HD)
    mixed = lax.map(jax.checkpoint(attend), (query.reshape(shape), keys.reshape(shape), values.reshape(shape)))
    mixed = rounded(mixed.reshape(source.shape[0], HEADS * HD))
    first = normalize(source + low_back(product(mixed, out_weight)) + out_bias, first_gain, first_shift)
    upper = low_back(product(low(first), up_weight) + up_bias)
    gated = low(jax.nn.gelu(upper, approximate=False))
    return normalize(first + low_back(product(gated, down_weight)) + down_bias, second_gain, second_shift)

def reference(inputs, query_weight, query_bias, key_weight, value_weight, value_bias, out_weight, out_bias, first_gain, first_shift, up_weight, up_bias, down_weight, down_bias, second_gain, second_shift, cotangent):
    source = inputs.astype(jnp.float32).reshape(-1, inputs.shape[-1])
    params = tuple((entry.astype(jnp.float32) for entry in (query_weight, query_bias, key_weight, value_weight, value_bias, out_weight, out_bias, first_gain, first_shift, up_weight, up_bias, down_weight, down_bias, second_gain, second_shift)))
    result, backward = jax.vjp(layer, params, source)
    grads, input_grad = backward(cotangent.astype(jnp.float32).reshape(result.shape))
    shape = inputs.shape
    return (result.astype(jnp.bfloat16).reshape(shape), input_grad.reshape(shape), grads[0], grads[1], grads[2], grads[3], grads[4], grads[5], grads[6], grads[7], grads[8], grads[9], grads[10], grads[11], grads[12], grads[13], grads[14])
```

```python
import functools
import math

import jax
import jax.numpy as jnp
import numpy as np
from jax import lax
from jax.experimental import pallas as pl
from jax.experimental.pallas import tpu as pltpu
from jax.sharding import PartitionSpec as P

HD = 64
LEN = 1024
EPSILON = 1e-05
SCALE = HD ** (-0.5)
LOG2E = math.log2(math.e)
BF = jnp.bfloat16
F32 = jnp.float32
AXES = ("dp", "tensor")
MIB = 1 << 20


def dot_nn(left, right):
    return jnp.dot(left, right, preferred_element_type=F32)


def dot_nt(left, right):
    return lax.dot_general(left, right, (((1,), (1,)), ((), ())), preferred_element_type=F32)


def dot_tn(left, right):
    return lax.dot_general(left, right, (((0,), (0,)), ((), ())), preferred_element_type=F32)


def joined(refs, pick=None):
    parts = []
    for ref in refs:
        value = ref[...] if pick is None else ref[:, :, pick]
        parts.append(value.reshape(-1, value.shape[-1]))
    return parts[0] if len(parts) == 1 else jnp.concatenate(parts, axis=0)


def call(kernel, grid, in_specs, out_specs, out_shape, scratch, flops, moved, limit=48, exps=0):
    return pl.pallas_call(
        kernel,
        grid=grid,
        in_specs=in_specs,
        out_specs=out_specs,
        out_shape=out_shape,
        scratch_shapes=scratch,
        compiler_params=pltpu.CompilerParams(vmem_limit_bytes=limit * MIB),
        cost_estimate=pl.CostEstimate(flops=flops, bytes_accessed=moved, transcendentals=exps),
    )


def whole_spec(shape):
    return pl.BlockSpec(shape, lambda *_: (0,) * len(shape))


def row_tile(rows):
    return min(rows, 512)


def qkv_kernel(count, x_ref, *refs):
    w_refs, bias_ref, out_ref = refs[:count], refs[count], refs[count + 1]
    acc = dot_nn(x_ref[...], joined(w_refs))
    scale = jnp.where(pl.program_id(0) == 0, SCALE, 1.0)
    out_ref[0] = ((acc + bias_ref[0]) * scale).astype(BF)


def project_qkv(x, slots, bias):
    rows, width = x.shape
    parts, cols = slots[0].shape[1], slots[0].shape[-1]
    specs = [
        pl.BlockSpec((s.shape[0], 1, 1, s.shape[3], cols), lambda w, z: (0, z, w, 0, 0)) for s in slots
    ]
    return call(
        functools.partial(qkv_kernel, len(slots)),
        (3, parts),
        [whole_spec(x.shape)] + specs + [pl.BlockSpec((1, 1, cols), lambda w, z: (w, 0, z))],
        pl.BlockSpec((1, rows, cols), lambda w, z: (w, 0, z)),
        jax.ShapeDtypeStruct((3, rows, parts * cols), BF),
        [],
        2 * rows * width * 3 * parts * cols,
        2 * (rows * width * 4 + 3 * width * parts * cols),
    )(x, *slots, bias)


def plain_kernel(count, x_ref, *refs):
    w_refs, out_ref = refs[:count], refs[count]
    out_ref[...] = dot_nn(x_ref[...], joined(w_refs)).astype(BF)


def project_back(x, slots, which):
    rows, width = x.shape
    parts, cols = slots[0].shape[1], slots[0].shape[-1]
    specs = [
        pl.BlockSpec((s.shape[0], 1, 1, s.shape[3], cols), lambda z: (0, z, which, 0, 0)) for s in slots
    ]
    return call(
        functools.partial(plain_kernel, len(slots)),
        (parts,),
        [whole_spec(x.shape)] + specs,
        pl.BlockSpec((rows, cols), lambda z: (0, z)),
        jax.ShapeDtypeStruct((rows, parts * cols), BF),
        [],
        2 * rows * width * parts * cols,
        2 * (rows * width * 2 + width * parts * cols),
    )(x, *slots)


def attend_kernel(count, q_ref, *refs):
    k_refs, v_refs, m_ref, l_ref = refs[:count], refs[count : 2 * count], refs[-2], refs[-1]
    factor = LOG2E
    mixed = []
    for head in range(q_ref.shape[-1] // HD):
        cols = slice(head * HD, head * HD + HD)
        q = q_ref[0][:, cols]
        scores = [dot_nt(k[0][:, cols], q) for k in k_refs]
        top = functools.reduce(jnp.maximum, [jnp.max(s, axis=0, keepdims=True) for s in scores])
        base = top * factor
        expo = [jnp.exp2(s * factor - base) for s in scores]
        total = functools.reduce(jnp.add, [jnp.sum(e, axis=0, keepdims=True) for e in expo])
        inverse = 1.0 / total
        mixed.append(
            functools.reduce(
                jnp.add, [dot_tn((e * inverse).astype(BF), v[0][:, cols]) for e, v in zip(expo, v_refs)]
            )
        )
        l_ref[0, 0, head : head + 1, :] = base + jnp.log2(total)
    m_ref[...] = jnp.concatenate(mixed, axis=1).astype(BF)


def attend_forward(qkv, other):
    _, rows, width = qkv.shape
    span = min(rows, LEN)
    number = rows // span
    pairs = width // (2 * HD)
    one = lambda place: pl.BlockSpec((1, span, 2 * HD), lambda n, h: (place, n, h))
    sources = [qkv] if other is None else [qkv, other]
    keys = [one(1)] + ([one(0)] if other is not None else [])
    values = [one(2)] + ([one(1)] if other is not None else [])
    count = len(sources)
    return call(
        functools.partial(attend_kernel, count),
        (number, pairs),
        [one(0)] + keys + values,
        (
            pl.BlockSpec((span, 2 * HD), lambda n, h: (n, h)),
            pl.BlockSpec((1, 1, 2, span), lambda n, h: (n, h, 0, 0)),
        ),
        (
            jax.ShapeDtypeStruct((rows, width), BF),
            jax.ShapeDtypeStruct((number, pairs, 2, span), F32),
        ),
        [],
        4 * rows * LEN * width * 4,
        2 * rows * width * 6,
        exps=rows * LEN * (width // HD),
    )(qkv, *sources, *sources)


def attend_back_kernel(count, q_ref, *refs):
    k_refs, v_refs = refs[:count], refs[count : 2 * count]
    dm_ref, l_ref, dq_ref = refs[2 * count : 2 * count + 3]
    out_refs = refs[2 * count + 3 :]
    dqs, dks, dvs = [], [[] for _ in range(count)], [[] for _ in range(count)]
    for head in range(q_ref.shape[-1] // HD):
        cols = slice(head * HD, head * HD + HD)
        q = q_ref[0][:, cols]
        dm = dm_ref[...][:, cols]
        base = l_ref[0, 0, head : head + 1, :]
        weights = [jnp.exp2(dot_nt(k[0][:, cols], q) * LOG2E - base) for k in k_refs]
        grads = [dot_nt(v[0][:, cols], dm) for v in v_refs]
        inner = functools.reduce(
            jnp.add, [jnp.sum(w * g, axis=0, keepdims=True) for w, g in zip(weights, grads)]
        )
        dq = None
        for i in range(count):
            ds = (weights[i] * (grads[i] - inner)).astype(BF)
            part = dot_tn(ds, k_refs[i][0][:, cols])
            dq = part if dq is None else dq + part
            dks[i].append(dot_nn(ds, q))
            dvs[i].append(dot_nn(weights[i].astype(BF), dm))
        dqs.append(dq)
    dq_ref[...] = (jnp.concatenate(dqs, axis=1).astype(BF).astype(F32) * SCALE).astype(BF)
    for i in range(count):
        out_refs[i][0] = jnp.concatenate(dks[i], axis=1).astype(out_refs[i].dtype)
        out_refs[i][1] = jnp.concatenate(dvs[i], axis=1).astype(out_refs[i].dtype)


def attend_backward(qkv, other, dm, logs):
    _, rows, width = qkv.shape
    span = min(rows, LEN)
    number = rows // span
    pairs = width // (2 * HD)
    one = lambda place: pl.BlockSpec((1, span, 2 * HD), lambda n, h: (place, n, h))
    flat = pl.BlockSpec((span, 2 * HD), lambda n, h: (n, h))
    both = pl.BlockSpec((2, span, 2 * HD), lambda n, h: (0, n, h))
    sources = [qkv] if other is None else [qkv, other]
    keys = [one(1)] + ([one(0)] if other is not None else [])
    values = [one(2)] + ([one(1)] if other is not None else [])
    count = len(sources)
    outs = [jax.ShapeDtypeStruct((2, rows, width), F32 if other is not None else BF)]
    if other is not None:
        outs.append(jax.ShapeDtypeStruct((2, rows, width), BF))
    return call(
        functools.partial(attend_back_kernel, count),
        (number, pairs),
        [one(0)] + keys + values + [flat, pl.BlockSpec((1, 1, 2, span), lambda n, h: (n, h, 0, 0))],
        tuple([flat] + [both] * count),
        tuple([jax.ShapeDtypeStruct((rows, width), BF)] + outs),
        [],
        10 * rows * LEN * width * 4,
        2 * rows * width * 12,
        exps=rows * LEN * (width // HD),
    )(qkv, *sources, *sources, dm, logs)


OUT_BIAS, FIRST_GAIN, FIRST_SHIFT, DOWN_BIAS, SECOND_GAIN, SECOND_SHIFT = range(6)


def vector(ref, place):
    return ref[place : place + 1, :]


def normed(hidden):
    average = jnp.mean(hidden, axis=-1, keepdims=True)
    center = hidden - average
    spread = jnp.mean(center * center, axis=-1, keepdims=True)
    inverse = lax.rsqrt(spread + EPSILON)
    return center * inverse, inverse


def norm_back(grad, z, inverse, gain):
    scaled = grad * gain
    average = jnp.mean(scaled, axis=-1, keepdims=True)
    along = jnp.mean(scaled * z, axis=-1, keepdims=True)
    return (scaled - average - z * along) * inverse


def total_rows(value):
    return jnp.sum(value, axis=0, keepdims=True)


def add_sums(ref, first, rows):
    value = jnp.concatenate(rows + [jnp.zeros((8 - len(rows), rows[0].shape[1]), F32)], axis=0)

    @pl.when(first)
    def _():
        ref[...] = value

    @pl.when(jnp.logical_not(first))
    def _():
        ref[...] += value


def accumulate(acc_ref, step, value):
    @pl.when(step == 0)
    def _():
        acc_ref[...] = value

    @pl.when(step > 0)
    def _():
        acc_ref[...] += value


def first_norm_kernel(count, m_ref, *refs):
    w_refs = refs[:count]
    x_ref, vec_ref, z_ref, r_ref, y_ref, acc_ref = refs[count:]
    step = pl.program_id(1)
    accumulate(acc_ref, step, dot_nt(m_ref[...], joined(w_refs)))

    @pl.when(step == pl.num_programs(1) - 1)
    def _():
        hidden = x_ref[...].astype(F32) + acc_ref[...] + vector(vec_ref, OUT_BIAS)
        z, inverse = normed(hidden)
        z_ref[...] = z
        r_ref[...] = inverse
        y_ref[...] = (z * vector(vec_ref, FIRST_GAIN) + vector(vec_ref, FIRST_SHIFT)).astype(BF)


def first_norm(mixed, slots, x, vectors):
    rows, width = x.shape
    tile = row_tile(rows)
    parts, cols = slots[0].shape[1], slots[0].shape[-1]
    specs = [
        pl.BlockSpec((s.shape[0], 1, 1, s.shape[3], cols), lambda i, z: (0, z, 3, 0, 0)) for s in slots
    ]
    flat = pl.BlockSpec((tile, width), lambda i, z: (i, 0))
    return call(
        functools.partial(first_norm_kernel, len(slots)),
        (rows // tile, parts),
        [pl.BlockSpec((tile, cols), lambda i, z: (i, z))] + specs + [flat, whole_spec(vectors.shape)],
        (flat, pl.BlockSpec((tile, 1), lambda i, z: (i, 0)), flat),
        (
            jax.ShapeDtypeStruct((rows, width), F32),
            jax.ShapeDtypeStruct((rows, 1), F32),
            jax.ShapeDtypeStruct((rows, width), BF),
        ),
        [pltpu.VMEM((tile, width), F32)],
        2 * rows * width * width,
        2 * (rows * width * 5 + width * width),
    )(mixed, *slots, x, vectors)


def up_kernel(count, y_ref, *refs):
    w_refs, bias_ref, g_ref, slope_ref = refs[:count], refs[count], refs[count + 1], refs[count + 2]
    upper = dot_nn(y_ref[...], joined(w_refs)) + bias_ref[...]
    half = 0.5 + 0.5 * lax.erf(upper * (0.5**0.5))
    g_ref[...] = (upper * half).astype(BF)
    bell = jnp.exp(upper * upper * -0.5) * ((2 * math.pi) ** -0.5)
    slope_ref[...] = (half + upper * bell).astype(BF)


def up_gelu(y, slots, bias):
    rows, width = y.shape
    parts, full = slots[0].shape[1], slots[0].shape[-1]
    cols = min(512, full)
    per = full // cols
    tile = row_tile(rows)
    specs = [
        pl.BlockSpec((s.shape[0], 1, s.shape[2], cols), lambda i, z: (0, z // per, 0, z % per)) for s in slots
    ]
    out = pl.BlockSpec((tile, cols), lambda i, z: (i, z))
    shape = jax.ShapeDtypeStruct((rows, parts * full), BF)
    return call(
        functools.partial(up_kernel, len(slots)),
        (rows // tile, parts * per),
        [pl.BlockSpec((tile, width), lambda i, z: (i, 0))]
        + specs
        + [pl.BlockSpec((1, cols), lambda i, z: (0, z))],
        (out, out),
        (shape, shape),
        [],
        2 * rows * width * parts * full,
        2 * (rows * width + 2 * rows * parts * full + width * parts * full),
        exps=2 * rows * parts * full,
    )(y, *slots, bias)


def second_norm_kernel(count, g_ref, *refs):
    w_refs = refs[:count]
    z1_ref, c_ref, vec_ref, out_ref, dh_ref, b_ref, sum_ref, acc_ref = refs[count:]
    step = pl.program_id(1)
    first = pl.program_id(0) == 0
    accumulate(acc_ref, step, dot_nt(g_ref[...], joined(w_refs)))

    @pl.when(step == pl.num_programs(1) - 1)
    def _():
        y1 = z1_ref[...] * vector(vec_ref, FIRST_GAIN) + vector(vec_ref, FIRST_SHIFT)
        hidden = y1 + acc_ref[...] + vector(vec_ref, DOWN_BIAS)
        z, inverse = normed(hidden)
        gain = vector(vec_ref, SECOND_GAIN)
        out_ref[...] = (z * gain + vector(vec_ref, SECOND_SHIFT)).astype(BF)
        grad = c_ref[...].astype(F32)
        dh = norm_back(grad, z, inverse, gain)
        dh_ref[...] = dh
        b_ref[...] = dh.astype(BF)
        add_sums(sum_ref, first, [total_rows(grad * z), total_rows(grad), total_rows(dh)])


def second_norm(gated, slots, z1, cot, vectors):
    rows, width = z1.shape
    tile = row_tile(rows)
    parts, cols = slots[0].shape[1], slots[0].shape[-1]
    specs = [pl.BlockSpec((s.shape[0], 1, s.shape[2], cols), lambda i, z: (0, z, 0, 0)) for s in slots]
    flat = pl.BlockSpec((tile, width), lambda i, z: (i, 0))
    return call(
        functools.partial(second_norm_kernel, len(slots)),
        (rows // tile, parts),
        [pl.BlockSpec((tile, cols), lambda i, z: (i, z))]
        + specs
        + [flat, flat, whole_spec(vectors.shape)],
        (flat, flat, flat, whole_spec((8, width))),
        (
            jax.ShapeDtypeStruct((rows, width), BF),
            jax.ShapeDtypeStruct((rows, width), F32),
            jax.ShapeDtypeStruct((rows, width), BF),
            jax.ShapeDtypeStruct((8, width), F32),
        ),
        [pltpu.VMEM((tile, width), F32)],
        2 * rows * width * parts * cols,
        2 * (rows * width * 7 + (rows + width) * parts * cols),
    )(gated, *slots, z1, cot, vectors)


def gate_back_kernel(count, b_ref, *refs):
    w_refs, slope_ref, du_ref, sum_ref = refs[:count], refs[count], refs[count + 1], refs[count + 2]
    grad = dot_nn(b_ref[...], joined(w_refs))
    low = (grad * slope_ref[...].astype(F32)).astype(BF)
    du_ref[...] = low
    value = total_rows(low.astype(F32))
    first = pl.program_id(1) == 0

    @pl.when(first)
    def _():
        sum_ref[...] = value

    @pl.when(jnp.logical_not(first))
    def _():
        sum_ref[...] += value


def gate_back(b, slots, slope):
    rows, width = b.shape
    parts, full = slots[0].shape[1], slots[0].shape[-1]
    cols = min(512, full)
    per = full // cols
    tile = row_tile(rows)
    specs = [
        pl.BlockSpec((s.shape[0], 1, s.shape[2], cols), lambda z, i: (0, z // per, 0, z % per)) for s in slots
    ]
    out = pl.BlockSpec((tile, cols), lambda z, i: (i, z))
    return call(
        functools.partial(gate_back_kernel, len(slots)),
        (parts * per, rows // tile),
        [pl.BlockSpec((tile, width), lambda z, i: (i, 0))] + specs + [out],
        (out, pl.BlockSpec((1, cols), lambda z, i: (0, z))),
        (
            jax.ShapeDtypeStruct((rows, parts * full), BF),
            jax.ShapeDtypeStruct((1, parts * full), F32),
        ),
        [],
        2 * rows * width * parts * full,
        2 * (rows * width + 2 * rows * parts * full + width * parts * full),
    )(b, *slots, slope)


def first_back_kernel(count, du_ref, *refs):
    w_refs = refs[:count]
    dh2_ref, z1_ref, r1_ref, vec_ref, dh_ref, b_ref, sum_ref, acc_ref = refs[count:]
    step = pl.program_id(1)
    first = pl.program_id(0) == 0
    accumulate(acc_ref, step, dot_nt(du_ref[...], joined(w_refs)))

    @pl.when(step == pl.num_programs(1) - 1)
    def _():
        grad = acc_ref[...] + dh2_ref[...]
        z = z1_ref[...]
        dh = norm_back(grad, z, r1_ref[...], vector(vec_ref, FIRST_GAIN))
        dh_ref[...] = dh
        b_ref[...] = dh.astype(BF)
        add_sums(sum_ref, first, [total_rows(grad * z), total_rows(grad), total_rows(dh)])


def first_back(du, slots, dh2, z1, r1, vectors):
    rows, width = z1.shape
    tile = row_tile(rows)
    parts, cols = slots[0].shape[1], slots[0].shape[-1]
    specs = [pl.BlockSpec((s.shape[0], 1, s.shape[2], cols), lambda i, z: (0, z, 0, 0)) for s in slots]
    flat = pl.BlockSpec((tile, width), lambda i, z: (i, 0))
    return call(
        functools.partial(first_back_kernel, len(slots)),
        (rows // tile, parts),
        [pl.BlockSpec((tile, cols), lambda i, z: (i, z))]
        + specs
        + [flat, flat, pl.BlockSpec((tile, 1), lambda i, z: (i, 0)), whole_spec(vectors.shape)],
        (flat, flat, whole_spec((8, width))),
        (
            jax.ShapeDtypeStruct((rows, width), F32),
            jax.ShapeDtypeStruct((rows, width), BF),
            jax.ShapeDtypeStruct((8, width), F32),
        ),
        [pltpu.VMEM((tile, width), F32)],
        2 * rows * width * parts * cols,
        2 * (rows * width * 8 + (rows + width) * parts * cols),
    )(du, *slots, dh2, z1, r1, vectors)


def input_back_kernel(count, dq_ref, dkv_ref, *refs):
    w_refs = refs[:count]
    dh_ref, out_ref, acc_ref = refs[count:]
    step = pl.program_id(1)
    value = dot_nt(dq_ref[...], joined(w_refs, 0))
    value += dot_nt(dkv_ref[0], joined(w_refs, 1))
    value += dot_nt(dkv_ref[1], joined(w_refs, 2))
    accumulate(acc_ref, step, value)

    @pl.when(step == pl.num_programs(1) - 1)
    def _():
        out_ref[...] = (acc_ref[...] + dh_ref[...]).astype(BF)


def input_back(dq, dkv, slots, dh1):
    rows, width = dh1.shape
    tile = row_tile(rows)
    parts, kinds, cols = slots[0].shape[1], slots[0].shape[2], slots[0].shape[-1]
    specs = [
        pl.BlockSpec((s.shape[0], 1, kinds, s.shape[3], cols), lambda i, z: (0, z, 0, 0, 0)) for s in slots
    ]
    flat = pl.BlockSpec((tile, width), lambda i, z: (i, 0))
    return call(
        functools.partial(input_back_kernel, len(slots)),
        (rows // tile, parts),
        [
            pl.BlockSpec((tile, cols), lambda i, z: (i, z)),
            pl.BlockSpec((2, tile, cols), lambda i, z: (0, i, z)),
        ]
        + specs
        + [flat],
        flat,
        jax.ShapeDtypeStruct((rows, width), BF),
        [pltpu.VMEM((tile, width), F32)],
        6 * rows * width * parts * cols,
        2 * (rows * width * 6 + 4 * width * parts * cols),
    )(dq, dkv, *slots, dh1)


def outer_kernel(left_ref, right_ref, out_ref):
    shape = out_ref.shape
    right = right_ref[...].reshape(right_ref.shape[-2:])
    out_ref[...] = dot_tn(left_ref[...], right).astype(BF).reshape(shape)


def outer(left, right, begin, count, depth, parts):
    rows = left.shape[0]
    cols = right.shape[-1] // parts
    return call(
        outer_kernel,
        (parts,),
        [
            pl.BlockSpec((rows, count * depth), lambda z: (0, begin // count)),
            pl.BlockSpec((rows, cols), lambda z: (0, z)),
        ],
        pl.BlockSpec((count, 1, depth, cols), lambda z: (0, z, 0, 0)),
        jax.ShapeDtypeStruct((count, parts, depth, parts * cols // parts), BF),
        [],
        2 * rows * count * depth * parts * cols,
        2 * (rows * (count * depth + parts * cols) + count * depth * parts * cols),
    )(left, right)


def outer_stack(left, stack, begin, count, depth, parts):
    rows = left.shape[0]
    kinds = stack.shape[0]
    cols = stack.shape[-1] // parts
    return call(
        outer_kernel,
        (kinds, parts),
        [
            pl.BlockSpec((rows, count * depth), lambda k, z: (0, begin // count)),
            pl.BlockSpec((1, rows, cols), lambda k, z: (k, 0, z)),
        ],
        pl.BlockSpec((count, 1, 1, depth, cols), lambda k, z: (0, z, k, 0, 0)),
        jax.ShapeDtypeStruct((count, parts, kinds, depth, cols), BF),
        [],
        2 * rows * count * depth * parts * cols * kinds,
        2 * kinds * (rows * (count * depth + parts * cols) + count * depth * parts * cols),
    )(left, stack)


class Links:
    def __init__(self, count, parts):
        self.count, self.parts = count, parts
        self.cube = count == 8
        self.place = lax.axis_index("dp")
        self.core = self.place % 2
        if self.cube:
            masks = [[0, 2, 4, 6, 1, 5, 3, 7], [0, 4, 2, 6, 1, 3, 5, 7]]
        else:
            masks = None
        if masks is None:
            self.owner = jnp.arange(count)
            self.inverse = jnp.arange(count)
        else:
            table = jnp.asarray(masks, jnp.int32)
            back = jnp.asarray([list(np.argsort(m)) for m in masks], jnp.int32)
            self.owner = table[self.core] ^ self.place
            self.inverse = back[self.core][jnp.arange(count) ^ self.place]

    def pairs(self, flip):
        out = []
        for place in range(self.count):
            for z in range(self.parts):
                out.append((place * self.parts + z, flip(place) * self.parts + z))
        return out

    def core_pairs(self):
        return self.pairs(lambda place: place ^ 1)

    def first_pairs(self):
        return self.pairs(lambda place: place ^ (4 if place % 2 else 2))

    def second_pairs(self):
        return self.pairs(lambda place: place ^ (2 if place % 2 else 4))

    def gather(self, local):
        block = lax.all_gather(local, "tensor", axis=0, tiled=False)
        if not self.cube:
            return [lax.all_gather(block, "dp", axis=0, tiled=False)]
        blocks = [block[None]]
        for pairs in (self.first_pairs(), self.second_pairs(), self.core_pairs()):
            blocks = blocks + [lax.ppermute(b, AXES, pairs) for b in blocks]
        return blocks

    def scatter(self, make):
        if not self.cube:
            full = lax.psum_scatter(make(0, self.count), "dp", scatter_dimension=0, tiled=False)
            return lax.psum_scatter(full, "tensor", scatter_dimension=0, tiled=False)
        far = lax.ppermute(make(4, 4), AXES, self.core_pairs())
        held = make(0, 4)
        away = summed(held[2:4], far[2:4])
        held = summed(held[0:2], far[0:2])
        far = lax.ppermute(away, AXES, self.second_pairs())
        away = summed(held[1:2], far[1:2])
        held = summed(held[0:1], far[0:1])
        far = lax.ppermute(away, AXES, self.first_pairs())
        held = summed(held, far)
        return lax.psum_scatter(held[0], "tensor", scatter_dimension=0, tiled=False)

    def row_pairs(self, second):
        half = self.parts // 2
        out = []
        for place in range(self.count):
            for z in range(self.parts):
                micro = (z + second) % 2
                target = (place // 2 * 2 + z // half) * self.parts + micro * half + place % 2
                out.append((place * self.parts + z, target))
        return out

    def rows_in(self, local):
        parity = lax.axis_index("tensor") % 2
        first = lax.dynamic_index_in_dim(local, parity, 0, keepdims=False)
        second = lax.dynamic_index_in_dim(local, 1 - parity, 0, keepdims=False)
        return jnp.concatenate(
            [
                lax.ppermute(first, AXES, self.row_pairs(0)),
                lax.ppermute(second, AXES, self.row_pairs(1)),
            ],
            axis=0,
        )

    def rows_out(self, held):
        parity = lax.axis_index("tensor") % 2
        rows = held.shape[0] // 2
        back = lambda second: [(b, a) for a, b in self.row_pairs(second)]
        first = lax.ppermute(held[:rows], AXES, back(0))
        second = lax.ppermute(held[rows:], AXES, back(1))
        swap = parity == 1
        return jnp.stack([jnp.where(swap, second, first), jnp.where(swap, first, second)])

    def total(self, value):
        step = 1
        while step < self.count:
            pairs = self.pairs(lambda place: place ^ step)
            value = value + lax.ppermute(value, AXES, pairs)
            step *= 2
        step = 1
        while step < self.parts:
            pairs = [
                (p * self.parts + z, p * self.parts + (z ^ step))
                for p in range(self.count)
                for z in range(self.parts)
            ]
            value = value + lax.ppermute(value, AXES, pairs)
            step *= 2
        return value


def summed(left, right):
    return (left.astype(F32) + right.astype(F32)).astype(BF)


def shards(
    inputs,
    query_weight,
    query_bias,
    key_weight,
    value_weight,
    value_bias,
    out_weight,
    out_bias,
    first_gain,
    first_shift,
    up_weight,
    up_bias,
    down_weight,
    down_bias,
    second_gain,
    second_shift,
    cotangent,
):
    count, parts = lax.axis_size("dp"), lax.axis_size("tensor")
    links = Links(count, parts)
    tensor_place = lax.axis_index("tensor")
    width = inputs.shape[-1]
    depth = width // count
    hidden = up_weight.shape[1] * parts

    source = jnp.repeat(links.owner, depth) * depth + jnp.tile(jnp.arange(depth), count)
    shuffle = (jnp.arange(width)[:, None] == source[None, :]).astype(BF)

    def ordered(rows):
        return dot_nn(rows, shuffle).astype(BF)

    def restored(rows):
        return dot_nt(rows, shuffle).astype(BF)

    def restored_vectors(rows):
        return rows.reshape(-1, count, depth)[:, links.inverse].reshape(-1, width)

    vectors = jnp.stack(
        [out_bias, first_gain, first_shift, down_bias, second_gain, second_shift]
        + [jnp.zeros_like(out_bias)] * 2
    )
    vectors = vectors.reshape(8, count, depth)[:, links.owner].reshape(8, width)

    shared = jnp.stack([query_weight, key_weight, value_weight, out_weight.T])
    att_slots = links.gather(shared)
    biases = lax.all_gather(
        jnp.concatenate([query_bias, value_bias, up_bias]), "tensor", axis=0, tiled=False
    )
    local = query_bias.shape[0]
    query_full = biases[:, :local].reshape(1, 1, -1)
    value_full = biases[:, local : 2 * local].reshape(1, 1, -1)
    up_full = biases[:, 2 * local :].reshape(1, -1)
    qkv_bias = jnp.concatenate([query_full, jnp.zeros_like(query_full), value_full], axis=0)
    x = ordered(links.rows_in(inputs))
    up_slots = links.gather(up_weight)
    cot = ordered(links.rows_in(cotangent))
    down_slots = links.gather(down_weight.T)

    qkv = project_qkv(x, att_slots, qkv_bias)
    share = x.shape[0] < LEN
    other = lax.ppermute(qkv[1:], AXES, links.core_pairs()) if share else None
    mixed, logs = attend_forward(qkv, other)
    z1, r1, y1 = first_norm(mixed, att_slots, x, vectors)
    gated, slope = up_gelu(y1, up_slots, up_full)
    out, dh2, b2, second_sums = second_norm(gated, down_slots, z1, cot, vectors)
    outputs = links.rows_out(restored(out))

    down_grad = links.scatter(lambda begin, n: outer(b2, gated, begin, n, depth, parts))
    du, up_bias_sum = gate_back(b2, down_slots, slope)
    up_grad = links.scatter(lambda begin, n: outer(y1, du, begin, n, depth, parts))
    dh1, b1, first_sums = first_back(du, up_slots, dh2, z1, r1, vectors)
    dm = project_back(b1, att_slots, 3)
    out_grad = links.scatter(lambda begin, n: outer(b1, mixed, begin, n, depth, parts))
    back = attend_backward(qkv, other, dm, logs)
    if share:
        dq, near, far = back
        dkv = (near + lax.ppermute(far, AXES, links.core_pairs()).astype(F32)).astype(BF)
    else:
        dq, dkv = back
    dx = input_back(dq, dkv, att_slots, dh1)
    input_grad = links.rows_out(restored(dx)).astype(F32)

    def qkv_outer(begin, n):
        return jnp.concatenate(
            [
                outer_stack(x, dq[None], begin, n, depth, parts),
                outer_stack(x, dkv, begin, n, depth, parts),
            ],
            axis=2,
        )

    qkv_grad = links.scatter(qkv_outer).astype(F32)

    sums = jnp.concatenate(
        [
            restored_vectors(jnp.concatenate([first_sums[:3], second_sums[:3]])),
            up_bias_sum.reshape(-1, width),
            jnp.sum(dq.astype(F32), axis=0, keepdims=True),
            jnp.sum(dkv[1].astype(F32), axis=0, keepdims=True),
        ]
    )
    sums = links.total(sums)
    wide = hidden // width

    def mine(vector_sum):
        size = vector_sum.shape[0] // parts
        return lax.dynamic_slice_in_dim(vector_sum, tensor_place * size, size)

    return (
        outputs,
        input_grad,
        qkv_grad[0],
        mine(sums[6 + wide]),
        qkv_grad[1],
        qkv_grad[2],
        mine(sums[7 + wide]),
        out_grad.astype(F32).T,
        sums[2],
        sums[0],
        sums[1],
        up_grad.astype(F32),
        mine(sums[6 : 6 + wide].reshape(-1)),
        down_grad.astype(F32).T,
        sums[5],
        sums[3],
        sums[4],
    )


def solution(mesh):
    rows = P(None, ("dp", "tensor"), None)
    return jax.shard_map(
        shards,
        mesh=mesh,
        in_specs=(
            rows,
            P("dp", "tensor"),
            P("tensor"),
            P("dp", "tensor"),
            P("dp", "tensor"),
            P("tensor"),
            P("tensor", "dp"),
            P(),
            P(),
            P(),
            P("dp", "tensor"),
            P("tensor"),
            P("tensor", "dp"),
            P(),
            P(),
            P(),
            rows,
        ),
        out_specs=(
            rows,
            rows,
            P("dp", "tensor"),
            P("tensor"),
            P("dp", "tensor"),
            P("dp", "tensor"),
            P("tensor"),
            P("tensor", "dp"),
            P(),
            P(),
            P(),
            P("dp", "tensor"),
            P("tensor"),
            P("tensor", "dp"),
            P(),
            P(),
            P(),
        ),
        check_vma=False,
    )
```

```python
import functools
import math

import jax
import jax.numpy as jnp
import numpy as np
from jax import lax
from jax.experimental import pallas as pl
from jax.experimental.pallas import tpu as pltpu
from jax.sharding import PartitionSpec as P

HD = 64
LEN = 1024
EPSILON = 1e-05
SCALE = HD ** (-0.5)
LOG2E = math.log2(math.e)
BF = jnp.bfloat16
F32 = jnp.float32
AXES = ("dp", "tensor")
MIB = 1 << 20


def dot_nn(left, right):
    return jnp.dot(left, right, preferred_element_type=F32)


def dot_nt(left, right):
    return lax.dot_general(left, right, (((1,), (1,)), ((), ())), preferred_element_type=F32)


def dot_tn(left, right):
    return lax.dot_general(left, right, (((0,), (0,)), ((), ())), preferred_element_type=F32)


def tile_of(ref):
    parts = [ref[i].reshape(-1, ref.shape[-1]) for i in range(ref.shape[0])]
    return parts[0] if len(parts) == 1 else jnp.concatenate(parts, axis=1)


def weight_spec(weights, subs, index):
    _, slots, _, depth, cols = weights.shape

    def place(*grid):
        sub, z = index(*grid)
        return (sub, 0, z, 0, 0)

    return pl.BlockSpec((subs, slots, 1, depth, cols), place)


def call(kernel, grid, in_specs, out_specs, out_shape, scratch, flops, moved, limit=48, exps=0):
    return pl.pallas_call(
        kernel,
        grid=grid,
        in_specs=in_specs,
        out_specs=out_specs,
        out_shape=out_shape,
        scratch_shapes=scratch,
        compiler_params=pltpu.CompilerParams(vmem_limit_bytes=limit * MIB),
        cost_estimate=pl.CostEstimate(flops=flops, bytes_accessed=moved, transcendentals=exps),
    )


def whole_spec(shape):
    return pl.BlockSpec(shape, lambda *_: (0,) * len(shape))


def row_tile(rows):
    return min(rows, 512)


def qkv_kernel(x_ref, w_ref, bias_ref, out_ref):
    acc = dot_nn(x_ref[...], tile_of(w_ref))
    scale = jnp.where(pl.program_id(0) == 0, SCALE, 1.0)
    out_ref[0] = ((acc + bias_ref[0]) * scale).astype(BF)


def project_qkv(x, weights, bias):
    rows, width = x.shape
    parts, cols = weights.shape[2], weights.shape[4]
    return call(
        qkv_kernel,
        (3, parts),
        [
            whole_spec(x.shape),
            weight_spec(weights, 1, lambda w, z: (w, z)),
            pl.BlockSpec((1, 1, cols), lambda w, z: (w, 0, z)),
        ],
        pl.BlockSpec((1, rows, cols), lambda w, z: (w, 0, z)),
        jax.ShapeDtypeStruct((3, rows, parts * cols), BF),
        [],
        2 * rows * width * 3 * parts * cols,
        2 * (rows * width * 4 + 3 * width * parts * cols),
    )(x, weights, bias)


def plain_kernel(x_ref, w_ref, out_ref):
    out_ref[...] = dot_nn(x_ref[...], tile_of(w_ref)).astype(BF)


def project_back(x, weights, which):
    rows, width = x.shape
    parts, cols = weights.shape[2], weights.shape[4]
    return call(
        plain_kernel,
        (parts,),
        [whole_spec(x.shape), weight_spec(weights, 1, lambda z: (which, z))],
        pl.BlockSpec((rows, cols), lambda z: (0, z)),
        jax.ShapeDtypeStruct((rows, parts * cols), BF),
        [],
        2 * rows * width * parts * cols,
        2 * (rows * width * 2 + width * parts * cols),
    )(x, weights)


def attend_kernel(count, q_ref, *refs):
    k_refs, v_refs, m_ref, l_ref = refs[:count], refs[count : 2 * count], refs[-2], refs[-1]
    factor = LOG2E
    mixed = []
    for head in range(q_ref.shape[-1] // HD):
        cols = slice(head * HD, head * HD + HD)
        q = q_ref[0][:, cols]
        scores = [dot_nt(k[0][:, cols], q) for k in k_refs]
        top = functools.reduce(jnp.maximum, [jnp.max(s, axis=0, keepdims=True) for s in scores])
        base = top * factor
        expo = [jnp.exp2(s * factor - base) for s in scores]
        total = functools.reduce(jnp.add, [jnp.sum(e, axis=0, keepdims=True) for e in expo])
        inverse = 1.0 / total
        mixed.append(
            functools.reduce(
                jnp.add, [dot_tn((e * inverse).astype(BF), v[0][:, cols]) for e, v in zip(expo, v_refs)]
            )
        )
        l_ref[0, 0, head : head + 1, :] = base + jnp.log2(total)
    m_ref[...] = jnp.concatenate(mixed, axis=1).astype(BF)


def attend_forward(qkv, other):
    _, rows, width = qkv.shape
    span = min(rows, LEN)
    number = rows // span
    pairs = width // (2 * HD)
    one = lambda place: pl.BlockSpec((1, span, 2 * HD), lambda n, h: (place, n, h))
    sources = [qkv] if other is None else [qkv, other]
    keys = [one(1)] + ([one(0)] if other is not None else [])
    values = [one(2)] + ([one(1)] if other is not None else [])
    count = len(sources)
    return call(
        functools.partial(attend_kernel, count),
        (number, pairs),
        [one(0)] + keys + values,
        (
            pl.BlockSpec((span, 2 * HD), lambda n, h: (n, h)),
            pl.BlockSpec((1, 1, 2, span), lambda n, h: (n, h, 0, 0)),
        ),
        (
            jax.ShapeDtypeStruct((rows, width), BF),
            jax.ShapeDtypeStruct((number, pairs, 2, span), F32),
        ),
        [],
        4 * rows * LEN * width * 4,
        2 * rows * width * 6,
        exps=rows * LEN * (width // HD),
    )(qkv, *sources, *sources)


def attend_back_kernel(count, q_ref, *refs):
    k_refs, v_refs = refs[:count], refs[count : 2 * count]
    dm_ref, l_ref, dq_ref = refs[2 * count : 2 * count + 3]
    out_refs = refs[2 * count + 3 :]
    dqs, dks, dvs = [], [[] for _ in range(count)], [[] for _ in range(count)]
    for head in range(q_ref.shape[-1] // HD):
        cols = slice(head * HD, head * HD + HD)
        q = q_ref[0][:, cols]
        dm = dm_ref[...][:, cols]
        base = l_ref[0, 0, head : head + 1, :]
        weights = [jnp.exp2(dot_nt(k[0][:, cols], q) * LOG2E - base) for k in k_refs]
        grads = [dot_nt(v[0][:, cols], dm) for v in v_refs]
        inner = functools.reduce(
            jnp.add, [jnp.sum(w * g, axis=0, keepdims=True) for w, g in zip(weights, grads)]
        )
        dq = None
        for i in range(count):
            ds = (weights[i] * (grads[i] - inner)).astype(BF)
            part = dot_tn(ds, k_refs[i][0][:, cols])
            dq = part if dq is None else dq + part
            dks[i].append(dot_nn(ds, q))
            dvs[i].append(dot_nn(weights[i].astype(BF), dm))
        dqs.append(dq)
    dq_ref[...] = (jnp.concatenate(dqs, axis=1).astype(BF).astype(F32) * SCALE).astype(BF)
    for i in range(count):
        out_refs[i][0] = jnp.concatenate(dks[i], axis=1).astype(out_refs[i].dtype)
        out_refs[i][1] = jnp.concatenate(dvs[i], axis=1).astype(out_refs[i].dtype)


def attend_backward(qkv, other, dm, logs):
    _, rows, width = qkv.shape
    span = min(rows, LEN)
    number = rows // span
    pairs = width // (2 * HD)
    one = lambda place: pl.BlockSpec((1, span, 2 * HD), lambda n, h: (place, n, h))
    flat = pl.BlockSpec((span, 2 * HD), lambda n, h: (n, h))
    both = pl.BlockSpec((2, span, 2 * HD), lambda n, h: (0, n, h))
    sources = [qkv] if other is None else [qkv, other]
    keys = [one(1)] + ([one(0)] if other is not None else [])
    values = [one(2)] + ([one(1)] if other is not None else [])
    count = len(sources)
    outs = [jax.ShapeDtypeStruct((2, rows, width), F32 if other is not None else BF)]
    if other is not None:
        outs.append(jax.ShapeDtypeStruct((2, rows, width), BF))
    return call(
        functools.partial(attend_back_kernel, count),
        (number, pairs),
        [one(0)] + keys + values + [flat, pl.BlockSpec((1, 1, 2, span), lambda n, h: (n, h, 0, 0))],
        tuple([flat] + [both] * count),
        tuple([jax.ShapeDtypeStruct((rows, width), BF)] + outs),
        [],
        10 * rows * LEN * width * 4,
        2 * rows * width * 12,
        exps=rows * LEN * (width // HD),
    )(qkv, *sources, *sources, dm, logs)


OUT_BIAS, FIRST_GAIN, FIRST_SHIFT, DOWN_BIAS, SECOND_GAIN, SECOND_SHIFT = range(6)


def vector(ref, place):
    return ref[place : place + 1, :]


def normed(hidden):
    average = jnp.mean(hidden, axis=-1, keepdims=True)
    center = hidden - average
    spread = jnp.mean(center * center, axis=-1, keepdims=True)
    inverse = lax.rsqrt(spread + EPSILON)
    return center * inverse, inverse


def norm_back(grad, z, inverse, gain):
    scaled = grad * gain
    average = jnp.mean(scaled, axis=-1, keepdims=True)
    along = jnp.mean(scaled * z, axis=-1, keepdims=True)
    return (scaled - average - z * along) * inverse


def total_rows(value):
    return jnp.sum(value, axis=0, keepdims=True)


def add_sums(ref, first, rows):
    value = jnp.concatenate(rows + [jnp.zeros((8 - len(rows), rows[0].shape[1]), F32)], axis=0)

    @pl.when(first)
    def _():
        ref[...] = value

    @pl.when(jnp.logical_not(first))
    def _():
        ref[...] += value


def accumulate(acc_ref, step, value):
    @pl.when(step == 0)
    def _():
        acc_ref[...] = value

    @pl.when(step > 0)
    def _():
        acc_ref[...] += value


def first_norm_kernel(m_ref, w_ref, x_ref, vec_ref, z_ref, r_ref, y_ref, acc_ref):
    step = pl.program_id(1)
    accumulate(acc_ref, step, dot_nt(m_ref[...], tile_of(w_ref)))

    @pl.when(step == pl.num_programs(1) - 1)
    def _():
        hidden = x_ref[...].astype(F32) + acc_ref[...] + vector(vec_ref, OUT_BIAS)
        z, inverse = normed(hidden)
        z_ref[...] = z
        r_ref[...] = inverse
        y_ref[...] = (z * vector(vec_ref, FIRST_GAIN) + vector(vec_ref, FIRST_SHIFT)).astype(BF)


def first_norm(mixed, weights, x, vectors):
    rows, width = x.shape
    tile = row_tile(rows)
    parts, cols = weights.shape[2], weights.shape[4]
    spec = weight_spec(weights, 1, lambda i, z: (3, z))
    flat = pl.BlockSpec((tile, width), lambda i, z: (i, 0))
    return call(
        first_norm_kernel,
        (rows // tile, parts),
        [pl.BlockSpec((tile, cols), lambda i, z: (i, z)), spec, flat, whole_spec(vectors.shape)],
        (flat, pl.BlockSpec((tile, 1), lambda i, z: (i, 0)), flat),
        (
            jax.ShapeDtypeStruct((rows, width), F32),
            jax.ShapeDtypeStruct((rows, 1), F32),
            jax.ShapeDtypeStruct((rows, width), BF),
        ),
        [pltpu.VMEM((tile, width), F32)],
        2 * rows * width * width,
        2 * (rows * width * 5 + width * width),
    )(mixed, weights, x, vectors)


def up_kernel(y_ref, w_ref, bias_ref, g_ref, slope_ref):
    upper = dot_nn(y_ref[...], tile_of(w_ref)) + bias_ref[...]
    half = 0.5 + 0.5 * lax.erf(upper * (0.5**0.5))
    g_ref[...] = (upper * half).astype(BF)
    bell = jnp.exp(upper * upper * -0.5) * ((2 * math.pi) ** -0.5)
    slope_ref[...] = (half + upper * bell).astype(BF)


def up_gelu(y, weights, bias):
    rows, width = y.shape
    parts, cols = weights.shape[2], weights.shape[4] * 2
    tile = row_tile(rows)
    full = parts * weights.shape[4] * 4
    out = pl.BlockSpec((tile, cols), lambda i, z: (i, z))
    shape = jax.ShapeDtypeStruct((rows, full), BF)
    return call(
        up_kernel,
        (rows // tile, full // cols),
        [
            pl.BlockSpec((tile, width), lambda i, z: (i, 0)),
            weight_spec(weights, 2, lambda i, z: (2 + z % 2, z // 2)),
            pl.BlockSpec((1, cols), lambda i, z: (0, z)),
        ],
        (out, out),
        (shape, shape),
        [],
        2 * rows * width * full,
        2 * (rows * width + 2 * rows * full + width * full),
        exps=2 * rows * full,
    )(y, weights, bias)


def second_norm_kernel(
    g_ref, w_ref, z1_ref, c_ref, vec_ref, out_ref, dh_ref, b_ref, sum_ref, acc_ref
):
    step = pl.program_id(1)
    first = pl.program_id(0) == 0
    accumulate(acc_ref, step, dot_nt(g_ref[...], tile_of(w_ref)))

    @pl.when(step == pl.num_programs(1) - 1)
    def _():
        y1 = z1_ref[...] * vector(vec_ref, FIRST_GAIN) + vector(vec_ref, FIRST_SHIFT)
        hidden = y1 + acc_ref[...] + vector(vec_ref, DOWN_BIAS)
        z, inverse = normed(hidden)
        gain = vector(vec_ref, SECOND_GAIN)
        out_ref[...] = (z * gain + vector(vec_ref, SECOND_SHIFT)).astype(BF)
        grad = c_ref[...].astype(F32)
        dh = norm_back(grad, z, inverse, gain)
        dh_ref[...] = dh
        b_ref[...] = dh.astype(BF)
        add_sums(sum_ref, first, [total_rows(grad * z), total_rows(grad), total_rows(dh)])


def second_norm(gated, weights, z1, cot, vectors):
    rows, width = z1.shape
    tile = row_tile(rows)
    parts, cols = weights.shape[2], weights.shape[4] * 4
    flat = pl.BlockSpec((tile, width), lambda i, z: (i, 0))
    return call(
        second_norm_kernel,
        (rows // tile, parts),
        [
            pl.BlockSpec((tile, cols), lambda i, z: (i, z)),
            weight_spec(weights, 4, lambda i, z: (2, z)),
            flat,
            flat,
            whole_spec(vectors.shape),
        ],
        (flat, flat, flat, whole_spec((8, width))),
        (
            jax.ShapeDtypeStruct((rows, width), BF),
            jax.ShapeDtypeStruct((rows, width), F32),
            jax.ShapeDtypeStruct((rows, width), BF),
            jax.ShapeDtypeStruct((8, width), F32),
        ),
        [pltpu.VMEM((tile, width), F32)],
        2 * rows * width * parts * cols,
        2 * (rows * width * 7 + (rows + width) * parts * cols),
    )(gated, weights, z1, cot, vectors)


def gate_back_kernel(b_ref, w_ref, slope_ref, du_ref, sum_ref):
    grad = dot_nn(b_ref[...], tile_of(w_ref))
    low = (grad * slope_ref[...].astype(F32)).astype(BF)
    du_ref[...] = low
    value = total_rows(low.astype(F32))
    first = pl.program_id(1) == 0

    @pl.when(first)
    def _():
        sum_ref[...] = value

    @pl.when(jnp.logical_not(first))
    def _():
        sum_ref[...] += value


def gate_back(b, weights, slope):
    rows, width = b.shape
    parts, cols = weights.shape[2], weights.shape[4] * 2
    tile = row_tile(rows)
    full = parts * weights.shape[4] * 4
    out = pl.BlockSpec((tile, cols), lambda z, i: (i, z))
    return call(
        gate_back_kernel,
        (full // cols, rows // tile),
        [
            pl.BlockSpec((tile, width), lambda z, i: (i, 0)),
            weight_spec(weights, 2, lambda z, i: (4 + z % 2, z // 2)),
            out,
        ],
        (out, pl.BlockSpec((1, cols), lambda z, i: (0, z))),
        (
            jax.ShapeDtypeStruct((rows, full), BF),
            jax.ShapeDtypeStruct((1, full), F32),
        ),
        [],
        2 * rows * width * full,
        2 * (rows * width + 2 * rows * full + width * full),
    )(b, weights, slope)


def first_back_kernel(
    du_ref, w_ref, dh2_ref, z1_ref, r1_ref, vec_ref, dh_ref, b_ref, sum_ref, acc_ref
):
    step = pl.program_id(1)
    first = pl.program_id(0) == 0
    accumulate(acc_ref, step, dot_nt(du_ref[...], tile_of(w_ref)))

    @pl.when(step == pl.num_programs(1) - 1)
    def _():
        grad = acc_ref[...] + dh2_ref[...]
        z = z1_ref[...]
        dh = norm_back(grad, z, r1_ref[...], vector(vec_ref, FIRST_GAIN))
        dh_ref[...] = dh
        b_ref[...] = dh.astype(BF)
        add_sums(sum_ref, first, [total_rows(grad * z), total_rows(grad), total_rows(dh)])


def first_back(du, weights, dh2, z1, r1, vectors):
    rows, width = z1.shape
    tile = row_tile(rows)
    parts, cols = weights.shape[2], weights.shape[4] * 4
    flat = pl.BlockSpec((tile, width), lambda i, z: (i, 0))
    return call(
        first_back_kernel,
        (rows // tile, parts),
        [
            pl.BlockSpec((tile, cols), lambda i, z: (i, z)),
            weight_spec(weights, 4, lambda i, z: (1, z)),
            flat,
            flat,
            pl.BlockSpec((tile, 1), lambda i, z: (i, 0)),
            whole_spec(vectors.shape),
        ],
        (flat, flat, whole_spec((8, width))),
        (
            jax.ShapeDtypeStruct((rows, width), F32),
            jax.ShapeDtypeStruct((rows, width), BF),
            jax.ShapeDtypeStruct((8, width), F32),
        ),
        [pltpu.VMEM((tile, width), F32)],
        2 * rows * width * parts * cols,
        2 * (rows * width * 8 + (rows + width) * parts * cols),
    )(du, weights, dh2, z1, r1, vectors)


def input_back_kernel(dq_ref, dkv_ref, w_ref, dh_ref, out_ref, acc_ref):
    step = pl.program_id(1)
    value = dot_nt(dq_ref[...], w_ref[0].reshape(-1, w_ref.shape[-1]))
    value += dot_nt(dkv_ref[0], w_ref[1].reshape(-1, w_ref.shape[-1]))
    value += dot_nt(dkv_ref[1], w_ref[2].reshape(-1, w_ref.shape[-1]))
    accumulate(acc_ref, step, value)

    @pl.when(step == pl.num_programs(1) - 1)
    def _():
        out_ref[...] = (acc_ref[...] + dh_ref[...]).astype(BF)


def input_back(dq, dkv, weights, dh1):
    rows, width = dh1.shape
    tile = row_tile(rows)
    parts, cols = weights.shape[2], weights.shape[4]
    flat = pl.BlockSpec((tile, width), lambda i, z: (i, 0))
    return call(
        input_back_kernel,
        (rows // tile, parts),
        [
            pl.BlockSpec((tile, cols), lambda i, z: (i, z)),
            pl.BlockSpec((2, tile, cols), lambda i, z: (0, i, z)),
            weight_spec(weights, 3, lambda i, z: (0, z)),
            flat,
        ],
        flat,
        jax.ShapeDtypeStruct((rows, width), BF),
        [pltpu.VMEM((tile, width), F32)],
        6 * rows * width * parts * cols,
        2 * (rows * width * 6 + 4 * width * parts * cols),
    )(dq, dkv, weights, dh1)


def outer_kernel(left_ref, right_ref, out_ref):
    shape = out_ref.shape
    right = right_ref[...].reshape(right_ref.shape[-2:])
    out_ref[...] = dot_tn(left_ref[...], right).astype(BF).reshape(shape)


def outer(left, right, begin, count, depth, parts):
    rows = left.shape[0]
    cols = right.shape[-1] // parts
    return call(
        outer_kernel,
        (parts,),
        [
            pl.BlockSpec((rows, count * depth), lambda z: (0, begin // count)),
            pl.BlockSpec((rows, cols), lambda z: (0, z)),
        ],
        pl.BlockSpec((count, 1, depth, cols), lambda z: (0, z, 0, 0)),
        jax.ShapeDtypeStruct((count, parts, depth, parts * cols // parts), BF),
        [],
        2 * rows * count * depth * parts * cols,
        2 * (rows * (count * depth + parts * cols) + count * depth * parts * cols),
    )(left, right)


def outer_stack(left, stack, begin, count, depth, parts):
    rows = left.shape[0]
    kinds = stack.shape[0]
    cols = stack.shape[-1] // parts
    return call(
        outer_kernel,
        (kinds, parts),
        [
            pl.BlockSpec((rows, count * depth), lambda k, z: (0, begin // count)),
            pl.BlockSpec((1, rows, cols), lambda k, z: (k, 0, z)),
        ],
        pl.BlockSpec((count, 1, 1, depth, cols), lambda k, z: (0, z, k, 0, 0)),
        jax.ShapeDtypeStruct((count, parts, kinds, depth, cols), BF),
        [],
        2 * rows * count * depth * parts * cols * kinds,
        2 * kinds * (rows * (count * depth + parts * cols) + count * depth * parts * cols),
    )(left, stack)


def remote(source, target, send, receive, device):
    return pltpu.make_async_remote_copy(
        source, target, send, receive, device_id=device, device_id_type=pl.DeviceIdType.MESH
    )


def greet(devices):
    barrier = pltpu.get_barrier_semaphore()
    for device in devices:
        pl.semaphore_signal(barrier, 1, device_id=device, device_id_type=pl.DeviceIdType.MESH)
    pl.semaphore_wait(barrier, len(devices))


class Cube:
    def __init__(self, count, parts):
        self.count, self.parts = count, parts
        self.place, self.z = lax.axis_index("dp"), lax.axis_index("tensor")
        self.core = lax.rem(self.place, 2)
        bits = [1 << i for i in range(1, count.bit_length() - 1)]
        self.orders = [bits, bits[::-1]]

    def stages(self):
        ups, downs = self.orders
        out = []
        for up, down in zip(ups, downs):
            out.append(self.place ^ jnp.where(self.core == 0, up, down))
        return out + [self.place ^ 1]

    def masks(self):
        table = []
        for order in self.orders:
            held = [0]
            for bit in order:
                held = held + [m ^ bit for m in held]
            table.append(held)
        return [a + [m ^ 1 for m in b] for a, b in (table, table[::-1])]


def gather_kernel(count, parts, ahead, w_ref, out_ref, local_sem, zs, zr, ss, sr):
    cube = Cube(count, parts)
    subs = w_ref.shape[0]
    partners = cube.stages()
    levels = len(partners)
    shifts = [lax.rem(cube.z + d, parts) for d in range(1, parts)]
    greet(
        [{"dp": cube.place, "tensor": z} for z in shifts]
        + [{"dp": p, "tensor": cube.z} for p in partners]
    )

    def own(sub):
        return pltpu.make_async_copy(w_ref.at[sub], out_ref.at[sub, 0, cube.z], local_sem.at[sub])

    def along(sub, d):
        return remote(
            w_ref.at[sub],
            out_ref.at[sub, 0, cube.z],
            zs.at[sub, d],
            zr.at[sub, d],
            {"dp": cube.place, "tensor": shifts[d]},
        )

    def stage(sub, level):
        size = 1 << level
        return remote(
            out_ref.at[sub, pl.ds(0, size)],
            out_ref.at[sub, pl.ds(size, size)],
            ss.at[sub, level],
            sr.at[sub, level],
            {"dp": partners[level], "tensor": cube.z},
        )

    def begin(sub):
        own(sub).start()
        for d in range(parts - 1):
            along(sub, d).start()

    for sub in range(min(ahead, subs)):
        begin(sub)
    for step in range(subs + levels):
        if step < subs:
            own(step).wait()
            for d in range(parts - 1):
                along(step, d).wait_recv()
            stage(step, 0).start()
            if step + ahead < subs:
                begin(step + ahead)
        for level in range(levels):
            sub = step - level - 1
            if 0 <= sub < subs:
                stage(sub, level).wait_recv()
                if level + 1 < levels:
                    stage(sub, level + 1).start()
    for sub in range(subs):
        for d in range(parts - 1):
            along(sub, d).wait_send()
        for level in range(levels):
            stage(sub, level).wait_send()


def gather(local, count, parts):
    subs, depth, cols = local.shape
    levels = count.bit_length() - 1
    dma = pltpu.SemaphoreType.DMA
    return pl.pallas_call(
        functools.partial(gather_kernel, count, parts, 6),
        in_specs=[pl.BlockSpec(memory_space=pl.ANY)],
        out_specs=pl.BlockSpec(memory_space=pl.ANY),
        out_shape=jax.ShapeDtypeStruct((subs, count, parts, depth, cols), BF),
        scratch_shapes=[
            dma((subs,)),
            dma((subs, parts - 1)),
            dma((subs, parts - 1)),
            dma((subs, levels)),
            dma((subs, levels)),
        ],
        compiler_params=pltpu.CompilerParams(collective_id=1, has_side_effects=True),
    )(local)


class Links:
    def __init__(self, count, parts):
        self.count, self.parts = count, parts
        self.cube = count == 8
        self.place = lax.axis_index("dp")
        self.core = self.place % 2
        masks = Cube(count, parts).masks()
        table = jnp.asarray(masks, jnp.int32)
        back = jnp.asarray([list(np.argsort(m)) for m in masks], jnp.int32)
        self.owner = table[self.core] ^ self.place
        self.inverse = back[self.core][jnp.arange(count) ^ self.place]

    def pairs(self, flip):
        out = []
        for place in range(self.count):
            for z in range(self.parts):
                out.append((place * self.parts + z, flip(place) * self.parts + z))
        return out

    def core_pairs(self):
        return self.pairs(lambda place: place ^ 1)

    def first_pairs(self):
        return self.pairs(lambda place: place ^ (4 if place % 2 else 2))

    def second_pairs(self):
        return self.pairs(lambda place: place ^ (2 if place % 2 else 4))

    def terms(self, make):
        half = self.count // 2
        return make(half, half), make(0, half)

    def scatter(self, terms):
        away, held = terms
        if not self.cube:
            full = jnp.concatenate([held, away])[self.inverse]
            full = lax.psum_scatter(full, "dp", scatter_dimension=0, tiled=False)
            return lax.psum_scatter(full, "tensor", scatter_dimension=0, tiled=False)
        far = lax.ppermute(away, AXES, self.core_pairs())
        away = summed(held[2:4], far[2:4])
        held = summed(held[0:2], far[0:2])
        far = lax.ppermute(away, AXES, self.second_pairs())
        away = summed(held[1:2], far[1:2])
        held = summed(held[0:1], far[0:1])
        far = lax.ppermute(away, AXES, self.first_pairs())
        held = summed(held, far)
        return lax.psum_scatter(held[0], "tensor", scatter_dimension=0, tiled=False)

    def row_pairs(self, second):
        half = self.parts // 2
        out = []
        for place in range(self.count):
            for z in range(self.parts):
                micro = (z + second) % 2
                target = (place // 2 * 2 + z // half) * self.parts + micro * half + place % 2
                out.append((place * self.parts + z, target))
        return out

    def rows_in(self, local):
        parity = lax.axis_index("tensor") % 2
        first = lax.dynamic_index_in_dim(local, parity, 0, keepdims=False)
        second = lax.dynamic_index_in_dim(local, 1 - parity, 0, keepdims=False)
        return jnp.concatenate(
            [
                lax.ppermute(first, AXES, self.row_pairs(0)),
                lax.ppermute(second, AXES, self.row_pairs(1)),
            ],
            axis=0,
        )

    def rows_out(self, held):
        parity = lax.axis_index("tensor") % 2
        rows = held.shape[0] // 2
        back = lambda second: [(b, a) for a, b in self.row_pairs(second)]
        first = lax.ppermute(held[:rows], AXES, back(0))
        second = lax.ppermute(held[rows:], AXES, back(1))
        swap = parity == 1
        return jnp.stack([jnp.where(swap, second, first), jnp.where(swap, first, second)])

    def total(self, value):
        step = 1
        while step < self.count:
            pairs = self.pairs(lambda place: place ^ step)
            value = value + lax.ppermute(value, AXES, pairs)
            step *= 2
        step = 1
        while step < self.parts:
            pairs = [
                (p * self.parts + z, p * self.parts + (z ^ step))
                for p in range(self.count)
                for z in range(self.parts)
            ]
            value = value + lax.ppermute(value, AXES, pairs)
            step *= 2
        return value


def summed(left, right):
    return (left.astype(F32) + right.astype(F32)).astype(BF)


def shards(
    inputs,
    query_weight,
    query_bias,
    key_weight,
    value_weight,
    value_bias,
    out_weight,
    out_bias,
    first_gain,
    first_shift,
    up_weight,
    up_bias,
    down_weight,
    down_bias,
    second_gain,
    second_shift,
    cotangent,
):
    count, parts = lax.axis_size("dp"), lax.axis_size("tensor")
    links = Links(count, parts)
    tensor_place = lax.axis_index("tensor")
    width = inputs.shape[-1]
    depth = width // count
    hidden = up_weight.shape[1] * parts

    source = jnp.repeat(links.owner, depth) * depth + jnp.tile(jnp.arange(depth), count)
    shuffle = (jnp.arange(width)[:, None] == source[None, :]).astype(BF)

    def ordered(rows):
        return dot_nn(rows, shuffle).astype(BF)

    def restored(rows):
        return dot_nt(rows, shuffle).astype(BF)

    def restored_vectors(rows):
        return rows.reshape(-1, count, depth)[:, links.inverse].reshape(-1, width)

    vectors = jnp.stack(
        [out_bias, first_gain, first_shift, down_bias, second_gain, second_shift]
        + [jnp.zeros_like(out_bias)] * 2
    )
    vectors = vectors.reshape(8, count, depth)[:, links.owner].reshape(8, width)

    cols = query_weight.shape[1]
    up_parts = [up_weight[:, i : i + cols] for i in range(0, up_weight.shape[1], cols)]
    down = down_weight.T
    down_parts = [down[:, i : i + cols] for i in range(0, down.shape[1], cols)]
    weights = gather(
        jnp.stack([query_weight, key_weight, value_weight, out_weight.T] + up_parts + down_parts),
        count,
        parts,
    )
    biases = lax.all_gather(
        jnp.concatenate([query_bias, value_bias, up_bias]), "tensor", axis=0, tiled=False
    )
    local = query_bias.shape[0]
    query_full = biases[:, :local].reshape(1, 1, -1)
    value_full = biases[:, local : 2 * local].reshape(1, 1, -1)
    up_full = biases[:, 2 * local :].reshape(1, -1)
    qkv_bias = jnp.concatenate([query_full, jnp.zeros_like(query_full), value_full], axis=0)
    x = ordered(links.rows_in(inputs))
    cot = ordered(links.rows_in(cotangent))

    qkv = project_qkv(x, weights, qkv_bias)
    share = x.shape[0] < LEN
    other = lax.ppermute(qkv[1:], AXES, links.core_pairs()) if share else None
    mixed, logs = attend_forward(qkv, other)
    z1, r1, y1 = first_norm(mixed, weights, x, vectors)
    gated, slope = up_gelu(y1, weights, up_full)
    out, dh2, b2, second_sums = second_norm(gated, weights, z1, cot, vectors)
    outputs = links.rows_out(restored(out))

    down_terms = links.terms(lambda begin, n: outer(b2, gated, begin, n, depth, parts))
    b2, down_terms = lax.optimization_barrier((b2, down_terms))
    down_grad = links.scatter(down_terms)
    du, up_bias_sum = gate_back(b2, weights, slope)
    up_terms = links.terms(lambda begin, n: outer(y1, du, begin, n, depth, parts))
    du, up_terms = lax.optimization_barrier((du, up_terms))
    up_grad = links.scatter(up_terms)
    dh1, b1, first_sums = first_back(du, weights, dh2, z1, r1, vectors)
    dm = project_back(b1, weights, 3)
    out_terms = links.terms(lambda begin, n: outer(b1, mixed, begin, n, depth, parts))
    dm, out_terms = lax.optimization_barrier((dm, out_terms))
    out_grad = links.scatter(out_terms)
    back = attend_backward(qkv, other, dm, logs)
    if share:
        dq, near, far = back
        dkv = (near + lax.ppermute(far, AXES, links.core_pairs()).astype(F32)).astype(BF)
    else:
        dq, dkv = back

    def qkv_outer(begin, n):
        return jnp.concatenate(
            [
                outer_stack(x, dq[None], begin, n, depth, parts),
                outer_stack(x, dkv, begin, n, depth, parts),
            ],
            axis=2,
        )

    qkv_terms = links.terms(qkv_outer)
    dq, dkv, qkv_terms = lax.optimization_barrier((dq, dkv, qkv_terms))
    qkv_grad = links.scatter(qkv_terms).astype(F32)
    dx = input_back(dq, dkv, weights, dh1)
    input_grad = links.rows_out(restored(dx)).astype(F32)

    sums = jnp.concatenate(
        [
            restored_vectors(jnp.concatenate([first_sums[:3], second_sums[:3]])),
            up_bias_sum.reshape(-1, width),
            jnp.sum(dq.astype(F32), axis=0, keepdims=True),
            jnp.sum(dkv[1].astype(F32), axis=0, keepdims=True),
        ]
    )
    sums = links.total(sums)
    wide = hidden // width

    def mine(vector_sum):
        size = vector_sum.shape[0] // parts
        return lax.dynamic_slice_in_dim(vector_sum, tensor_place * size, size)

    return (
        outputs,
        input_grad,
        qkv_grad[0],
        mine(sums[6 + wide]),
        qkv_grad[1],
        qkv_grad[2],
        mine(sums[7 + wide]),
        out_grad.astype(F32).T,
        sums[2],
        sums[0],
        sums[1],
        up_grad.astype(F32),
        mine(sums[6 : 6 + wide].reshape(-1)),
        down_grad.astype(F32).T,
        sums[5],
        sums[3],
        sums[4],
    )


def solution(mesh):
    rows = P(None, ("dp", "tensor"), None)
    return jax.shard_map(
        shards,
        mesh=mesh,
        in_specs=(
            rows,
            P("dp", "tensor"),
            P("tensor"),
            P("dp", "tensor"),
            P("dp", "tensor"),
            P("tensor"),
            P("tensor", "dp"),
            P(),
            P(),
            P(),
            P("dp", "tensor"),
            P("tensor"),
            P("tensor", "dp"),
            P(),
            P(),
            P(),
            rows,
        ),
        out_specs=(
            rows,
            rows,
            P("dp", "tensor"),
            P("tensor"),
            P("dp", "tensor"),
            P("dp", "tensor"),
            P("tensor"),
            P("tensor", "dp"),
            P(),
            P(),
            P(),
            P("dp", "tensor"),
            P("tensor"),
            P("tensor", "dp"),
            P(),
            P(),
            P(),
        ),
        check_vma=False,
    )
```

```python
import functools
import math

import jax
import jax.numpy as jnp
from jax import lax
from jax.experimental import pallas as pl
from jax.experimental.pallas import tpu as pltpu
from jax.sharding import PartitionSpec as P

HD = 64
LEN = 1024
EPSILON = 1e-05
SCALE = HD ** (-0.5)
LOG2E = math.log2(math.e)
BF = jnp.bfloat16
F32 = jnp.float32
MIB = 1 << 20


def dot_nn(left, right):
    return jnp.dot(left, right, preferred_element_type=F32)


def dot_nt(left, right):
    return lax.dot_general(left, right, (((1,), (1,)), ((), ())), preferred_element_type=F32)


def dot_tn(left, right):
    return lax.dot_general(left, right, (((0,), (0,)), ((), ())), preferred_element_type=F32)


OUT_BIAS, FIRST_GAIN, FIRST_SHIFT, DOWN_BIAS, SECOND_GAIN, SECOND_SHIFT = range(6)


def vector(ref, place):
    return ref[place : place + 1, :]


def normed(hidden):
    average = jnp.mean(hidden, axis=-1, keepdims=True)
    center = hidden - average
    spread = jnp.mean(center * center, axis=-1, keepdims=True)
    inverse = lax.rsqrt(spread + EPSILON)
    return center * inverse, inverse


def norm_back(grad, z, inverse, gain):
    scaled = grad * gain
    average = jnp.mean(scaled, axis=-1, keepdims=True)
    along = jnp.mean(scaled * z, axis=-1, keepdims=True)
    return (scaled - average - z * along) * inverse


def total_rows(value):
    return jnp.sum(value, axis=0, keepdims=True)


def remote(source, target, send, receive, device):
    return pltpu.make_async_remote_copy(
        source, target, send, receive, device_id=device, device_id_type=pl.DeviceIdType.MESH
    )


def greet(devices):
    barrier = pltpu.get_barrier_semaphore()
    for device in devices:
        pl.semaphore_signal(barrier, 1, device_id=device, device_id_type=pl.DeviceIdType.MESH)
    pl.semaphore_wait(barrier, len(devices))


class Cube:
    def __init__(self, count, parts):
        self.count, self.parts, self.half = count, parts, parts // 2
        self.place, self.z = lax.axis_index("dp"), lax.axis_index("tensor")
        self.core = lax.rem(self.place, 2)
        self.levels = count.bit_length() - 1
        bits = [1 << i for i in range(1, self.levels)]
        self.orders = [bits, bits[::-1]]

    def stages(self):
        ups, downs = self.orders
        out = []
        for up, down in zip(ups, downs):
            out.append(self.place ^ jnp.where(self.core == 0, up, down))
        return out + [self.place ^ 1]

    def masks(self):
        table = []
        for order in self.orders:
            held = [0]
            for bit in order:
                held = held + [m ^ bit for m in held]
            table.append(held)
        return [a + [m ^ 1 for m in b] for a, b in (table, table[::-1])]

    def column(self):
        mine = [{"dp": self.place, "tensor": lax.rem(self.z + d, self.parts)} for d in range(1, self.parts)]
        others = [{"dp": self.place ^ 1, "tensor": lax.rem(self.z + d, self.parts)} for d in range(self.parts)]
        return mine + others

    def neighbours(self):
        return [{"dp": p, "tensor": self.z} for p in self.stages()[:-1]]

    def shuffle(self, width):
        depth = width // self.count
        column = lax.broadcasted_iota(jnp.int32, (1, width), 1)
        slot = column // depth
        far = slot // (self.count // 2)
        flips = far
        for level, (up, down) in enumerate(zip(*self.orders)):
            bit = jnp.where(self.core == 0, up, down)
            other = jnp.where(self.core == 0, down, up)
            held = lax.rem(slot // (1 << level), 2)
            flips = flips + held * jnp.where(far == 0, bit, other)
        owner = self.place ^ flips
        source = owner * depth + lax.rem(column, depth)
        row = lax.broadcasted_iota(jnp.int32, (width, width), 0)
        return (row == source).astype(F32).astype(BF)


class Rows:
    def __init__(self, cube, send, receive, here):
        self.cube, self.send, self.receive, self.here = cube, send, receive, here
        c = cube
        self.slot = lax.rem(c.z, c.half)
        self.targets = [(c.place - c.core + c.z // c.half, m * c.half + c.core) for m in range(2)]
        self.micro = c.z // c.half
        self.sources = [(c.place - c.core + lax.rem(c.z, c.half), c.half * c.core + p) for p in range(2)]

    def own(self, device):
        return jnp.logical_and(device[0] == self.cube.place, device[1] == self.cube.z)

    def at(self, device):
        return {"dp": device[0], "tensor": device[1]}

    def into(self, source, target, piece, pieces):
        size = source.shape[1] // pieces
        at = pl.ds(pl.multiple_of(piece * size, size), size)
        for m, device in enumerate(self.targets):
            own = self.own(device)

            @pl.when(own)
            def _(m=m):
                pltpu.make_async_copy(source.at[m, at], target.at[self.slot, at], self.here).start()

            @pl.when(jnp.logical_not(own))
            def _(m=m, device=device):
                remote(
                    source.at[m, at],
                    target.at[self.slot, at],
                    self.send.at[m],
                    self.receive.at[self.slot],
                    self.at(device),
                ).start()

    def into_wait(self, source, target):
        for p, device in enumerate(self.sources):
            own = self.own(device)

            @pl.when(own)
            def _(p=p):
                pltpu.make_async_copy(source.at[0], target.at[p], self.here).wait()

            @pl.when(jnp.logical_not(own))
            def _(p=p, device=device):
                remote(
                    source.at[0], target.at[p], self.send.at[0], self.receive.at[p], self.at(device)
                ).wait_recv()

    def into_end(self, source, target):
        for m, device in enumerate(self.targets):

            @pl.when(jnp.logical_not(self.own(device)))
            def _(m=m, device=device):
                remote(
                    source.at[m], target.at[self.slot], self.send.at[m], self.receive.at[0], self.at(device)
                ).wait_send()


    def back(self, source, lead, target, piece, pieces):
        size = target.shape[1] // pieces
        for p, device in enumerate(self.sources):
            own = self.own(device)
            here = pl.ds(pl.multiple_of(p * target.shape[1] + piece * size, size), size)
            there = pl.ds(pl.multiple_of(piece * size, size), size)

            @pl.when(own)
            def _(here=here, there=there):
                pltpu.make_async_copy(
                    source.at[lead, here], target.at[self.micro, there], self.here
                ).start()

            @pl.when(jnp.logical_not(own))
            def _(p=p, device=device, here=here, there=there):
                remote(
                    source.at[lead, here],
                    target.at[self.micro, there],
                    self.send.at[p],
                    self.receive.at[self.micro],
                    self.at(device),
                ).start()

    def back_wait(self, source, lead, target):
        rows = target.shape[1]
        for m, device in enumerate(self.targets):

            @pl.when(jnp.logical_not(self.own(device)))
            def _(m=m, device=device):
                remote(
                    source.at[lead, pl.ds(0, rows)],
                    target.at[m],
                    self.send.at[0],
                    self.receive.at[m],
                    self.at(device),
                ).wait_recv()

    def back_end(self, source, lead, target):
        rows = target.shape[1]
        for p, device in enumerate(self.sources):
            own = self.own(device)

            @pl.when(own)
            def _(p=p):
                pltpu.make_async_copy(
                    source.at[lead, pl.ds(p * rows, rows)], target.at[self.micro], self.here
                ).wait()

            @pl.when(jnp.logical_not(own))
            def _(p=p, device=device):
                remote(
                    source.at[lead, pl.ds(p * rows, rows)],
                    target.at[self.micro],
                    self.send.at[p],
                    self.receive.at[0],
                    self.at(device),
                ).wait_send()


SUBS, UP, DOWN = 12, 4, 8
XP, CS, CP = 4, 4, 8


def loop(count, body):
    lax.fori_loop(0, count, lambda i, _: (body(i), None)[1], None)


def chunk(i, size):
    return pl.ds(pl.multiple_of(i * size, size), size)


def weight_tile(ref, slot, z):
    value = ref[slot, :, z]
    return value.reshape(-1, value.shape[-1])


def forward_kernel(
    count,
    parts,
    local_ref,
    bias_ref,
    vec_ref,
    in_ref,
    cot_ref,
    weights_ref,
    x_out,
    qkv_out,
    other_out,
    mixed_out,
    logs_out,
    z1_out,
    r1_out,
    y1_out,
    gated_out,
    slope_out,
    normed_out,
    dh2_out,
    b2_out,
    sums_out,
    raw_ref,
    cot_raw,
    shuffle_ref,
    x_ref,
    c_ref,
    bias_all,
    qkv_ref,
    other_ref,
    mixed_ref,
    logs_ref,
    z1_ref,
    r1_ref,
    y1_ref,
    gated_ref,
    slope_ref,
    acc_ref,
    normed_ref,
    dh2_ref,
    b2_ref,
    sums_ref,
    wbuf,
    local_sem,
    zs,
    zr,
    ss,
    sr,
    wsem,
    bias_send,
    bias_recv,
    row_send,
    row_recv,
    row_here,
    kv_send,
    kv_recv,
    out_sem,
):
    cube = Cube(count, parts)
    partners, levels = cube.stages(), cube.levels
    shifts = [lax.rem(cube.z + d, parts) for d in range(1, parts)]
    ahead = 5
    rows = x_ref.shape[0]
    cols = weights_ref.shape[-1]
    greet(cube.column() + cube.neighbours())

    def own(sub):
        return pltpu.make_async_copy(local_ref.at[sub], weights_ref.at[sub, 0, cube.z], local_sem.at[sub])

    inner = jnp.logical_or(cube.z == 1, cube.z == 2)
    mine, theirs = cube.z // 2 * 2, 2 - cube.z // 2 * 2

    def along(sub, hop):
        if hop == 0:
            source, target, z = local_ref.at[sub], weights_ref.at[sub, 0, cube.z], cube.z ^ 1
        else:
            source = weights_ref.at[sub, 0, pl.ds(mine if hop == 1 else theirs, 2)]
            target, z = source, (3 - cube.z if hop == 1 else cube.z ^ 1)
        return remote(
            source, target, zs.at[sub, hop], zr.at[sub, hop], {"dp": cube.place, "tensor": z}
        )

    def stage(sub, level):
        size = 1 << level
        return remote(
            weights_ref.at[sub, pl.ds(0, size)],
            weights_ref.at[sub, pl.ds(size, size)],
            ss.at[sub, level],
            sr.at[sub, level],
            {"dp": partners[level], "tensor": cube.z},
        )

    def begin(sub):
        own(sub).start()
        along(sub, 0).start()

    def pass_pair(sub):
        own(sub).wait()
        along(sub, 0).wait_recv()

        @pl.when(inner)
        def _():
            along(sub, 1).start()

    def pass_on(sub):
        @pl.when(inner)
        def _():
            along(sub, 1).wait_recv()
            along(sub, 2).start()

    def relay(step):
        @pl.when(step < SUBS)
        def _():
            @pl.when(jnp.logical_not(inner))
            def _():
                along(step, 2).wait_recv()

            stage(step, 0).start()

        for level in range(levels):
            sub = step - level - 1

            @pl.when(jnp.logical_and(sub >= 0, sub < SUBS))
            def _(sub=sub, level=level):
                stage(sub, level).wait_recv()
                if level + 1 < levels:
                    stage(sub, level + 1).start()

        @pl.when(step < XP)
        def _():
            rows_x.into(in_ref, raw_ref, step, XP)

        @pl.when(jnp.logical_and(step >= CS, step < CS + CP))
        def _():
            rows_c.into(cot_ref, cot_raw, step - CS, CP)

        @pl.when(step + 1 < SUBS)
        def _():
            pass_on(step + 1)

        @pl.when(step + 2 < SUBS)
        def _():
            pass_pair(step + 2)

        @pl.when(step + ahead < SUBS)
        def _():
            begin(step + ahead)

    def relays(first, last):
        loop(last - first, lambda i: relay(first + i))

    def load(sub):
        return pltpu.make_async_copy(weights_ref.at[sub], wbuf.at[sub % 4], wsem.at[sub % 4])

    def share_bias(d):
        return remote(
            bias_ref,
            bias_all.at[cube.z],
            bias_send.at[d],
            bias_recv.at[d],
            {"dp": cube.place, "tensor": shifts[d]},
        )

    rows_x = Rows(cube, row_send.at[0], row_recv.at[0], row_here.at[0])
    rows_c = Rows(cube, row_send.at[1], row_recv.at[1], row_here.at[1])
    outs = []

    def keep(source, target):
        copy = pltpu.make_async_copy(source, target, out_sem.at[len(outs)])
        copy.start()
        outs.append(copy)

    loop(ahead, begin)
    for d in range(parts - 1):
        share_bias(d).start()
    pass_pair(0)
    pass_pair(1)
    pass_on(0)
    shuffle_ref[...] = cube.shuffle(x_ref.shape[1])
    bias_all[cube.z] = bias_ref[...]
    relays(0, levels + 1)
    rows_x.into_wait(in_ref, raw_ref)
    half_rows = raw_ref.shape[1]
    for p in range(2):
        x_ref[p * half_rows : (p + 1) * half_rows, :] = dot_nn(raw_ref[p], shuffle_ref[...]).astype(BF)
    keep(x_ref, x_out)
    for d in range(parts - 1):
        share_bias(d).wait_recv()

    for kind in range(3):
        load(kind).start()
        if kind < 2:
            relays(levels + kind + 1, levels + kind + 2)
        load(kind).wait()

        def project(z, kind=kind):
            acc = dot_nn(x_ref[...], weight_tile(wbuf, kind, z))
            if kind == 0:
                acc = (acc + bias_all[z, 0:1, :]) * SCALE
            elif kind == 2:
                acc = acc + bias_all[z, 1:2, :]
            qkv_ref[kind, :, chunk(z, cols)] = acc.astype(BF)

        loop(parts, project)

    swap = remote(qkv_ref.at[pl.ds(1, 2)], other_ref, kv_send, kv_recv, {"dp": cube.place ^ 1, "tensor": cube.z})
    swap.start()
    keep(qkv_ref, qkv_out)
    relays(levels + 3, levels + 4)
    swap.wait_recv()
    keep(other_ref, other_out)

    def attend(pair):
        lanes = chunk(pair, 2 * HD)
        q2 = qkv_ref[0, :, lanes]
        k2 = [qkv_ref[1, :, lanes], other_ref[0, :, lanes]]
        v2 = [qkv_ref[2, :, lanes], other_ref[1, :, lanes]]
        mixed, logs = [], []
        for head in range(2):
            part = slice(head * HD, head * HD + HD)
            scores = [dot_nt(k[:, part], q2[:, part]) for k in k2]
            top = functools.reduce(jnp.maximum, [jnp.max(s, axis=0, keepdims=True) for s in scores])
            base = top * LOG2E
            expo = [jnp.exp2(s * LOG2E - base) for s in scores]
            total = functools.reduce(jnp.add, [jnp.sum(e, axis=0, keepdims=True) for e in expo])
            inverse = 1.0 / total
            mixed.append(
                functools.reduce(
                    jnp.add, [dot_tn((e * inverse).astype(BF), v[:, part]) for e, v in zip(expo, v2)]
                )
            )
            logs.append(base + jnp.log2(total))
        mixed_ref[:, lanes] = jnp.concatenate(mixed, axis=1).astype(BF)
        logs_ref[pair] = jnp.concatenate(logs + [jnp.zeros((6, rows), F32)], axis=0)

    pairs = mixed_ref.shape[1] // (2 * HD)
    loop(pairs // 2, attend)
    relays(levels + 4, levels + 5)
    loop(pairs // 2, lambda i: attend(pairs // 2 + i))
    relays(levels + 5, levels + 6)
    keep(mixed_ref, mixed_out)
    keep(logs_ref, logs_out)

    load(3).start()
    load(4).start()
    load(3).wait()

    def mix(z):
        value = dot_nt(mixed_ref[:, chunk(z, cols)], weight_tile(wbuf, 3, z))

        @pl.when(z == 0)
        def _():
            acc_ref[...] = value

        @pl.when(z > 0)
        def _():
            acc_ref[...] += value

    loop(parts, mix)
    size = 128

    def norm_first(i):
        at = chunk(i, size)
        hidden = x_ref[at, :].astype(F32) + acc_ref[at, :] + vector(vec_ref, OUT_BIAS)
        z, inverse = normed(hidden)
        z1_ref[at, :] = z
        r1_ref[at, :] = jnp.broadcast_to(inverse, (size, 128))
        y = z * vector(vec_ref, FIRST_GAIN) + vector(vec_ref, FIRST_SHIFT)
        y1_ref[at, :] = y.astype(BF)
        acc_ref[at, :] = y + vector(vec_ref, DOWN_BIAS)

    loop(rows // size, norm_first)
    keep(z1_ref, z1_out)
    keep(r1_ref, r1_out)
    keep(y1_ref, y1_out)

    def gate(sub):
        load(sub).wait()

        def part(z):
            lanes = chunk(z, cols)
            upper = dot_nn(y1_ref[...], weight_tile(wbuf, sub % 4, z)) + bias_all[z, sub - UP + 2 : sub - UP + 3, :]
            half = 0.5 + 0.5 * lax.erf(upper * (0.5**0.5))
            gated_ref[sub - UP, :, lanes] = (upper * half).astype(BF)
            bell = jnp.exp(upper * upper * -0.5) * ((2 * math.pi) ** -0.5)
            slope_ref[sub - UP, :, lanes] = (half + upper * bell).astype(BF)

        loop(parts, part)
        keep(gated_ref.at[sub - UP], gated_out.at[sub - UP])
        keep(slope_ref.at[sub - UP], slope_out.at[sub - UP])

    last = SUBS + levels
    done = levels + 6
    for sub in range(UP, DOWN):
        gate(sub)
        if done < last:
            relays(done, done + 1)
            done += 1
        if sub + 1 < DOWN:
            load(sub + 1).start()

    rows_c.into_wait(cot_ref, cot_raw)
    for p in range(2):
        c_ref[p * half_rows : (p + 1) * half_rows, :] = dot_nn(cot_raw[p], shuffle_ref[...]).astype(BF)

    for sub in range(DOWN, SUBS):
        if done < sub + levels + 1:
            relays(done, sub + levels + 1)
            done = sub + levels + 1
        load(sub).start()
        load(sub).wait()

        def fold(z, sub=sub):
            acc_ref[...] += dot_nt(gated_ref[sub - DOWN, :, chunk(z, cols)], weight_tile(wbuf, sub % 4, z))

        loop(parts, fold)

    sums_ref[...] = jnp.zeros_like(sums_ref)

    def norm_second(i):
        at = chunk(i, size)
        z, inverse = normed(acc_ref[at, :])
        gain = vector(vec_ref, SECOND_GAIN)
        normed_ref[at, :] = (z * gain + vector(vec_ref, SECOND_SHIFT)).astype(BF)
        grad = c_ref[at, :].astype(F32)
        dh = norm_back(grad, z, inverse, gain)
        dh2_ref[at, :] = dh
        b2_ref[at, :] = dh.astype(BF)
        sums_ref[0:1, :] += total_rows(grad * z)
        sums_ref[1:2, :] += total_rows(grad)
        sums_ref[2:3, :] += total_rows(dh)

    loop(rows // size, norm_second)
    keep(normed_ref, normed_out)
    keep(dh2_ref, dh2_out)
    keep(b2_ref, b2_out)
    keep(sums_ref, sums_out)

    def sent(sub):
        along(sub, 0).wait_send()

        @pl.when(inner)
        def _():
            along(sub, 1).wait_send()
            along(sub, 2).wait_send()

        for level in range(levels):
            stage(sub, level).wait_send()

    loop(SUBS, sent)
    for d in range(parts - 1):
        share_bias(d).wait_send()
    swap.wait_send()
    rows_x.into_end(in_ref, raw_ref)
    rows_c.into_end(cot_ref, cot_raw)
    for copy in outs:
        copy.wait()


def forward(local, bias, vectors, inputs, cotangent, count, parts):
    subs, depth, cols = local.shape
    _, half_rows, width = inputs.shape
    rows = 2 * half_rows
    levels = count.bit_length() - 1
    pairs = width // (2 * HD)
    dma = pltpu.SemaphoreType.DMA
    low = lambda *shape: (shape, BF)
    high = lambda *shape: (shape, F32)
    results = [
        low(subs, count, parts, depth, cols),
        low(rows, width),
        low(3, rows, width),
        low(2, rows, width),
        low(rows, width),
        high(pairs, 8, rows),
        high(rows, width),
        high(rows, 128),
        low(rows, width),
        low(4, rows, parts * cols),
        low(4, rows, parts * cols),
        low(rows, width),
        high(rows, width),
        low(rows, width),
        high(8, width),
    ]
    scratch = [
        low(2, half_rows, width),
        low(2, half_rows, width),
        low(width, width),
        low(rows, width),
        low(rows, width),
        high(parts, 8, cols),
        low(3, rows, width),
        low(2, rows, width),
        low(rows, width),
        high(pairs, 8, rows),
        high(rows, width),
        high(rows, 128),
        low(rows, width),
        low(4, rows, parts * cols),
        low(4, rows, parts * cols),
        high(rows, width),
        low(rows, width),
        high(rows, width),
        low(rows, width),
        high(8, width),
        low(4, count, parts, depth, cols),
    ]
    hbm = pl.BlockSpec(memory_space=pl.ANY)
    vmem = pl.BlockSpec(memory_space=pltpu.VMEM)
    return pl.pallas_call(
        functools.partial(forward_kernel, count, parts),
        in_specs=[hbm, vmem, vmem, hbm, hbm],
        out_specs=[hbm] * len(results),
        out_shape=[jax.ShapeDtypeStruct(*r) for r in results],
        scratch_shapes=[pltpu.VMEM(*s) for s in scratch]
        + [
            dma((subs,)),
            dma((subs, 3)),
            dma((subs, 3)),
            dma((subs, levels)),
            dma((subs, levels)),
            dma((4,)),
            dma((parts - 1,)),
            dma((parts - 1,)),
            dma((2, 2)),
            dma((2, 2)),
            dma((2,)),
            dma,
            dma,
            dma((24,)),
        ],
        compiler_params=pltpu.CompilerParams(
            collective_id=1, has_side_effects=True, vmem_limit_bytes=60 * MIB
        ),
    )(local, bias, vectors, inputs, cotangent)


HELD = 6
ORDER = [8, 9, 10, 11, 4, 5, 6, 7, 3, 0, 2, 1]


def backward_kernel(
    count,
    parts,
    vec_ref,
    second_ref,
    weights_ref,
    x_in,
    qkv_in,
    other_in,
    mixed_in,
    logs_in,
    z1_in,
    r1_in,
    y1_in,
    gated_in,
    slope_in,
    normed_in,
    dh2_in,
    b2_in,
    grads_ref,
    sums_out,
    outputs_ref,
    input_ref,
    first_ref,
    pool,
    logs_ref,
    y_ref,
    dh_ref,
    z1_ref,
    r1_ref,
    b_ref,
    mixed_ref,
    acc_ref,
    near_ref,
    far_ref,
    swap_ref,
    back_ref,
    wbuf,
    send_ref,
    staged_ref,
    held_ref,
    small_ref,
    zed_ref,
    sums_ref,
    sums_in,
    load_sem,
    wsem,
    stage_sem,
    ss,
    sr,
    zs,
    zr,
    swap_send,
    swap_recv,
    row_send,
    row_recv,
    row_here,
    sum_send,
    sum_recv,
    out_sem,
):
    cube = Cube(count, parts)
    partners, levels = cube.stages(), cube.levels
    top = levels - 1
    half = count // 2
    shifts = [lax.rem(cube.z + d, parts) for d in range(1, parts)]
    rows, width = b_ref.shape
    cols = weights_ref.shape[-1]
    depth = weights_ref.shape[-2]
    wide = half * depth
    size = 128
    greet(cube.column() + cube.neighbours())

    def load(place, source, target):
        return pltpu.make_async_copy(source, target, load_sem.at[place])

    def weight(sub, slot):
        return pltpu.make_async_copy(weights_ref.at[sub], wbuf.at[slot], wsem.at[slot])

    gate_load = [load(j % 2, gated_in.at[j], pool.at[j % 2]) for j in range(4)]
    slope_load = [load(2 + j % 2, slope_in.at[j], pool.at[2 + j % 2]) for j in range(4)]
    b_load = load(4, b2_in, b_ref)
    out_load = load(5, normed_in, near_ref.at[0])
    y_load = load(6, y1_in, y_ref)
    dh_load = load(7, dh2_in, dh_ref)
    z_load = load(8, z1_in, z1_ref)
    r_load = load(9, r1_in, r1_ref)
    mixed_load = load(10, mixed_in, mixed_ref)
    logs_load = load(11, logs_in, logs_ref)
    qkv_load = load(12, qkv_in, pool.at[pl.ds(0, 3)])
    other_load = load(13, other_in, pool.at[pl.ds(3, 2)])
    x_load = load(14, x_in, y_ref)

    def stage(r, level):
        if level == top:
            source, target = send_ref.at[lax.rem(r, 3)], first_ref.at[r]
        else:
            source = held_ref.at[lax.rem(r, HELD), pl.ds(1 << level, 1 << level)]
            target = small_ref.at[r, pl.ds((1 << level) - 1, 1 << level)]
        return remote(
            source, target, ss.at[r, level], sr.at[r, level], {"dp": partners[level], "tensor": cube.z}
        )

    def away(r, d):
        return remote(
            held_ref.at[lax.rem(r, HELD), 0, shifts[d]],
            zed_ref.at[r, d],
            zs.at[r, d],
            zr.at[r, d],
            {"dp": cube.place, "tensor": shifts[d]},
        )

    def fetch(r):
        return pltpu.make_async_copy(first_ref.at[r], staged_ref.at[r % 2], stage_sem.at[r % 2])

    def give(r, left, right):
        if r >= 3:
            stage(r - 3, top).wait_send()

        def part(z):
            value = dot_tn(left[:, wide:], right[:, chunk(z, cols)])
            send_ref[r % 3, :, z] = value.astype(BF).reshape(half, depth, cols)

        loop(parts, part)
        stage(r, top).start()

    def arrive(r):
        stage(r, top).wait_recv()
        fetch(r).start()

    def hold(r, left, right):
        advances(r - HELD + top + 1)
        fetch(r).wait()

        def part(z):
            value = dot_tn(left[:, :wide], right[:, chunk(z, cols)])
            value = value + staged_ref[r % 2, :, z].reshape(wide, cols).astype(F32)
            held_ref[r % HELD, :, z] = value.astype(BF).reshape(half, depth, cols)

        loop(parts, part)
        stage(r, top - 1).start()

    def advance(k):
        for i in range(top):
            level = top - 1 - i
            r = k - i

            @pl.when(jnp.logical_and(r >= 0, r < SUBS))
            def _(r=r, level=level):
                stage(r, level).wait_recv()
                place = lax.rem(r, HELD)

                def fold(slot):
                    mine = held_ref[place, slot].astype(F32)
                    mine = mine + small_ref[r, (1 << level) - 1 + slot].astype(F32)
                    held_ref[place, slot] = mine.astype(BF)

                loop(1 << level, fold)
                if level > 0:
                    stage(r, level - 1).start()
                else:
                    for d in range(parts - 1):
                        away(r, d).start()

        r = k - top

        @pl.when(jnp.logical_and(r >= 0, r < SUBS))
        def _():
            value = held_ref[lax.rem(r, HELD), 0, cube.z].astype(F32)
            for d in range(parts - 1):
                away(r, d).wait_recv()
                value = value + zed_ref[r, d].astype(F32)
            grads_ref[r] = value
            for d in range(parts - 1):
                away(r, d).wait_send()
            for level in range(top):
                stage(r, level).wait_send()

    done = [0]

    def advances(last):
        if last > done[0]:
            first = done[0]
            loop(last - first, lambda i: advance(first + i))
            done[0] = last

    back_out = Rows(cube, row_send.at[0], row_recv.at[0], row_here.at[0])
    back_in = Rows(cube, row_send.at[1], row_recv.at[1], row_here.at[1])
    pieces = 8

    sums_ref[...] = jnp.zeros_like(sums_ref)
    sums_ref[3:6, :] = second_ref[0:3, :]

    b_load.start()
    gate_load[0].start()
    weight(8, 0).start()
    slope_load[0].start()
    gate_load[1].start()
    out_load.start()
    y_load.start()
    b_load.wait()
    gate_load[0].wait()
    give(0, b_ref, pool.at[0])
    slope_load[1].start()
    weight(9, 1).start()
    dh_load.start()
    z_load.start()
    r_load.start()
    mixed_load.start()
    logs_load.start()
    gate_load[1].wait()
    give(1, b_ref, pool.at[1])
    arrive(0)

    out_load.wait()
    near_ref[1] = dot_nt(near_ref[0], cube.shuffle(width)).astype(BF)

    def send_out(piece):
        back_out.back(near_ref, 1, outputs_ref, piece, pieces)

    loop(2, send_out)
    hold(0, b_ref, pool.at[0])
    arrive(1)
    gate_load[2].start()

    def gate_back(j):
        slope_load[j].wait()
        weight(8 + j, j % 2).wait()

        def part(z):
            lanes = chunk(z, cols)
            grad = dot_nn(b_ref[...], weight_tile(wbuf, j % 2, z))
            low = (grad * pool[2 + j % 2, :, lanes].astype(F32)).astype(BF)
            pool[4 + j, :, lanes] = low
            sums_ref[6 + j : 7 + j, lanes] = total_rows(low.astype(F32))

        loop(parts, part)

    gate_back(0)
    slope_load[2].start()
    weight(10, 0).start()
    loop(2, lambda i: send_out(2 + i))
    hold(1, b_ref, pool.at[1])
    gate_load[3].start()
    gate_load[2].wait()
    give(2, b_ref, pool.at[0])
    gate_back(1)
    slope_load[3].start()
    weight(11, 1).start()
    loop(2, lambda i: send_out(4 + i))
    arrive(2)
    advances(1)
    gate_load[3].wait()
    give(3, b_ref, pool.at[1])
    hold(2, b_ref, pool.at[0])
    gate_back(2)
    weight(4, 0).start()
    loop(2, lambda i: send_out(6 + i))
    arrive(3)
    hold(3, b_ref, pool.at[1])
    qkv_waits = []
    gate_back(3)
    weight(5, 1).start()
    qkv_load.start()
    advances(2)
    y_load.wait()

    def fold_up(j):
        weight(4 + j, j % 2).wait()

        def part(z):
            value = dot_nt(pool[4 + j, :, chunk(z, cols)], weight_tile(wbuf, j % 2, z))
            if j == 0:

                @pl.when(z == 0)
                def _():
                    acc_ref[...] = value

                @pl.when(z > 0)
                def _():
                    acc_ref[...] += value
            else:
                acc_ref[...] += value

        loop(parts, part)

    give(4, y_ref, pool.at[4])
    fold_up(0)
    weight(6, 0).start()
    arrive(4)
    give(5, y_ref, pool.at[5])
    hold(4, y_ref, pool.at[4])
    fold_up(1)
    weight(7, 1).start()
    arrive(5)
    give(6, y_ref, pool.at[6])
    hold(5, y_ref, pool.at[5])
    advances(3)
    fold_up(2)
    weight(3, 0).start()
    arrive(6)
    give(7, y_ref, pool.at[7])
    hold(6, y_ref, pool.at[6])
    fold_up(3)
    arrive(7)
    advances(4)
    hold(7, y_ref, pool.at[7])
    x_load.start()
    other_load.start()

    dh_load.wait()
    z_load.wait()
    r_load.wait()

    def norm_first(i):
        at = chunk(i, size)
        grad = acc_ref[at, :] + dh_ref[at, :]
        z = z1_ref[at, :]
        dh = norm_back(grad, z, r1_ref[at, 0:1], vector(vec_ref, FIRST_GAIN))
        dh_ref[at, :] = dh
        b_ref[at, :] = dh.astype(BF)
        sums_ref[0:1, :] += total_rows(grad * z)
        sums_ref[1:2, :] += total_rows(grad)
        sums_ref[2:3, :] += total_rows(dh)

    loop(rows // size, norm_first)
    mixed_load.wait()
    advances(5)
    give(8, b_ref, mixed_ref)
    weight(3, 0).wait()
    dm = 5

    def mix_back(z):
        pool[dm, :, chunk(z, cols)] = dot_nn(b_ref[...], weight_tile(wbuf, 0, z)).astype(BF)

    loop(parts, mix_back)
    arrive(8)
    weight(0, 0).start()
    weight(1, 1).start()
    hold(8, b_ref, mixed_ref)

    qkv_load.wait()
    other_load.wait()
    logs_load.wait()

    def swap(pair):
        lanes = chunk(pair, 2 * HD)
        return remote(
            far_ref.at[:, :, lanes],
            swap_ref.at[:, :, lanes],
            swap_send.at[pair],
            swap_recv.at[pair],
            {"dp": cube.place ^ 1, "tensor": cube.z},
        )

    def attend(pair):
        lanes = chunk(pair, 2 * HD)
        q2, dm2 = pool[0, :, lanes], pool[dm, :, lanes]
        k2 = [pool[1, :, lanes], pool[3, :, lanes]]
        v2 = [pool[2, :, lanes], pool[4, :, lanes]]
        dqs, dks, dvs = [], [[], []], [[], []]
        for head in range(2):
            part = slice(head * HD, head * HD + HD)
            q, dmix = q2[:, part], dm2[:, part]
            base = logs_ref[pair, head : head + 1, :]
            chance = [jnp.exp2(dot_nt(k[:, part], q) * LOG2E - base) for k in k2]
            grads = [dot_nt(v[:, part], dmix) for v in v2]
            inner = functools.reduce(
                jnp.add, [jnp.sum(w * g, axis=0, keepdims=True) for w, g in zip(chance, grads)]
            )
            dq = None
            for i in range(2):
                ds = (chance[i] * (grads[i] - inner)).astype(BF)
                term = dot_tn(ds, k2[i][:, part])
                dq = term if dq is None else dq + term
                dks[i].append(dot_nn(ds, q))
                dvs[i].append(dot_nn(chance[i].astype(BF), dmix))
            dqs.append(dq)
        dq = jnp.concatenate(dqs, axis=1).astype(BF).astype(F32) * SCALE
        mixed_ref[:, lanes] = dq.astype(BF)
        sums_ref[10:11, lanes] = total_rows(dq)
        for i, ref in enumerate((near_ref, far_ref)):
            ref[0, :, lanes] = jnp.concatenate(dks[i], axis=1).astype(BF)
            ref[1, :, lanes] = jnp.concatenate(dvs[i], axis=1).astype(BF)
        swap(pair).start()

    back_out.back_end(near_ref, 1, outputs_ref)
    pairs = width // (2 * HD)
    loop(2, attend)
    advances(6)
    loop(2, lambda i: attend(2 + i))
    advances(7)
    loop(2, lambda i: attend(4 + i))
    loop(pairs - 6, lambda i: attend(6 + i))
    advances(8)
    x_load.wait()
    give(9, y_ref, mixed_ref)

    def both(pair):
        swap(pair).wait_recv()
        lanes = chunk(pair, 2 * HD)
        for i in range(2):
            total = near_ref[i, :, lanes].astype(F32) + swap_ref[i, :, lanes].astype(F32)
            low = total.astype(BF)
            near_ref[i, :, lanes] = low
            if i == 1:
                sums_ref[11:12, lanes] = total_rows(low.astype(F32))

    loop(pairs, both)
    arrive(9)
    give(10, y_ref, near_ref.at[1])
    hold(9, y_ref, mixed_ref)
    arrive(10)
    give(11, y_ref, near_ref.at[0])
    hold(10, y_ref, near_ref.at[1])
    arrive(11)
    advances(9)
    hold(11, y_ref, near_ref.at[0])

    value = sums_ref[0:8, :]
    thirds = []
    for _ in range(3):
        thirds.append(value.astype(BF))
        value = value - thirds[-1].astype(F32)
    value = dot_nt(jnp.concatenate(thirds, axis=0), cube.shuffle(width))
    sums_ref[0:6, :] = (value[0:8] + value[8:16] + value[16:24])[0:6, :]

    rounds = [{"dp": p, "tensor": cube.z} for p in partners]
    rounds += [{"dp": cube.place, "tensor": cube.z ^ 1}, {"dp": cube.place, "tensor": cube.z ^ 2}]

    def pool_sums(i):
        return remote(sums_ref, sums_in.at[i], sum_send.at[i], sum_recv.at[i], rounds[i])

    def next_sum(i):
        if i > 0:
            pool_sums(i - 1).wait()
            sums_ref[...] += sums_in[i - 1]
        if i < len(rounds):
            pool_sums(i).start()

    next_sum(0)

    def fold_in(kind, slot, right):
        weight(kind, slot).wait()

        def part(z):
            value = dot_nt(right[:, chunk(z, cols)], weight_tile(wbuf, slot, z))
            dh_ref[...] += value

        loop(parts, part)

    fold_in(0, 0, mixed_ref)
    weight(2, 0).start()
    next_sum(1)
    fold_in(1, 1, near_ref.at[0])
    next_sum(2)
    advances(10)
    fold_in(2, 0, near_ref.at[1])
    next_sum(3)
    swaps_done = lambda pair: swap(pair).wait_send()
    loop(pairs, swaps_done)
    far_ref[0] = dot_nt(dh_ref[...].astype(BF), cube.shuffle(width)).astype(BF)

    def send_in(piece):
        back_in.back(far_ref, 0, back_ref, piece, pieces)

    loop(4, send_in)
    advances(11)
    for i in range(4, len(rounds) + 1):
        next_sum(i)
    loop(4, lambda i: send_in(4 + i))
    advances(12)
    back_in.back_end(far_ref, 0, back_ref)
    back_in.back_wait(far_ref, 0, back_ref)
    result = []
    for m in range(2):
        at = slice(m * (rows // 2), (m + 1) * (rows // 2))
        acc_ref[at, :] = back_ref[m].astype(F32)
        copy = pltpu.make_async_copy(acc_ref.at[at], input_ref.at[m], out_sem.at[m])
        copy.start()
        result.append(copy)
    sums_out[...] = sums_ref[...]
    advances(SUBS + top)

    for r in range(SUBS - 3, SUBS):
        stage(r, top).wait_send()
    back_out.back_wait(near_ref, 1, outputs_ref)
    for copy in result:
        copy.wait()


def backward(vectors, second_sums, held, count, parts):
    (weights, x, qkv, other, mixed, logs, z1, r1, y1, gated, slope, normed_rows, dh2, b2) = held
    subs, _, _, depth, cols = weights.shape
    rows, width = x.shape
    levels = count.bit_length() - 1
    half = count // 2
    pairs = width // (2 * HD)
    dma = pltpu.SemaphoreType.DMA
    low = lambda *shape: (shape, BF)
    high = lambda *shape: (shape, F32)
    hbm = pl.BlockSpec(memory_space=pl.ANY)
    vmem = pl.BlockSpec(memory_space=pltpu.VMEM)
    results = [
        high(subs, depth, cols),
        high(16, width),
        low(2, rows // 2, width),
        high(2, rows // 2, width),
        low(subs, half, parts, depth, cols),
    ]
    scratch = [
        low(8, rows, width),
        high(pairs, 8, rows),
        low(rows, width),
        high(rows, width),
        high(rows, width),
        high(rows, 128),
        low(rows, width),
        low(rows, width),
        high(rows, width),
        low(2, rows, width),
        low(2, rows, width),
        low(2, rows, width),
        low(2, rows // 2, width),
        low(2, count, parts, depth, cols),
        low(3, half, parts, depth, cols),
        low(2, half, parts, depth, cols),
        low(HELD, half, parts, depth, cols),
        low(subs, half - 1, parts, depth, cols),
        low(subs, parts - 1, depth, cols),
        high(16, width),
        high(levels + 2, 16, width),
    ]
    return pl.pallas_call(
        functools.partial(backward_kernel, count, parts),
        in_specs=[vmem, vmem] + [hbm] * 14,
        out_specs=[vmem, vmem, hbm, hbm, hbm],
        out_shape=[jax.ShapeDtypeStruct(*r) for r in results],
        scratch_shapes=[pltpu.VMEM(*s) for s in scratch]
        + [
            dma((15,)),
            dma((2,)),
            dma((2,)),
            dma((subs, levels)),
            dma((subs, levels)),
            dma((subs, parts - 1)),
            dma((subs, parts - 1)),
            dma((pairs,)),
            dma((pairs,)),
            dma((2, 2)),
            dma((2, 2)),
            dma((2,)),
            dma((levels + 2,)),
            dma((levels + 2,)),
            dma((2,)),
        ],
        compiler_params=pltpu.CompilerParams(
            collective_id=2, has_side_effects=True, vmem_limit_bytes=62 * MIB
        ),
    )(vectors, second_sums, weights, x, qkv, other, mixed, logs, z1, r1, y1, gated, slope, normed_rows, dh2, b2)


def shards(
    inputs,
    query_weight,
    query_bias,
    key_weight,
    value_weight,
    value_bias,
    out_weight,
    out_bias,
    first_gain,
    first_shift,
    up_weight,
    up_bias,
    down_weight,
    down_bias,
    second_gain,
    second_shift,
    cotangent,
):
    count, parts = lax.axis_size("dp"), lax.axis_size("tensor")
    z = lax.axis_index("tensor")
    width = inputs.shape[-1]
    depth = width // count
    cols = query_weight.shape[1]
    cube = Cube(count, parts)
    owner = jnp.asarray(cube.masks(), jnp.int32)[cube.core] ^ cube.place

    vectors = jnp.stack(
        [out_bias, first_gain, first_shift, down_bias, second_gain, second_shift]
        + [jnp.zeros_like(out_bias)] * 2
    )
    vectors = vectors.reshape(8, count, depth)[:, owner].reshape(8, width)

    def split(value):
        return [value[..., i : i + cols] for i in range(0, value.shape[-1], cols)]

    local = jnp.stack(
        [query_weight, key_weight, value_weight, out_weight.T] + split(up_weight) + split(down_weight.T)
    )
    bias = jnp.stack([query_bias, value_bias] + split(up_bias))
    bias = jnp.concatenate([bias, jnp.zeros_like(bias[:2])])
    *held, second_sums = forward(local, bias, vectors, inputs, cotangent, count, parts)
    grads, sums, outputs, input_grad, _ = backward(vectors, second_sums, held, count, parts)

    grad = {sub: grads[r] for r, sub in enumerate(ORDER)}
    up_grad = jnp.concatenate([grad[UP + i] for i in range(4)], axis=1)
    down_grad = jnp.concatenate([grad[DOWN + i].T for i in range(4)], axis=0)
    mine = lambda row: lax.dynamic_slice_in_dim(row, z * cols, cols)
    up_bias_grad = jnp.concatenate([mine(sums[6 + i]) for i in range(4)])
    return (
        outputs,
        input_grad,
        grad[0],
        mine(sums[10]),
        grad[1],
        grad[2],
        mine(sums[11]),
        grad[3].T,
        sums[2],
        sums[0],
        sums[1],
        up_grad,
        up_bias_grad,
        down_grad,
        sums[5],
        sums[3],
        sums[4],
    )


def solution(mesh):
    rows = P(None, ("dp", "tensor"), None)
    return jax.shard_map(
        shards,
        mesh=mesh,
        in_specs=(
            rows,
            P("dp", "tensor"),
            P("tensor"),
            P("dp", "tensor"),
            P("dp", "tensor"),
            P("tensor"),
            P("tensor", "dp"),
            P(),
            P(),
            P(),
            P("dp", "tensor"),
            P("tensor"),
            P("tensor", "dp"),
            P(),
            P(),
            P(),
            rows,
        ),
        out_specs=(
            rows,
            rows,
            P("dp", "tensor"),
            P("tensor"),
            P("dp", "tensor"),
            P("dp", "tensor"),
            P("tensor"),
            P("tensor", "dp"),
            P(),
            P(),
            P(),
            P("dp", "tensor"),
            P("tensor"),
            P("tensor", "dp"),
            P(),
            P(),
            P(),
        ),
        check_vma=False,
    )
```

```python
import functools
import math

import jax
import jax.numpy as jnp
from jax import lax
from jax.experimental import pallas as pl
from jax.experimental.pallas import tpu as pltpu
from jax.sharding import PartitionSpec as P

HD = 64
LEN = 1024
EPSILON = 1e-05
SCALE = HD ** (-0.5)
LOG2E = math.log2(math.e)
BF = jnp.bfloat16
F32 = jnp.float32
MIB = 1 << 20


def dot_nn(left, right):
    return jnp.dot(left, right, preferred_element_type=F32)


def dot_nt(left, right):
    return lax.dot_general(left, right, (((1,), (1,)), ((), ())), preferred_element_type=F32)


def dot_tn(left, right):
    return lax.dot_general(left, right, (((0,), (0,)), ((), ())), preferred_element_type=F32)


OUT_BIAS, FIRST_GAIN, FIRST_SHIFT, DOWN_BIAS, SECOND_GAIN, SECOND_SHIFT = range(6)


def vector(ref, place):
    return ref[place : place + 1, :]


def normed(hidden):
    average = jnp.mean(hidden, axis=-1, keepdims=True)
    center = hidden - average
    spread = jnp.mean(center * center, axis=-1, keepdims=True)
    inverse = lax.rsqrt(spread + EPSILON)
    return center * inverse, inverse


def norm_back(grad, z, inverse, gain):
    scaled = grad * gain
    average = jnp.mean(scaled, axis=-1, keepdims=True)
    along = jnp.mean(scaled * z, axis=-1, keepdims=True)
    return (scaled - average - z * along) * inverse


def total_rows(value):
    return jnp.sum(value, axis=0, keepdims=True)


def remote(source, target, send, receive, device):
    return pltpu.make_async_remote_copy(
        source, target, send, receive, device_id=device, device_id_type=pl.DeviceIdType.MESH
    )


def greet(devices):
    barrier = pltpu.get_barrier_semaphore()
    for device in devices:
        pl.semaphore_signal(barrier, 1, device_id=device, device_id_type=pl.DeviceIdType.MESH)
    pl.semaphore_wait(barrier, len(devices))


class Cube:
    def __init__(self, count, parts):
        self.count, self.parts, self.half = count, parts, parts // 2
        self.place, self.z = lax.axis_index("dp"), lax.axis_index("tensor")
        self.core = lax.rem(self.place, 2)
        self.levels = count.bit_length() - 1
        bits = [1 << i for i in range(1, self.levels)]
        self.orders = [bits, bits[::-1]]

    def stages(self):
        ups, downs = self.orders
        out = []
        for up, down in zip(ups, downs):
            out.append(self.place ^ jnp.where(self.core == 0, up, down))
        return out + [self.place ^ 1]

    def masks(self):
        table = []
        for order in self.orders:
            held = [0]
            for bit in order:
                held = held + [m ^ bit for m in held]
            table.append(held)
        return [a + [m ^ 1 for m in b] for a, b in (table, table[::-1])]

    def column(self):
        mine = [{"dp": self.place, "tensor": lax.rem(self.z + d, self.parts)} for d in range(1, self.parts)]
        others = [{"dp": self.place ^ 1, "tensor": lax.rem(self.z + d, self.parts)} for d in range(self.parts)]
        return mine + others

    def neighbours(self):
        return [{"dp": p, "tensor": self.z} for p in self.stages()[:-1]]

    def shuffle(self, width):
        depth = width // self.count
        column = lax.broadcasted_iota(jnp.int32, (1, width), 1)
        slot = column // depth
        far = slot // (self.count // 2)
        flips = far
        for level, (up, down) in enumerate(zip(*self.orders)):
            bit = jnp.where(self.core == 0, up, down)
            other = jnp.where(self.core == 0, down, up)
            held = lax.rem(slot // (1 << level), 2)
            flips = flips + held * jnp.where(far == 0, bit, other)
        owner = self.place ^ flips
        source = owner * depth + lax.rem(column, depth)
        row = lax.broadcasted_iota(jnp.int32, (width, width), 0)
        return (row == source).astype(F32).astype(BF)


class Rows:
    def __init__(self, cube, send, receive, here):
        self.cube, self.send, self.receive, self.here = cube, send, receive, here
        c = cube
        self.slot = lax.rem(c.z, c.half)
        self.targets = [(c.place - c.core + c.z // c.half, m * c.half + c.core) for m in range(2)]
        self.micro = c.z // c.half
        self.sources = [(c.place - c.core + lax.rem(c.z, c.half), c.half * c.core + p) for p in range(2)]

    def own(self, device):
        return jnp.logical_and(device[0] == self.cube.place, device[1] == self.cube.z)

    def at(self, device):
        return {"dp": device[0], "tensor": device[1]}

    def into(self, source, target, piece, pieces):
        size = source.shape[1] // pieces
        at = pl.ds(pl.multiple_of(piece * size, size), size)
        for m, device in enumerate(self.targets):
            own = self.own(device)

            @pl.when(own)
            def _(m=m):
                pltpu.make_async_copy(source.at[m, at], target.at[self.slot, at], self.here).start()

            @pl.when(jnp.logical_not(own))
            def _(m=m, device=device):
                remote(
                    source.at[m, at],
                    target.at[self.slot, at],
                    self.send.at[m],
                    self.receive.at[self.slot],
                    self.at(device),
                ).start()

    def into_wait(self, source, target):
        for p, device in enumerate(self.sources):
            own = self.own(device)

            @pl.when(own)
            def _(p=p):
                pltpu.make_async_copy(source.at[0], target.at[p], self.here).wait()

            @pl.when(jnp.logical_not(own))
            def _(p=p, device=device):
                remote(
                    source.at[0], target.at[p], self.send.at[0], self.receive.at[p], self.at(device)
                ).wait_recv()

    def into_end(self, source, target):
        for m, device in enumerate(self.targets):

            @pl.when(jnp.logical_not(self.own(device)))
            def _(m=m, device=device):
                remote(
                    source.at[m], target.at[self.slot], self.send.at[m], self.receive.at[0], self.at(device)
                ).wait_send()


    def back(self, source, lead, target, piece, pieces):
        size = target.shape[1] // pieces
        for p, device in enumerate(self.sources):
            own = self.own(device)
            here = pl.ds(pl.multiple_of(p * target.shape[1] + piece * size, size), size)
            there = pl.ds(pl.multiple_of(piece * size, size), size)

            @pl.when(own)
            def _(here=here, there=there):
                pltpu.make_async_copy(
                    source.at[lead, here], target.at[self.micro, there], self.here
                ).start()

            @pl.when(jnp.logical_not(own))
            def _(p=p, device=device, here=here, there=there):
                remote(
                    source.at[lead, here],
                    target.at[self.micro, there],
                    self.send.at[p],
                    self.receive.at[self.micro],
                    self.at(device),
                ).start()

    def back_wait(self, source, lead, target):
        rows = target.shape[1]
        for m, device in enumerate(self.targets):

            @pl.when(jnp.logical_not(self.own(device)))
            def _(m=m, device=device):
                remote(
                    source.at[lead, pl.ds(0, rows)],
                    target.at[m],
                    self.send.at[0],
                    self.receive.at[m],
                    self.at(device),
                ).wait_recv()

    def back_end(self, source, lead, target):
        rows = target.shape[1]
        for p, device in enumerate(self.sources):
            own = self.own(device)

            @pl.when(own)
            def _(p=p):
                pltpu.make_async_copy(
                    source.at[lead, pl.ds(p * rows, rows)], target.at[self.micro], self.here
                ).wait()

            @pl.when(jnp.logical_not(own))
            def _(p=p, device=device):
                remote(
                    source.at[lead, pl.ds(p * rows, rows)],
                    target.at[self.micro],
                    self.send.at[p],
                    self.receive.at[0],
                    self.at(device),
                ).wait_send()


SUBS, UP, DOWN = 12, 4, 8
XP, CS, CP = 4, 4, 8


def loop(count, body):
    lax.fori_loop(0, count, lambda i, _: (body(i), None)[1], None)


def chunk(i, size):
    return pl.ds(pl.multiple_of(i * size, size), size)


def weight_tile(ref, slot, z):
    value = ref[slot, :, z]
    return value.reshape(-1, value.shape[-1])


def forward_kernel(
    count,
    parts,
    q_in,
    k_in,
    v_in,
    o_in,
    up_in,
    down_in,
    q_bias,
    v_bias,
    up_bias,
    vec0,
    vec1,
    vec2,
    vec3,
    vec4,
    vec5,
    in_ref,
    cot_ref,
    weights_ref,
    vec_out,
    x_out,
    qkv_out,
    other_out,
    mixed_out,
    logs_out,
    z1_out,
    r1_out,
    y1_out,
    gated_out,
    slope_out,
    normed_out,
    dh2_out,
    b2_out,
    sums_out,
    local_ref,
    o_raw,
    down_raw,
    bias_ref,
    vec_ref,
    raw_ref,
    cot_raw,
    shuffle_ref,
    x_ref,
    c_ref,
    bias_all,
    qkv_ref,
    other_ref,
    mixed_ref,
    logs_ref,
    z1_ref,
    r1_ref,
    y1_ref,
    gated_ref,
    slope_ref,
    acc_ref,
    normed_ref,
    dh2_ref,
    b2_ref,
    sums_ref,
    wbuf,
    prep_sem,
    local_sem,
    zs,
    zr,
    ss,
    sr,
    wsem,
    bias_send,
    bias_recv,
    row_send,
    row_recv,
    row_here,
    kv_send,
    kv_recv,
    out_sem,
):
    cube = Cube(count, parts)
    partners, levels = cube.stages(), cube.levels
    shifts = [lax.rem(cube.z + d, parts) for d in range(1, parts)]
    ahead = 5
    rows = x_ref.shape[0]
    cols = weights_ref.shape[-1]
    depth = weights_ref.shape[-2]
    sources = [q_in, k_in, v_in] + [up_in.at[:, i * cols : (i + 1) * cols] for i in range(4)]
    places = [local_ref.at[i] for i in (0, 1, 2, 4, 5, 6, 7)]
    prep = [
        pltpu.make_async_copy(source, place, prep_sem.at[i])
        for i, (source, place) in enumerate(zip(sources + [o_in, down_in], places + [o_raw, down_raw]))
    ]
    for copy in prep:
        copy.start()
    bias_ref[...] = jnp.zeros_like(bias_ref)
    bias_ref[0:1, :] = q_bias[...]
    bias_ref[1:2, :] = v_bias[...]
    for i in range(4):
        bias_ref[2 + i : 3 + i, :] = up_bias[:, i * cols : (i + 1) * cols]
    same = lax.broadcasted_iota(jnp.int32, (depth, depth), 0) == lax.broadcasted_iota(
        jnp.int32, (depth, depth), 1
    )
    eye = same.astype(F32).astype(BF)
    greet(cube.column() + cube.neighbours())
    for i in range(3):
        prep[i].wait()

    def own(sub):
        return pltpu.make_async_copy(local_ref.at[sub], weights_ref.at[sub, 0, cube.z], local_sem.at[sub])

    inner = jnp.logical_or(cube.z == 1, cube.z == 2)
    mine, theirs = cube.z // 2 * 2, 2 - cube.z // 2 * 2

    def along(sub, hop):
        if hop == 0:
            source, target, z = local_ref.at[sub], weights_ref.at[sub, 0, cube.z], cube.z ^ 1
        else:
            source = weights_ref.at[sub, 0, pl.ds(mine if hop == 1 else theirs, 2)]
            target, z = source, (3 - cube.z if hop == 1 else cube.z ^ 1)
        return remote(
            source, target, zs.at[sub, hop], zr.at[sub, hop], {"dp": cube.place, "tensor": z}
        )

    def stage(sub, level):
        size = 1 << level
        return remote(
            weights_ref.at[sub, pl.ds(0, size)],
            weights_ref.at[sub, pl.ds(size, size)],
            ss.at[sub, level],
            sr.at[sub, level],
            {"dp": partners[level], "tensor": cube.z},
        )

    def begin(sub):
        own(sub).start()
        along(sub, 0).start()

    def pass_pair(sub):
        own(sub).wait()
        along(sub, 0).wait_recv()

        @pl.when(inner)
        def _():
            along(sub, 1).start()

    def pass_on(sub):
        @pl.when(inner)
        def _():
            along(sub, 1).wait_recv()
            along(sub, 2).start()

    def relay(step):
        @pl.when(step < SUBS)
        def _():
            @pl.when(jnp.logical_not(inner))
            def _():
                along(step, 2).wait_recv()

            stage(step, 0).start()

        for level in range(levels):
            sub = step - level - 1

            @pl.when(jnp.logical_and(sub >= 0, sub < SUBS))
            def _(sub=sub, level=level):
                stage(sub, level).wait_recv()
                if level + 1 < levels:
                    stage(sub, level + 1).start()

        @pl.when(step < XP)
        def _():
            rows_x.into(in_ref, raw_ref, step, XP)

        @pl.when(jnp.logical_and(step >= CS, step < CS + CP))
        def _():
            rows_c.into(cot_ref, cot_raw, step - CS, CP)

        @pl.when(step + 1 < SUBS)
        def _():
            pass_on(step + 1)

        @pl.when(step + 2 < SUBS)
        def _():
            pass_pair(step + 2)

        @pl.when(step + ahead < SUBS)
        def _():
            begin(step + ahead)

    def relays(first, last):
        loop(last - first, lambda i: relay(first + i))

    def load(sub):
        return pltpu.make_async_copy(weights_ref.at[sub], wbuf.at[sub % 4], wsem.at[sub % 4])

    def share_bias(d):
        return remote(
            bias_ref,
            bias_all.at[cube.z],
            bias_send.at[d],
            bias_recv.at[d],
            {"dp": cube.place, "tensor": shifts[d]},
        )

    rows_x = Rows(cube, row_send.at[0], row_recv.at[0], row_here.at[0])
    rows_c = Rows(cube, row_send.at[1], row_recv.at[1], row_here.at[1])
    outs = []

    def keep(source, target):
        copy = pltpu.make_async_copy(source, target, out_sem.at[len(outs)])
        copy.start()
        outs.append(copy)

    loop(3, begin)
    for copy in prep[3:]:
        copy.wait()
    local_ref[3] = dot_nt(eye, o_raw[...]).astype(BF)
    loop(ahead - 3, lambda i: begin(3 + i))
    for i in range(4):
        local_ref[DOWN + i] = dot_nt(eye, down_raw[i * cols : (i + 1) * cols, :]).astype(BF)
    for d in range(parts - 1):
        share_bias(d).start()
    pass_pair(0)
    pass_pair(1)
    pass_on(0)
    shuffle_ref[...] = cube.shuffle(x_ref.shape[1])
    bias_all[cube.z] = bias_ref[...]
    value = jnp.concatenate([v[...] for v in (vec0, vec1, vec2, vec3, vec4, vec5)] + [vec0[...]] * 2, axis=0)
    thirds = []
    for _ in range(3):
        thirds.append(value.astype(BF))
        value = value - thirds[-1].astype(F32)
    value = dot_nn(jnp.concatenate(thirds, axis=0), shuffle_ref[...])
    vec_ref[...] = value[0:8] + value[8:16] + value[16:24]
    keep(vec_ref, vec_out)
    relays(0, levels + 1)
    rows_x.into_wait(in_ref, raw_ref)
    half_rows = raw_ref.shape[1]
    for p in range(2):
        x_ref[p * half_rows : (p + 1) * half_rows, :] = dot_nn(raw_ref[p], shuffle_ref[...]).astype(BF)
    keep(x_ref, x_out)
    for d in range(parts - 1):
        share_bias(d).wait_recv()

    for kind in range(3):
        load(kind).start()
        if kind < 2:
            relays(levels + kind + 1, levels + kind + 2)
        load(kind).wait()

        def project(z, kind=kind):
            acc = dot_nn(x_ref[...], weight_tile(wbuf, kind, z))
            if kind == 0:
                acc = (acc + bias_all[z, 0:1, :]) * SCALE
            elif kind == 2:
                acc = acc + bias_all[z, 1:2, :]
            qkv_ref[kind, :, chunk(z, cols)] = acc.astype(BF)

        loop(parts, project)

    swap = remote(qkv_ref.at[pl.ds(1, 2)], other_ref, kv_send, kv_recv, {"dp": cube.place ^ 1, "tensor": cube.z})
    swap.start()
    keep(qkv_ref, qkv_out)
    relays(levels + 3, levels + 4)
    swap.wait_recv()
    keep(other_ref, other_out)

    def attend(pair):
        lanes = chunk(pair, 2 * HD)
        q2 = qkv_ref[0, :, lanes]
        k2 = [qkv_ref[1, :, lanes], other_ref[0, :, lanes]]
        v2 = [qkv_ref[2, :, lanes], other_ref[1, :, lanes]]
        mixed, logs = [], []
        for head in range(2):
            part = slice(head * HD, head * HD + HD)
            scores = [dot_nt(k[:, part], q2[:, part]) for k in k2]
            top = functools.reduce(jnp.maximum, [jnp.max(s, axis=0, keepdims=True) for s in scores])
            base = top * LOG2E
            expo = [jnp.exp2(s * LOG2E - base) for s in scores]
            total = functools.reduce(jnp.add, [jnp.sum(e, axis=0, keepdims=True) for e in expo])
            inverse = 1.0 / total
            mixed.append(
                functools.reduce(
                    jnp.add, [dot_tn((e * inverse).astype(BF), v[:, part]) for e, v in zip(expo, v2)]
                )
            )
            logs.append(base + jnp.log2(total))
        mixed_ref[:, lanes] = jnp.concatenate(mixed, axis=1).astype(BF)
        logs_ref[pair] = jnp.concatenate(logs + [jnp.zeros((6, rows), F32)], axis=0)

    pairs = mixed_ref.shape[1] // (2 * HD)
    loop(pairs // 2, attend)
    relays(levels + 4, levels + 5)
    loop(pairs // 2, lambda i: attend(pairs // 2 + i))
    relays(levels + 5, levels + 6)
    keep(mixed_ref, mixed_out)
    keep(logs_ref, logs_out)

    load(3).start()
    load(4).start()
    load(3).wait()

    def mix(z):
        value = dot_nt(mixed_ref[:, chunk(z, cols)], weight_tile(wbuf, 3, z))

        @pl.when(z == 0)
        def _():
            acc_ref[...] = value

        @pl.when(z > 0)
        def _():
            acc_ref[...] += value

    loop(parts, mix)
    size = 128

    def norm_first(i):
        at = chunk(i, size)
        hidden = x_ref[at, :].astype(F32) + acc_ref[at, :] + vector(vec_ref, OUT_BIAS)
        z, inverse = normed(hidden)
        z1_ref[at, :] = z
        r1_ref[at, :] = jnp.broadcast_to(inverse, (size, 128))
        y = z * vector(vec_ref, FIRST_GAIN) + vector(vec_ref, FIRST_SHIFT)
        y1_ref[at, :] = y.astype(BF)
        acc_ref[at, :] = y + vector(vec_ref, DOWN_BIAS)

    loop(rows // size, norm_first)
    keep(z1_ref, z1_out)
    keep(r1_ref, r1_out)
    keep(y1_ref, y1_out)

    def gate(sub):
        load(sub).wait()

        def part(z):
            lanes = chunk(z, cols)
            upper = dot_nn(y1_ref[...], weight_tile(wbuf, sub % 4, z)) + bias_all[z, sub - UP + 2 : sub - UP + 3, :]
            half = 0.5 + 0.5 * lax.erf(upper * (0.5**0.5))
            gated_ref[sub - UP, :, lanes] = (upper * half).astype(BF)
            bell = jnp.exp(upper * upper * -0.5) * ((2 * math.pi) ** -0.5)
            slope_ref[sub - UP, :, lanes] = (half + upper * bell).astype(BF)

        loop(parts, part)
        keep(gated_ref.at[sub - UP], gated_out.at[sub - UP])
        keep(slope_ref.at[sub - UP], slope_out.at[sub - UP])

    last = SUBS + levels
    done = levels + 6
    for sub in range(UP, DOWN):
        gate(sub)
        if done < last:
            relays(done, done + 1)
            done += 1
        if sub + 1 < DOWN:
            load(sub + 1).start()

    rows_c.into_wait(cot_ref, cot_raw)
    for p in range(2):
        c_ref[p * half_rows : (p + 1) * half_rows, :] = dot_nn(cot_raw[p], shuffle_ref[...]).astype(BF)

    for sub in range(DOWN, SUBS):
        if done < sub + levels + 1:
            relays(done, sub + levels + 1)
            done = sub + levels + 1
        load(sub).start()
        load(sub).wait()

        def fold(z, sub=sub):
            acc_ref[...] += dot_nt(gated_ref[sub - DOWN, :, chunk(z, cols)], weight_tile(wbuf, sub % 4, z))

        loop(parts, fold)

    sums_ref[...] = jnp.zeros_like(sums_ref)

    def norm_second(i):
        at = chunk(i, size)
        z, inverse = normed(acc_ref[at, :])
        gain = vector(vec_ref, SECOND_GAIN)
        normed_ref[at, :] = (z * gain + vector(vec_ref, SECOND_SHIFT)).astype(BF)
        grad = c_ref[at, :].astype(F32)
        dh = norm_back(grad, z, inverse, gain)
        dh2_ref[at, :] = dh
        b2_ref[at, :] = dh.astype(BF)
        sums_ref[0:1, :] += total_rows(grad * z)
        sums_ref[1:2, :] += total_rows(grad)
        sums_ref[2:3, :] += total_rows(dh)

    loop(rows // size, norm_second)
    keep(normed_ref, normed_out)
    keep(dh2_ref, dh2_out)
    keep(b2_ref, b2_out)
    keep(sums_ref, sums_out)

    def sent(sub):
        along(sub, 0).wait_send()

        @pl.when(inner)
        def _():
            along(sub, 1).wait_send()
            along(sub, 2).wait_send()

        for level in range(levels):
            stage(sub, level).wait_send()

    loop(SUBS, sent)
    for d in range(parts - 1):
        share_bias(d).wait_send()
    swap.wait_send()
    rows_x.into_end(in_ref, raw_ref)
    rows_c.into_end(cot_ref, cot_raw)
    for copy in outs:
        copy.wait()


def forward(weights, biases, vectors, inputs, cotangent, count, parts):
    subs = SUBS
    depth, cols = weights[0].shape
    _, half_rows, width = inputs.shape
    rows = 2 * half_rows
    levels = count.bit_length() - 1
    pairs = width // (2 * HD)
    dma = pltpu.SemaphoreType.DMA
    low = lambda *shape: (shape, BF)
    high = lambda *shape: (shape, F32)
    results = [
        low(subs, count, parts, depth, cols),
        high(8, width),
        low(rows, width),
        low(3, rows, width),
        low(2, rows, width),
        low(rows, width),
        high(pairs, 8, rows),
        high(rows, width),
        high(rows, 128),
        low(rows, width),
        low(4, rows, parts * cols),
        low(4, rows, parts * cols),
        low(rows, width),
        high(rows, width),
        low(rows, width),
        high(8, width),
    ]
    scratch = [
        low(subs, depth, cols),
        low(cols, depth),
        low(4 * cols, depth),
        high(8, cols),
        high(8, width),
        low(2, half_rows, width),
        low(2, half_rows, width),
        low(width, width),
        low(rows, width),
        low(rows, width),
        high(parts, 8, cols),
        low(3, rows, width),
        low(2, rows, width),
        low(rows, width),
        high(pairs, 8, rows),
        high(rows, width),
        high(rows, 128),
        low(rows, width),
        low(4, rows, parts * cols),
        low(4, rows, parts * cols),
        high(rows, width),
        low(rows, width),
        high(rows, width),
        low(rows, width),
        high(8, width),
        low(4, count, parts, depth, cols),
    ]
    hbm = pl.BlockSpec(memory_space=pl.ANY)
    vmem = pl.BlockSpec(memory_space=pltpu.VMEM)
    return pl.pallas_call(
        functools.partial(forward_kernel, count, parts),
        in_specs=[hbm] * 6 + [vmem] * 9 + [hbm, hbm],
        out_specs=[hbm] * len(results),
        out_shape=[jax.ShapeDtypeStruct(*r) for r in results],
        scratch_shapes=[pltpu.VMEM(*s) for s in scratch]
        + [
            dma((9,)),
            dma((subs,)),
            dma((subs, 3)),
            dma((subs, 3)),
            dma((subs, levels)),
            dma((subs, levels)),
            dma((4,)),
            dma((parts - 1,)),
            dma((parts - 1,)),
            dma((2, 2)),
            dma((2, 2)),
            dma((2,)),
            dma,
            dma,
            dma((24,)),
        ],
        compiler_params=pltpu.CompilerParams(
            collective_id=1, has_side_effects=True, vmem_limit_bytes=60 * MIB
        ),
    )(*weights, *biases, *vectors, inputs, cotangent)


HELD, RING, LINE = 5, 2, 4
ORDER = [8, 9, 10, 11, 3, 4, 5, 6, 7, 0, 2, 1]


def backward_kernel(
    count,
    parts,
    vec_ref,
    second_ref,
    weights_ref,
    x_in,
    qkv_in,
    other_in,
    mixed_in,
    logs_in,
    z1_in,
    r1_in,
    y1_in,
    gated_in,
    slope_in,
    normed_in,
    dh2_in,
    b2_in,
    grads_ref,
    sums_out,
    outputs_ref,
    back_ref,
    pool,
    logs_ref,
    y_ref,
    dh_ref,
    z1_ref,
    r1_ref,
    b_ref,
    mixed_ref,
    near_ref,
    far_ref,
    swap_ref,
    wbuf,
    send_ref,
    staged_ref,
    held_ref,
    line_ref,
    small_ref,
    zed_ref,
    sums_ref,
    sums_in,
    load_sem,
    wsem,
    free_sem,
    ss,
    sr,
    zs,
    zr,
    swap_send,
    swap_recv,
    row_send,
    row_recv,
    row_here,
    sum_send,
    sum_recv,
):
    cube = Cube(count, parts)
    partners, levels = cube.stages(), cube.levels
    top = levels - 1
    half = count // 2
    shifts = [lax.rem(cube.z + d, parts) for d in range(1, parts)]
    rows, width = b_ref.shape
    cols = weights_ref.shape[-1]
    depth = weights_ref.shape[-2]
    wide = half * depth
    size = 128
    greet(cube.column() + cube.neighbours())

    def load(place, source, target):
        return pltpu.make_async_copy(source, target, load_sem.at[place])

    def weight(sub, slot):
        return pltpu.make_async_copy(weights_ref.at[sub], wbuf.at[slot], wsem.at[slot])

    gate_load = [load(j % 2, gated_in.at[j], pool.at[j % 2]) for j in range(4)]
    slope_load = [load(2 + j % 2, slope_in.at[j], pool.at[2 + j % 2]) for j in range(4)]
    b_load = load(4, b2_in, b_ref)
    out_load = load(5, normed_in, near_ref.at[0])
    y_load = load(6, y1_in, y_ref)
    dh_load = load(7, dh2_in, dh_ref)
    z_load = load(8, z1_in, z1_ref)
    r_load = load(9, r1_in, r1_ref)
    mixed_load = load(10, mixed_in, mixed_ref)
    logs_load = load(11, logs_in, logs_ref)
    qkv_load = load(12, qkv_in, pool.at[pl.ds(0, 3)])
    other_load = load(13, other_in, pool.at[pl.ds(8, 2)])
    x_load = load(14, x_in, y_ref)

    def stage(r, level):
        if level == top:
            source, target = send_ref.at[lax.rem(r, RING)], staged_ref.at[lax.rem(r, RING)]
        else:
            source = held_ref.at[lax.rem(r, HELD), pl.ds(1 << level, 1 << level)]
            target = small_ref.at[r, pl.ds((1 << level) - 1, 1 << level)]
        return remote(
            source, target, ss.at[r, level], sr.at[r, level], {"dp": partners[level], "tensor": cube.z}
        )

    inner = jnp.logical_or(cube.z == 1, cube.z == 2)
    mine, theirs = cube.z // 2 * 2, 2 - cube.z // 2 * 2

    def along(r, hop):
        line = lax.rem(r, LINE)
        if hop == 0:
            source = line_ref.at[line, pl.ds(jnp.where(cube.z == 0, 1, 0), parts - 1)]
            target, z = zed_ref.at[r, pl.ds(0, parts - 1)], cube.z ^ 1
        elif hop == 1:
            source = line_ref.at[line, pl.ds(theirs, 2)]
            target, z = zed_ref.at[r, pl.ds(parts - 1, 2)], 3 - cube.z
        else:
            source = line_ref.at[line, cube.z ^ 1]
            target, z = zed_ref.at[r, 0], cube.z ^ 1
        return remote(source, target, zs.at[r, hop], zr.at[r, hop], {"dp": cube.place, "tensor": z})

    def add_line(r, block, place):
        line = lax.rem(r, LINE)
        value = line_ref[line, block].astype(F32) + zed_ref[r, place].astype(F32)
        line_ref[line, block] = value.astype(BF)

    def give(r, left, right):
        if r >= RING:
            stage(r - RING, top).wait_send()
        value = dot_tn(left[:, wide:], right[...]).astype(BF)
        for z in range(parts):
            send_ref[r % RING, :, z] = value[:, z * cols : (z + 1) * cols].reshape(half, depth, cols)
        if r >= RING:
            pl.semaphore_wait(free_sem, 1)
        stage(r, top).start()

    def hold(r, left, right):
        advances(r - HELD + top)
        value = dot_tn(left[:, :wide], right[...])
        stage(r, top).wait_recv()
        for z in range(parts):
            part = value[:, z * cols : (z + 1) * cols].reshape(half, depth, cols)
            part = part + staged_ref[r % RING, :, z].astype(F32)
            held_ref[r % HELD, :, z] = part.astype(BF)
        if r + RING < SUBS:
            pl.semaphore_signal(
                free_sem,
                1,
                device_id={"dp": cube.place ^ 1, "tensor": cube.z},
                device_id_type=pl.DeviceIdType.MESH,
            )
        stage(r, top - 1).start()

    def advance(k):
        for i in range(top):
            level = top - 1 - i
            r = k - i

            @pl.when(jnp.logical_and(r >= 0, r < SUBS))
            def _(r=r, level=level):
                stage(r, level).wait_recv()
                place = lax.rem(r, HELD)

                def fold(slot):
                    value = held_ref[place, slot].astype(F32)
                    value = value + small_ref[r, (1 << level) - 1 + slot].astype(F32)
                    if level > 0:
                        held_ref[place, slot] = value.astype(BF)
                    else:
                        line_ref[lax.rem(r, LINE)] = value.astype(BF)

                loop(1 << level, fold)
                if level > 0:
                    stage(r, level - 1).start()
                else:

                    @pl.when(jnp.logical_not(inner))
                    def _():
                        along(r, 0).start()

                    for other in range(top):
                        stage(r, other).wait_send()

        r = k - top

        @pl.when(jnp.logical_and(inner, jnp.logical_and(r >= 0, r < SUBS)))
        def _(r=r):
            along(r, 0).wait_recv()
            for i in range(parts - 1):
                add_line(r, jnp.where(cube.z == 1, 1, 0) + i, i)
            along(r, 1).start()

        r = k - top - 1

        @pl.when(jnp.logical_and(inner, jnp.logical_and(r >= 0, r < SUBS)))
        def _(r=r):
            along(r, 1).wait_recv()
            for i in range(2):
                add_line(r, mine + i, parts - 1 + i)
            along(r, 2).start()
            grads_ref[r] = line_ref[lax.rem(r, LINE), cube.z].astype(F32)

        r = k - top - 2

        @pl.when(jnp.logical_and(r >= 0, r < SUBS))
        def _(r=r):
            @pl.when(inner)
            def _():
                along(r, 1).wait_send()
                along(r, 2).wait_send()

            @pl.when(jnp.logical_not(inner))
            def _():
                along(r, 2).wait_recv()
                value = line_ref[lax.rem(r, LINE), cube.z].astype(F32)
                grads_ref[r] = value + zed_ref[r, 0].astype(F32)
                along(r, 0).wait_send()

    done = [0]

    def advances(last):
        if last > done[0]:
            first = done[0]
            loop(last - first, lambda i: advance(first + i))
            done[0] = last

    back_out = Rows(cube, row_send.at[0], row_recv.at[0], row_here.at[0])
    back_in = Rows(cube, row_send.at[1], row_recv.at[1], row_here.at[1])
    pieces = 8

    sums_ref[...] = jnp.zeros_like(sums_ref)
    sums_ref[3:6, :] = second_ref[0:3, :]

    b_load.start()
    gate_load[0].start()
    weight(8, 0).start()
    slope_load[0].start()
    gate_load[1].start()
    out_load.start()
    y_load.start()
    b_load.wait()
    gate_load[0].wait()
    give(0, b_ref, pool.at[0])
    slope_load[1].start()
    weight(9, 1).start()
    dh_load.start()
    z_load.start()
    r_load.start()
    mixed_load.start()
    logs_load.start()
    gate_load[1].wait()
    give(1, b_ref, pool.at[1])

    out_load.wait()
    near_ref[1] = dot_nt(near_ref[0], cube.shuffle(width)).astype(BF)

    def send_out(piece):
        back_out.back(near_ref, 1, outputs_ref, piece, pieces)

    loop(2, send_out)
    hold(0, b_ref, pool.at[0])
    gate_load[2].start()

    def gate_back(j):
        slope_load[j].wait()
        weight(8 + j, j % 2).wait()

        def part(z):
            lanes = chunk(z, cols)
            grad = dot_nn(b_ref[...], weight_tile(wbuf, j % 2, z))
            low = (grad * pool[2 + j % 2, :, lanes].astype(F32)).astype(BF)
            pool[4 + j, :, lanes] = low
            sums_ref[6 + j : 7 + j, lanes] = total_rows(low.astype(F32))

        loop(parts, part)

    gate_back(0)
    slope_load[2].start()
    weight(10, 0).start()
    loop(2, lambda i: send_out(2 + i))
    hold(1, b_ref, pool.at[1])
    gate_load[3].start()
    gate_load[2].wait()
    give(2, b_ref, pool.at[0])
    gate_back(1)
    slope_load[3].start()
    weight(11, 1).start()
    loop(2, lambda i: send_out(4 + i))
    gate_load[3].wait()
    give(3, b_ref, pool.at[1])
    hold(2, b_ref, pool.at[0])
    gate_back(2)
    weight(4, 0).start()
    loop(2, lambda i: send_out(6 + i))
    hold(3, b_ref, pool.at[1])
    advances(1)
    gate_back(3)
    weight(5, 1).start()
    qkv_load.start()
    other_load.start()

    def fold_up(j):
        weight(4 + j, j % 2).wait()

        def part(z):
            dh_ref[...] += dot_nt(pool[4 + j, :, chunk(z, cols)], weight_tile(wbuf, j % 2, z))

        loop(parts, part)

    dh_load.wait()
    fold_up(0)
    weight(6, 0).start()
    fold_up(1)
    weight(7, 1).start()
    fold_up(2)
    weight(3, 0).start()
    fold_up(3)

    z_load.wait()
    r_load.wait()

    def norm_first(i):
        at = chunk(i, size)
        grad = dh_ref[at, :]
        z = z1_ref[at, :]
        dh = norm_back(grad, z, r1_ref[at, 0:1], vector(vec_ref, FIRST_GAIN))
        dh_ref[at, :] = dh
        b_ref[at, :] = dh.astype(BF)
        sums_ref[0:1, :] += total_rows(grad * z)
        sums_ref[1:2, :] += total_rows(grad)
        sums_ref[2:3, :] += total_rows(dh)

    loop(rows // size, norm_first)
    mixed_load.wait()
    give(4, b_ref, mixed_ref)
    weight(3, 0).wait()
    dm = 3

    def mix_back(z):
        pool[dm, :, chunk(z, cols)] = dot_nn(b_ref[...], weight_tile(wbuf, 0, z)).astype(BF)

    loop(parts, mix_back)
    weight(0, 0).start()
    weight(1, 1).start()
    advances(2)
    hold(4, b_ref, mixed_ref)
    y_load.wait()

    qkv_load.wait()
    other_load.wait()
    logs_load.wait()

    def swap(pair):
        lanes = chunk(pair, 2 * HD)
        return remote(
            far_ref.at[lax.rem(pair, 4)],
            swap_ref.at[:, :, lanes],
            swap_send.at[pair],
            swap_recv.at[pair],
            {"dp": cube.place ^ 1, "tensor": cube.z},
        )

    def attend(pair):
        lanes = chunk(pair, 2 * HD)
        q2, dm2 = pool[0, :, lanes], pool[dm, :, lanes]
        k2 = [pool[1, :, lanes], pool[8, :, lanes]]
        v2 = [pool[2, :, lanes], pool[9, :, lanes]]
        dqs, dks, dvs = [], [[], []], [[], []]
        for head in range(2):
            part = slice(head * HD, head * HD + HD)
            q, dmix = q2[:, part], dm2[:, part]
            base = logs_ref[pair, head : head + 1, :]
            chance = [jnp.exp2(dot_nt(k[:, part], q) * LOG2E - base) for k in k2]
            grads = [dot_nt(v[:, part], dmix) for v in v2]
            inner = functools.reduce(
                jnp.add, [jnp.sum(w * g, axis=0, keepdims=True) for w, g in zip(chance, grads)]
            )
            dq = None
            for i in range(2):
                ds = (chance[i] * (grads[i] - inner)).astype(BF)
                term = dot_tn(k2[i][:, part], ds)
                dq = term if dq is None else dq + term
                dks[i].append(dot_nn(ds, q))
                dvs[i].append(dot_nn(chance[i].astype(BF), dmix))
            dqs.append(dq)
        dq = jnp.concatenate(dqs, axis=0).T.astype(BF).astype(F32) * SCALE
        mixed_ref[:, lanes] = dq.astype(BF)
        sums_ref[10:11, lanes] = total_rows(dq)
        near_ref[0, :, lanes] = jnp.concatenate(dks[0], axis=1).astype(BF)
        near_ref[1, :, lanes] = jnp.concatenate(dvs[0], axis=1).astype(BF)

        @pl.when(pair >= 4)
        def _():
            swap(pair - 4).wait_send()

        far_ref[lax.rem(pair, 4), 0] = jnp.concatenate(dks[1], axis=1).astype(BF)
        far_ref[lax.rem(pair, 4), 1] = jnp.concatenate(dvs[1], axis=1).astype(BF)
        swap(pair).start()

    back_out.back_end(near_ref, 1, outputs_ref)
    pairs = width // (2 * HD)
    loop(2, attend)
    give(5, y_ref, pool.at[4])
    advances(3)
    hold(5, y_ref, pool.at[4])
    loop(2, lambda i: attend(2 + i))
    give(6, y_ref, pool.at[5])
    advances(4)
    hold(6, y_ref, pool.at[5])
    loop(2, lambda i: attend(4 + i))
    give(7, y_ref, pool.at[6])
    advances(5)
    hold(7, y_ref, pool.at[6])
    loop(pairs - 6, lambda i: attend(6 + i))
    give(8, y_ref, pool.at[7])
    advances(6)
    hold(8, y_ref, pool.at[7])
    x_load.start()

    def both(pair):
        swap(pair).wait_recv()
        lanes = chunk(pair, 2 * HD)
        for i in range(2):
            total = near_ref[i, :, lanes].astype(F32) + swap_ref[i, :, lanes].astype(F32)
            low = total.astype(BF)
            near_ref[i, :, lanes] = low
            if i == 1:
                sums_ref[11:12, lanes] = total_rows(low.astype(F32))

    loop(pairs, both)
    x_load.wait()
    give(9, y_ref, mixed_ref)

    value = sums_ref[0:8, :]
    thirds = []
    for _ in range(3):
        thirds.append(value.astype(BF))
        value = value - thirds[-1].astype(F32)
    value = dot_nt(jnp.concatenate(thirds, axis=0), cube.shuffle(width))
    sums_ref[0:6, :] = (value[0:8] + value[8:16] + value[16:24])[0:6, :]

    rounds = [{"dp": p, "tensor": cube.z} for p in partners]
    rounds += [{"dp": cube.place, "tensor": cube.z ^ 1}, {"dp": cube.place, "tensor": cube.z ^ 2}]

    def pool_sums(i):
        return remote(sums_ref, sums_in.at[i], sum_send.at[i], sum_recv.at[i], rounds[i])

    def next_sum(i):
        if 0 < i <= len(rounds):
            pool_sums(i - 1).wait()
            sums_ref[...] += sums_in[i - 1]
        if i < len(rounds):
            pool_sums(i).start()

    next_sum(0)

    def fold_in(kind, slot, right):
        weight(kind, slot).wait()

        def part(z):
            value = dot_nt(right[:, chunk(z, cols)], weight_tile(wbuf, slot, z))
            dh_ref[...] += value

        loop(parts, part)

    fold_in(0, 0, mixed_ref)
    weight(2, 0).start()
    fold_in(1, 1, near_ref.at[0])
    next_sum(1)
    fold_in(2, 0, near_ref.at[1])
    loop(4, lambda i: swap(pairs - 4 + i).wait_send())
    pool[0] = dot_nt(dh_ref[...].astype(BF), cube.shuffle(width)).astype(BF)

    def send_in(piece):
        back_in.back(pool, 0, back_ref, piece, pieces)

    loop(2, send_in)
    next_sum(2)
    advances(7)
    give(10, y_ref, near_ref.at[1])
    hold(9, y_ref, mixed_ref)
    next_sum(3)
    loop(2, lambda i: send_in(2 + i))
    give(11, y_ref, near_ref.at[0])
    hold(10, y_ref, near_ref.at[1])
    next_sum(4)
    loop(2, lambda i: send_in(4 + i))
    advances(8)
    hold(11, y_ref, near_ref.at[0])
    loop(2, lambda i: send_in(6 + i))
    advances(9)
    for i in range(5, len(rounds) + 1):
        next_sum(i)
    advances(10)
    advances(11)
    advances(12)
    sums_out[...] = sums_ref[...]
    advances(SUBS + top + 2)

    for r in range(SUBS - RING, SUBS):
        stage(r, top).wait_send()
    back_in.back_end(pool, 0, back_ref)
    back_in.back_wait(pool, 0, back_ref)
    back_out.back_wait(near_ref, 1, outputs_ref)


def backward(second_sums, held, count, parts):
    (weights, vectors, x, qkv, other, mixed, logs, z1, r1, y1, gated, slope, normed_rows, dh2, b2) = held
    subs, _, _, depth, cols = weights.shape
    rows, width = x.shape
    levels = count.bit_length() - 1
    half = count // 2
    pairs = width // (2 * HD)
    dma = pltpu.SemaphoreType.DMA
    low = lambda *shape: (shape, BF)
    high = lambda *shape: (shape, F32)
    hbm = pl.BlockSpec(memory_space=pl.ANY)
    vmem = pl.BlockSpec(memory_space=pltpu.VMEM)
    results = [
        high(subs, depth, cols),
        high(16, width),
        low(2, rows // 2, width),
        low(2, rows // 2, width),
    ]
    scratch = [
        low(10, rows, width),
        high(pairs, 8, rows),
        low(rows, width),
        high(rows, width),
        high(rows, width),
        high(rows, 128),
        low(rows, width),
        low(rows, width),
        low(2, rows, width),
        low(4, 2, rows, 2 * HD),
        low(2, rows, width),
        low(2, count, parts, depth, cols),
        low(RING, half, parts, depth, cols),
        low(RING, half, parts, depth, cols),
        low(HELD, half, parts, depth, cols),
        low(LINE, parts, depth, cols),
        low(subs, half - 1, parts, depth, cols),
        low(subs, parts + 1, depth, cols),
        high(16, width),
        high(levels + 2, 16, width),
    ]
    return pl.pallas_call(
        functools.partial(backward_kernel, count, parts),
        in_specs=[vmem, vmem] + [hbm] * 14,
        out_specs=[vmem, vmem, hbm, hbm],
        out_shape=[jax.ShapeDtypeStruct(*r) for r in results],
        scratch_shapes=[pltpu.VMEM(*s) for s in scratch]
        + [
            dma((15,)),
            dma((2,)),
            pltpu.SemaphoreType.REGULAR,
            dma((subs, levels)),
            dma((subs, levels)),
            dma((subs, 3)),
            dma((subs, 3)),
            dma((pairs,)),
            dma((pairs,)),
            dma((2, 2)),
            dma((2, 2)),
            dma((2,)),
            dma((levels + 2,)),
            dma((levels + 2,)),
        ],
        compiler_params=pltpu.CompilerParams(
            collective_id=2, has_side_effects=True, vmem_limit_bytes=62 * MIB
        ),
    )(vectors, second_sums, weights, x, qkv, other, mixed, logs, z1, r1, y1, gated, slope, normed_rows, dh2, b2)


def result_kernel(
    rows_ref,
    back_ref,
    down_ref,
    up_ref,
    q_ref,
    k_ref,
    v_ref,
    o_ref,
    sums_ref,
    rows_out,
    input_out,
    down_out,
    up_out,
    q_out,
    k_out,
    v_out,
    o_out,
    *small,
):
    rows_out[...] = rows_ref[...]
    input_out[...] = back_ref[...].astype(F32)
    down_out[...] = down_ref[0].T
    up_out[...] = up_ref[0]

    @pl.when(pl.program_id(0) == 0)
    def _():
        for source, target in ((q_ref, q_out), (k_ref, k_out), (v_ref, v_out)):
            target[...] = source[0]
        o_out[...] = o_ref[0].T
        for i in range(6):
            small[i][...] = sums_ref[i : i + 1, :]
        cols = small[7].shape[1]
        mine = chunk(lax.axis_index("tensor"), cols)
        small[7][...] = sums_ref[10:11, mine]
        small[8][...] = sums_ref[11:12, mine]
        for i in range(4):
            small[6][:, i * cols : (i + 1) * cols] = sums_ref[6 + i : 7 + i, mine]


def results(grads, sums, outputs, back):
    _, depth, cols = grads.shape
    _, rows, width = outputs.shape
    steps = 4
    at = {sub: r for r, sub in enumerate(ORDER)}
    row_spec = pl.BlockSpec((2, rows // steps, width), lambda j: (0, j, 0))
    one = lambda r: pl.BlockSpec((1, depth, cols), lambda j: (r, 0, 0))
    run = lambda r: pl.BlockSpec((1, depth, cols), lambda j: (r + j, 0, 0))
    whole = lambda *shape: pl.BlockSpec(shape, lambda j: (0,) * len(shape))
    high = lambda *shape: jax.ShapeDtypeStruct(shape, F32)
    return pl.pallas_call(
        result_kernel,
        grid=(steps,),
        in_specs=[row_spec, row_spec, run(at[DOWN]), run(at[UP])]
        + [one(at[0]), one(at[1]), one(at[2]), one(at[3]), whole(*sums.shape)],
        out_specs=[
            row_spec,
            row_spec,
            pl.BlockSpec((cols, depth), lambda j: (j, 0)),
            pl.BlockSpec((depth, cols), lambda j: (0, j)),
        ]
        + [whole(depth, cols)] * 3
        + [whole(cols, depth)]
        + [whole(1, width)] * 6
        + [whole(1, 4 * cols), whole(1, cols), whole(1, cols)],
        out_shape=[
            jax.ShapeDtypeStruct(outputs.shape, BF),
            high(*outputs.shape),
            high(4 * cols, depth),
            high(depth, 4 * cols),
        ]
        + [high(depth, cols)] * 3
        + [high(cols, depth)]
        + [high(1, width)] * 6
        + [high(1, 4 * cols), high(1, cols), high(1, cols)],
        compiler_params=pltpu.CompilerParams(vmem_limit_bytes=32 * MIB),
    )(outputs, back, grads, grads, grads, grads, grads, grads, sums)


def shards(
    inputs,
    query_weight,
    query_bias,
    key_weight,
    value_weight,
    value_bias,
    out_weight,
    out_bias,
    first_gain,
    first_shift,
    up_weight,
    up_bias,
    down_weight,
    down_bias,
    second_gain,
    second_shift,
    cotangent,
):
    count, parts = lax.axis_size("dp"), lax.axis_size("tensor")
    flat = lambda *values: [value.reshape(1, -1) for value in values]
    *held, second_sums = forward(
        [query_weight, key_weight, value_weight, out_weight, up_weight, down_weight],
        flat(query_bias, value_bias, up_bias),
        flat(out_bias, first_gain, first_shift, down_bias, second_gain, second_shift),
        inputs,
        cotangent,
        count,
        parts,
    )
    grads, sums, outputs, back = backward(second_sums, held, count, parts)
    outputs, input_grad, down, up, query, key, value, out, *small = results(grads, sums, outputs, back)
    small = [row.reshape(-1) for row in small]
    return (
        outputs,
        input_grad,
        query,
        small[7],
        key,
        value,
        small[8],
        out,
        small[2],
        small[0],
        small[1],
        up,
        small[6],
        down,
        small[5],
        small[3],
        small[4],
    )


def solution(mesh):
    rows = P(None, ("dp", "tensor"), None)
    return jax.shard_map(
        shards,
        mesh=mesh,
        in_specs=(
            rows,
            P("dp", "tensor"),
            P("tensor"),
            P("dp", "tensor"),
            P("dp", "tensor"),
            P("tensor"),
            P("tensor", "dp"),
            P(),
            P(),
            P(),
            P("dp", "tensor"),
            P("tensor"),
            P("tensor", "dp"),
            P(),
            P(),
            P(),
            rows,
        ),
        out_specs=(
            rows,
            rows,
            P("dp", "tensor"),
            P("tensor"),
            P("dp", "tensor"),
            P("dp", "tensor"),
            P("tensor"),
            P("tensor", "dp"),
            P(),
            P(),
            P(),
            P("dp", "tensor"),
            P("tensor"),
            P("tensor", "dp"),
            P(),
            P(),
            P(),
        ),
        check_vma=False,
    )
```

```python
import functools
import math

import jax
import jax.numpy as jnp
from jax import lax
from jax.experimental import pallas as pl
from jax.experimental.pallas import tpu as pltpu
from jax.sharding import PartitionSpec as P

HD = 64
LEN = 1024
EPSILON = 1e-05
SCALE = HD ** (-0.5)
LOG2E = math.log2(math.e)
BF = jnp.bfloat16
F32 = jnp.float32
MIB = 1 << 20


def dot_nn(left, right):
    return jnp.dot(left, right, preferred_element_type=F32)


def dot_nt(left, right):
    return lax.dot_general(left, right, (((1,), (1,)), ((), ())), preferred_element_type=F32)


def dot_tn(left, right):
    return lax.dot_general(left, right, (((0,), (0,)), ((), ())), preferred_element_type=F32)


OUT_BIAS, FIRST_GAIN, FIRST_SHIFT, DOWN_BIAS, SECOND_GAIN, SECOND_SHIFT = range(6)


def vector(ref, place):
    return ref[place : place + 1, :]


def normed(hidden):
    average = jnp.mean(hidden, axis=-1, keepdims=True)
    center = hidden - average
    spread = jnp.mean(center * center, axis=-1, keepdims=True)
    inverse = lax.rsqrt(spread + EPSILON)
    return center * inverse, inverse


def norm_back(grad, z, inverse, gain):
    scaled = grad * gain
    average = jnp.mean(scaled, axis=-1, keepdims=True)
    along = jnp.mean(scaled * z, axis=-1, keepdims=True)
    return (scaled - average - z * along) * inverse


def total_rows(value):
    return jnp.sum(value, axis=0, keepdims=True)


def remote(source, target, send, receive, device):
    return pltpu.make_async_remote_copy(
        source, target, send, receive, device_id=device, device_id_type=pl.DeviceIdType.MESH
    )


def greet(devices):
    barrier = pltpu.get_barrier_semaphore()
    for device in devices:
        pl.semaphore_signal(barrier, 1, device_id=device, device_id_type=pl.DeviceIdType.MESH)
    pl.semaphore_wait(barrier, len(devices))


class Cube:
    def __init__(self, count, parts):
        self.count, self.parts, self.half = count, parts, parts // 2
        self.place, self.z = lax.axis_index("dp"), lax.axis_index("tensor")
        self.core = lax.rem(self.place, 2)
        self.levels = count.bit_length() - 1
        bits = [1 << i for i in range(1, self.levels)]
        self.orders = [bits, bits[::-1]]

    def stages(self):
        ups, downs = self.orders
        out = []
        for up, down in zip(ups, downs):
            out.append(self.place ^ jnp.where(self.core == 0, up, down))
        return out + [self.place ^ 1]

    def masks(self):
        table = []
        for order in self.orders:
            held = [0]
            for bit in order:
                held = held + [m ^ bit for m in held]
            table.append(held)
        return [a + [m ^ 1 for m in b] for a, b in (table, table[::-1])]

    def column(self):
        mine = [{"dp": self.place, "tensor": lax.rem(self.z + d, self.parts)} for d in range(1, self.parts)]
        others = [{"dp": self.place ^ 1, "tensor": lax.rem(self.z + d, self.parts)} for d in range(self.parts)]
        return mine + others

    def neighbours(self):
        return [{"dp": p, "tensor": self.z} for p in self.stages()[:-1]]

    def shuffle(self, width):
        depth = width // self.count
        column = lax.broadcasted_iota(jnp.int32, (1, width), 1)
        slot = column // depth
        far = slot // (self.count // 2)
        flips = far
        for level, (up, down) in enumerate(zip(*self.orders)):
            bit = jnp.where(self.core == 0, up, down)
            other = jnp.where(self.core == 0, down, up)
            held = lax.rem(slot // (1 << level), 2)
            flips = flips + held * jnp.where(far == 0, bit, other)
        owner = self.place ^ flips
        source = owner * depth + lax.rem(column, depth)
        row = lax.broadcasted_iota(jnp.int32, (width, width), 0)
        return (row == source).astype(F32).astype(BF)


class Rows:
    def __init__(self, cube, send, receive, here):
        self.cube, self.send, self.receive, self.here = cube, send, receive, here
        c = cube
        self.slot = lax.rem(c.z, c.half)
        self.targets = [(c.place - c.core + c.z // c.half, m * c.half + c.core) for m in range(2)]
        self.micro = c.z // c.half
        self.sources = [(c.place - c.core + lax.rem(c.z, c.half), c.half * c.core + p) for p in range(2)]

    def own(self, device):
        return jnp.logical_and(device[0] == self.cube.place, device[1] == self.cube.z)

    def at(self, device):
        return {"dp": device[0], "tensor": device[1]}

    def into(self, source, target, piece, pieces):
        size = source.shape[1] // pieces
        at = pl.ds(pl.multiple_of(piece * size, size), size)
        for m, device in enumerate(self.targets):
            own = self.own(device)

            @pl.when(own)
            def _(m=m):
                pltpu.make_async_copy(source.at[m, at], target.at[self.slot, at], self.here).start()

            @pl.when(jnp.logical_not(own))
            def _(m=m, device=device):
                remote(
                    source.at[m, at],
                    target.at[self.slot, at],
                    self.send.at[m],
                    self.receive.at[self.slot],
                    self.at(device),
                ).start()

    def into_wait(self, source, target):
        for p, device in enumerate(self.sources):
            own = self.own(device)

            @pl.when(own)
            def _(p=p):
                pltpu.make_async_copy(source.at[0], target.at[p], self.here).wait()

            @pl.when(jnp.logical_not(own))
            def _(p=p, device=device):
                remote(
                    source.at[0], target.at[p], self.send.at[0], self.receive.at[p], self.at(device)
                ).wait_recv()

    def into_end(self, source, target):
        for m, device in enumerate(self.targets):

            @pl.when(jnp.logical_not(self.own(device)))
            def _(m=m, device=device):
                remote(
                    source.at[m], target.at[self.slot], self.send.at[m], self.receive.at[0], self.at(device)
                ).wait_send()


    def back(self, source, lead, target, piece, pieces):
        size = target.shape[1] // pieces
        for p, device in enumerate(self.sources):
            own = self.own(device)
            here = pl.ds(pl.multiple_of(p * target.shape[1] + piece * size, size), size)
            there = pl.ds(pl.multiple_of(piece * size, size), size)

            @pl.when(own)
            def _(here=here, there=there):
                pltpu.make_async_copy(
                    source.at[lead, here], target.at[self.micro, there], self.here
                ).start()

            @pl.when(jnp.logical_not(own))
            def _(p=p, device=device, here=here, there=there):
                remote(
                    source.at[lead, here],
                    target.at[self.micro, there],
                    self.send.at[p],
                    self.receive.at[self.micro],
                    self.at(device),
                ).start()

    def back_wait(self, source, lead, target):
        rows = target.shape[1]
        for m, device in enumerate(self.targets):

            @pl.when(jnp.logical_not(self.own(device)))
            def _(m=m, device=device):
                remote(
                    source.at[lead, pl.ds(0, rows)],
                    target.at[m],
                    self.send.at[0],
                    self.receive.at[m],
                    self.at(device),
                ).wait_recv()

    def back_end(self, source, lead, target):
        rows = target.shape[1]
        for p, device in enumerate(self.sources):
            own = self.own(device)

            @pl.when(own)
            def _(p=p):
                pltpu.make_async_copy(
                    source.at[lead, pl.ds(p * rows, rows)], target.at[self.micro], self.here
                ).wait()

            @pl.when(jnp.logical_not(own))
            def _(p=p, device=device):
                remote(
                    source.at[lead, pl.ds(p * rows, rows)],
                    target.at[self.micro],
                    self.send.at[p],
                    self.receive.at[0],
                    self.at(device),
                ).wait_send()


SUBS, UP, DOWN = 12, 4, 8
XS, XP, CS, CP, EARLY = 0, 4, 4, 8, 0
PACE = [4, 5, 6, 7, 7, 8, 8, 9, 10, 11, 12, 13]


def loop(count, body):
    lax.fori_loop(0, count, lambda i, _: (body(i), None)[1], None)


def chunk(i, size):
    return pl.ds(pl.multiple_of(i * size, size), size)


def weight_tile(ref, slot, z):
    value = ref[slot, :, z]
    return value.reshape(-1, value.shape[-1])


def forward_kernel(
    count,
    parts,
    q_in,
    k_in,
    v_in,
    o_in,
    up_in,
    down_in,
    q_bias,
    v_bias,
    up_bias,
    vec0,
    vec1,
    vec2,
    vec3,
    vec4,
    vec5,
    in_ref,
    cot_ref,
    weights_ref,
    vec_out,
    x_out,
    qkv_out,
    other_out,
    mixed_out,
    chance_out,
    z1_out,
    r1_out,
    y1_out,
    gated_out,
    slope_out,
    normed_out,
    dh2_out,
    b2_out,
    sums_out,
    local_ref,
    o_raw,
    down_raw,
    bias_ref,
    vec_ref,
    raw_ref,
    cot_raw,
    shuffle_ref,
    x_ref,
    c_ref,
    bias_all,
    qkv_ref,
    other_ref,
    mixed_ref,
    chance_ref,
    z1_ref,
    r1_ref,
    y1_ref,
    gated_ref,
    slope_ref,
    acc_ref,
    normed_ref,
    dh2_ref,
    b2_ref,
    sums_ref,
    wbuf,
    prep_sem,
    local_sem,
    zs,
    zr,
    ss,
    sr,
    wsem,
    bias_send,
    bias_recv,
    row_send,
    row_recv,
    row_here,
    kv_send,
    kv_recv,
    out_sem,
    save_sem,
):
    cube = Cube(count, parts)
    partners, levels = cube.stages(), cube.levels
    shifts = [lax.rem(cube.z + d, parts) for d in range(1, parts)]
    ahead = 5
    rows = x_ref.shape[0]
    cols = weights_ref.shape[-1]
    depth = weights_ref.shape[-2]
    sources = [q_in, k_in, v_in] + [up_in.at[:, i * cols : (i + 1) * cols] for i in range(4)]
    places = [local_ref.at[i] for i in (0, 1, 2, 4, 5, 6, 7)]
    prep = [
        pltpu.make_async_copy(source, place, prep_sem.at[i])
        for i, (source, place) in enumerate(zip(sources + [o_in, down_in], places + [o_raw, down_raw]))
    ]
    for copy in prep:
        copy.start()
    bias_ref[...] = jnp.zeros_like(bias_ref)
    bias_ref[0:1, :] = q_bias[...]
    bias_ref[1:2, :] = v_bias[...]
    for i in range(4):
        bias_ref[2 + i : 3 + i, :] = up_bias[:, i * cols : (i + 1) * cols]
    same = lax.broadcasted_iota(jnp.int32, (depth, depth), 0) == lax.broadcasted_iota(
        jnp.int32, (depth, depth), 1
    )
    eye = same.astype(F32).astype(BF)
    greet(cube.column() + cube.neighbours())
    for i in range(3):
        prep[i].wait()

    def own(sub):
        return pltpu.make_async_copy(local_ref.at[sub], weights_ref.at[sub, 0, cube.z], local_sem.at[sub])

    inner = jnp.logical_or(cube.z == 1, cube.z == 2)
    mine, theirs = cube.z // 2 * 2, 2 - cube.z // 2 * 2

    def along(sub, hop):
        if hop == 0:
            source, target, z = local_ref.at[sub], weights_ref.at[sub, 0, cube.z], cube.z ^ 1
        else:
            source = weights_ref.at[sub, 0, pl.ds(mine if hop == 1 else theirs, 2)]
            target, z = source, (3 - cube.z if hop == 1 else cube.z ^ 1)
        return remote(
            source, target, zs.at[sub, hop], zr.at[sub, hop], {"dp": cube.place, "tensor": z}
        )

    def stage(sub, level):
        size = 1 << level
        return remote(
            weights_ref.at[sub, pl.ds(0, size)],
            weights_ref.at[sub, pl.ds(size, size)],
            ss.at[sub, level],
            sr.at[sub, level],
            {"dp": partners[level], "tensor": cube.z},
        )

    def begin(sub):
        own(sub).start()
        along(sub, 0).start()

    def pass_pair(sub):
        own(sub).wait()
        along(sub, 0).wait_recv()

        @pl.when(inner)
        def _():
            along(sub, 1).start()

    def pass_on(sub):
        @pl.when(inner)
        def _():
            along(sub, 1).wait_recv()
            along(sub, 2).start()

    def first_stage(sub):
        @pl.when(jnp.logical_not(inner))
        def _():
            along(sub, 2).wait_recv()

        stage(sub, 0).start()

    def prepare(sub):
        @pl.when(sub + 1 < SUBS)
        def _():
            pass_on(sub + 1)

        @pl.when(sub + 2 < SUBS)
        def _():
            pass_pair(sub + 2)

        @pl.when(sub + ahead < SUBS)
        def _():
            begin(sub + ahead)

    def relay(step):
        @pl.when(step + EARLY < SUBS)
        def _():
            first_stage(step + EARLY)

        for level in range(levels):
            sub = step - level - 1

            @pl.when(jnp.logical_and(sub >= 0, sub < SUBS))
            def _(sub=sub, level=level):
                stage(sub, level).wait_recv()
                if level + 1 < levels:
                    stage(sub, level + 1).start()

        @pl.when(jnp.logical_and(step >= XS, step < XS + XP))
        def _():
            rows_x.into(in_ref, raw_ref, step - XS, XP)

        @pl.when(jnp.logical_and(step >= CS, step < CS + CP))
        def _():
            rows_c.into(cot_ref, cot_raw, step - CS, CP)

        prepare(step + EARLY)

    done = [0]

    def relays(last):
        if last > done[0]:
            first = done[0]
            loop(last - first, lambda i: relay(first + i))
            done[0] = last

    def load(sub):
        return pltpu.make_async_copy(weights_ref.at[sub], wbuf.at[sub % 4], wsem.at[sub % 4])

    def share_bias(d):
        return remote(
            bias_ref,
            bias_all.at[cube.z],
            bias_send.at[d],
            bias_recv.at[d],
            {"dp": cube.place, "tensor": shifts[d]},
        )

    rows_x = Rows(cube, row_send.at[0], row_recv.at[0], row_here.at[0])
    rows_c = Rows(cube, row_send.at[1], row_recv.at[1], row_here.at[1])
    outs = []

    def keep(source, target):
        copy = pltpu.make_async_copy(source, target, out_sem.at[len(outs)])
        copy.start()
        outs.append(copy)

    loop(3, begin)
    for copy in prep[3:]:
        copy.wait()
    local_ref[3] = dot_nt(eye, o_raw[...]).astype(BF)
    loop(ahead - 3, lambda i: begin(3 + i))
    for i in range(4):
        local_ref[DOWN + i] = dot_nt(eye, down_raw[i * cols : (i + 1) * cols, :]).astype(BF)
    for d in range(parts - 1):
        share_bias(d).start()
    pass_pair(0)
    pass_pair(1)
    pass_on(0)
    for sub in range(EARLY):
        first_stage(sub)
        prepare(sub)
    shuffle_ref[...] = cube.shuffle(x_ref.shape[1])
    bias_all[cube.z] = bias_ref[...]
    value = jnp.concatenate([v[...] for v in (vec0, vec1, vec2, vec3, vec4, vec5)] + [vec0[...]] * 2, axis=0)
    thirds = []
    for _ in range(3):
        thirds.append(value.astype(BF))
        value = value - thirds[-1].astype(F32)
    value = dot_nn(jnp.concatenate(thirds, axis=0), shuffle_ref[...])
    vec_ref[...] = value[0:8] + value[8:16] + value[16:24]
    keep(vec_ref, vec_out)
    relays(max(PACE[0], levels + 1))
    rows_x.into_wait(in_ref, raw_ref)
    half_rows = raw_ref.shape[1]
    for p in range(2):
        x_ref[p * half_rows : (p + 1) * half_rows, :] = dot_nn(raw_ref[p], shuffle_ref[...]).astype(BF)
    keep(x_ref, x_out)
    for d in range(parts - 1):
        share_bias(d).wait_recv()

    for kind in range(3):
        relays(max(PACE[kind], levels + kind + 1))
        load(kind).start()
        load(kind).wait()

        def project(z, kind=kind):
            acc = dot_nn(x_ref[...], weight_tile(wbuf, kind, z))
            if kind == 0:
                acc = (acc + bias_all[z, 0:1, :]) * SCALE
            elif kind == 2:
                acc = acc + bias_all[z, 1:2, :]
            qkv_ref[kind, :, chunk(z, cols)] = acc.astype(BF)

        loop(parts, project)

    swap = remote(qkv_ref.at[pl.ds(1, 2)], other_ref, kv_send, kv_recv, {"dp": cube.place ^ 1, "tensor": cube.z})
    swap.start()
    keep(qkv_ref, qkv_out)
    relays(PACE[3])
    swap.wait_recv()
    keep(other_ref, other_out)

    def save(pair):
        slot = lax.rem(pair, 2)
        return pltpu.make_async_copy(chance_ref.at[slot], chance_out.at[pair], save_sem.at[slot])

    def attend(pair):
        lanes = chunk(pair, 2 * HD)
        q2 = qkv_ref[0, :, lanes]
        k2 = [qkv_ref[1, :, lanes], other_ref[0, :, lanes]]
        v2 = [qkv_ref[2, :, lanes], other_ref[1, :, lanes]]
        mixed = []
        slot = lax.rem(pair, 2)

        @pl.when(pair >= 2)
        def _():
            save(pair - 2).wait()

        for head in range(2):
            part = slice(head * HD, head * HD + HD)
            scores = [dot_nt(k[:, part], q2[:, part]) for k in k2]
            top = functools.reduce(jnp.maximum, [jnp.max(s, axis=0, keepdims=True) for s in scores])
            base = top * LOG2E
            expo = [jnp.exp2(s * LOG2E - base) for s in scores]
            total = functools.reduce(jnp.add, [jnp.sum(e, axis=0, keepdims=True) for e in expo])
            inverse = 1.0 / total
            chance = [(e * inverse).astype(BF) for e in expo]
            mixed.append(functools.reduce(jnp.add, [dot_tn(v[:, part], c) for c, v in zip(chance, v2)]))
            for i in range(2):
                chance_ref[slot, head, i * rows : (i + 1) * rows, :] = chance[i]
        mixed_ref[:, lanes] = jnp.concatenate(mixed, axis=0).T.astype(BF)
        save(pair).start()

    pairs = mixed_ref.shape[1] // (2 * HD)
    loop(2, attend)
    relays(PACE[4])
    loop(2, lambda i: attend(2 + i))
    relays(PACE[5])
    loop(2, lambda i: attend(4 + i))
    relays(PACE[6])
    loop(pairs - 6, lambda i: attend(6 + i))
    relays(max(PACE[7], levels + 5))
    keep(mixed_ref, mixed_out)
    loop(2, lambda i: save(pairs - 2 + i).wait())

    load(3).start()
    load(4).start()
    load(3).wait()

    def mix(z):
        value = dot_nt(mixed_ref[:, chunk(z, cols)], weight_tile(wbuf, 3, z))

        @pl.when(z == 0)
        def _():
            acc_ref[...] = value

        @pl.when(z > 0)
        def _():
            acc_ref[...] += value

    loop(parts, mix)
    size = 128

    def norm_first(i):
        at = chunk(i, size)
        hidden = x_ref[at, :].astype(F32) + acc_ref[at, :] + vector(vec_ref, OUT_BIAS)
        z, inverse = normed(hidden)
        z1_ref[at, :] = z
        r1_ref[at, :] = jnp.broadcast_to(inverse, (size, 128))
        y = z * vector(vec_ref, FIRST_GAIN) + vector(vec_ref, FIRST_SHIFT)
        y1_ref[at, :] = y.astype(BF)
        acc_ref[at, :] = y + vector(vec_ref, DOWN_BIAS)

    loop(rows // size, norm_first)
    keep(z1_ref, z1_out)
    keep(r1_ref, r1_out)
    keep(y1_ref, y1_out)

    def gate(sub):
        load(sub).wait()

        def part(z):
            lanes = chunk(z, cols)
            upper = dot_nn(y1_ref[...], weight_tile(wbuf, sub % 4, z)) + bias_all[z, sub - UP + 2 : sub - UP + 3, :]
            half = 0.5 + 0.5 * lax.erf(upper * (0.5**0.5))
            gated_ref[sub - UP, :, lanes] = (upper * half).astype(BF)
            bell = jnp.exp(upper * upper * -0.5) * ((2 * math.pi) ** -0.5)
            slope_ref[sub - UP, :, lanes] = (half + upper * bell).astype(BF)

        loop(parts, part)
        keep(gated_ref.at[sub - UP], gated_out.at[sub - UP])
        keep(slope_ref.at[sub - UP], slope_out.at[sub - UP])

    for sub in range(UP, DOWN):
        gate(sub)
        relays(max(PACE[8 + sub - UP], min(sub + 1, DOWN - 1) + levels + 1))
        if sub + 1 < DOWN:
            load(sub + 1).start()

    rows_c.into_wait(cot_ref, cot_raw)
    for p in range(2):
        c_ref[p * half_rows : (p + 1) * half_rows, :] = dot_nn(cot_raw[p], shuffle_ref[...]).astype(BF)

    for sub in range(DOWN, SUBS):
        relays(sub + levels + 1)
        load(sub).start()
        load(sub).wait()

        def fold(z, sub=sub):
            acc_ref[...] += dot_nt(gated_ref[sub - DOWN, :, chunk(z, cols)], weight_tile(wbuf, sub % 4, z))

        loop(parts, fold)

    sums_ref[...] = jnp.zeros_like(sums_ref)

    def norm_second(i):
        at = chunk(i, size)
        z, inverse = normed(acc_ref[at, :])
        gain = vector(vec_ref, SECOND_GAIN)
        normed_ref[at, :] = (z * gain + vector(vec_ref, SECOND_SHIFT)).astype(BF)
        grad = c_ref[at, :].astype(F32)
        dh = norm_back(grad, z, inverse, gain)
        dh2_ref[at, :] = dh
        b2_ref[at, :] = dh.astype(BF)
        sums_ref[0:1, :] += total_rows(grad * z)
        sums_ref[1:2, :] += total_rows(grad)
        sums_ref[2:3, :] += total_rows(dh)

    loop(rows // size, norm_second)
    keep(normed_ref, normed_out)
    keep(dh2_ref, dh2_out)
    keep(b2_ref, b2_out)
    keep(sums_ref, sums_out)

    def sent(sub):
        along(sub, 0).wait_send()

        @pl.when(inner)
        def _():
            along(sub, 1).wait_send()
            along(sub, 2).wait_send()

        for level in range(levels):
            stage(sub, level).wait_send()

    loop(SUBS, sent)
    for d in range(parts - 1):
        share_bias(d).wait_send()
    swap.wait_send()
    rows_x.into_end(in_ref, raw_ref)
    rows_c.into_end(cot_ref, cot_raw)
    for copy in outs:
        copy.wait()


def forward(weights, biases, vectors, inputs, cotangent, count, parts):
    subs = SUBS
    depth, cols = weights[0].shape
    _, half_rows, width = inputs.shape
    rows = 2 * half_rows
    levels = count.bit_length() - 1
    pairs = width // (2 * HD)
    dma = pltpu.SemaphoreType.DMA
    low = lambda *shape: (shape, BF)
    high = lambda *shape: (shape, F32)
    results = [
        low(subs, count, parts, depth, cols),
        high(8, width),
        low(rows, width),
        low(3, rows, width),
        low(2, rows, width),
        low(rows, width),
        low(pairs, 2, 2 * rows, rows),
        high(rows, width),
        high(rows, 128),
        low(rows, width),
        low(4, rows, parts * cols),
        low(4, rows, parts * cols),
        low(rows, width),
        high(rows, width),
        low(rows, width),
        high(8, width),
    ]
    scratch = [
        low(subs, depth, cols),
        low(cols, depth),
        low(4 * cols, depth),
        high(8, cols),
        high(8, width),
        low(2, half_rows, width),
        low(2, half_rows, width),
        low(width, width),
        low(rows, width),
        low(rows, width),
        high(parts, 8, cols),
        low(3, rows, width),
        low(2, rows, width),
        low(rows, width),
        low(2, 2, 2 * rows, rows),
        high(rows, width),
        high(rows, 128),
        low(rows, width),
        low(4, rows, parts * cols),
        low(4, rows, parts * cols),
        high(rows, width),
        low(rows, width),
        high(rows, width),
        low(rows, width),
        high(8, width),
        low(4, count, parts, depth, cols),
    ]
    hbm = pl.BlockSpec(memory_space=pl.ANY)
    vmem = pl.BlockSpec(memory_space=pltpu.VMEM)
    return pl.pallas_call(
        functools.partial(forward_kernel, count, parts),
        in_specs=[hbm] * 6 + [vmem] * 9 + [hbm, hbm],
        out_specs=[hbm] * len(results),
        out_shape=[jax.ShapeDtypeStruct(*r) for r in results],
        scratch_shapes=[pltpu.VMEM(*s) for s in scratch]
        + [
            dma((9,)),
            dma((subs,)),
            dma((subs, 3)),
            dma((subs, 3)),
            dma((subs, levels)),
            dma((subs, levels)),
            dma((4,)),
            dma((parts - 1,)),
            dma((parts - 1,)),
            dma((2, 2)),
            dma((2, 2)),
            dma((2,)),
            dma,
            dma,
            dma((24,)),
            dma((2,)),
        ],
        compiler_params=pltpu.CompilerParams(
            collective_id=1, has_side_effects=True, vmem_limit_bytes=62 * MIB
        ),
    )(*weights, *biases, *vectors, inputs, cotangent)


HELD, RING, LINE = 5, 2, 4
ORDER = [8, 9, 10, 11, 3, 4, 5, 6, 7, 0, 2, 1]


def backward_kernel(
    count,
    parts,
    vec_ref,
    second_ref,
    weights_ref,
    x_in,
    qkv_in,
    other_in,
    mixed_in,
    chance_in,
    z1_in,
    r1_in,
    y1_in,
    gated_in,
    slope_in,
    normed_in,
    dh2_in,
    b2_in,
    grads_ref,
    sums_out,
    outputs_ref,
    back_ref,
    pool,
    chance_ref,
    y_ref,
    dh_ref,
    z1_ref,
    r1_ref,
    b_ref,
    mixed_ref,
    near_ref,
    far_ref,
    swap_ref,
    wbuf,
    send_ref,
    staged_ref,
    held_ref,
    line_ref,
    small_ref,
    zed_ref,
    sums_ref,
    sums_in,
    load_sem,
    fetch_sem,
    wsem,
    free_sem,
    ss,
    sr,
    zs,
    zr,
    swap_send,
    swap_recv,
    row_send,
    row_recv,
    row_here,
    sum_send,
    sum_recv,
):
    cube = Cube(count, parts)
    partners, levels = cube.stages(), cube.levels
    top = levels - 1
    half = count // 2
    shifts = [lax.rem(cube.z + d, parts) for d in range(1, parts)]
    rows, width = b_ref.shape
    cols = weights_ref.shape[-1]
    depth = weights_ref.shape[-2]
    wide = half * depth
    size = 128

    pairs = width // (2 * HD)

    def fetch(pair):
        slot = lax.rem(pair, 2)
        return pltpu.make_async_copy(chance_in.at[pair], chance_ref.at[slot], fetch_sem.at[slot])

    def load(place, source, target):
        return pltpu.make_async_copy(source, target, load_sem.at[place])

    def weight(sub, slot):
        return pltpu.make_async_copy(weights_ref.at[sub], wbuf.at[slot], wsem.at[slot])

    gate_load = [load(j % 2, gated_in.at[j], pool.at[j % 2]) for j in range(4)]
    slope_load = [load(2 + j % 2, slope_in.at[j], pool.at[2 + j % 2]) for j in range(4)]
    b_load = load(4, b2_in, b_ref)
    out_load = load(5, normed_in, near_ref.at[0])
    y_load = load(6, y1_in, y_ref)
    dh_load = load(7, dh2_in, dh_ref)
    z_load = load(8, z1_in, z1_ref)
    r_load = load(9, r1_in, r1_ref)
    mixed_load = load(10, mixed_in, mixed_ref)
    qkv_load = load(12, qkv_in, pool.at[pl.ds(0, 3)])
    other_load = load(13, other_in, pool.at[pl.ds(8, 2)])
    x_load = load(14, x_in, y_ref)

    def stage(r, level):
        if level == top:
            source, target = send_ref.at[lax.rem(r, RING)], staged_ref.at[lax.rem(r, RING)]
        else:
            source = held_ref.at[lax.rem(r, HELD), pl.ds(1 << level, 1 << level)]
            target = small_ref.at[r, pl.ds((1 << level) - 1, 1 << level)]
        return remote(
            source, target, ss.at[r, level], sr.at[r, level], {"dp": partners[level], "tensor": cube.z}
        )

    inner = jnp.logical_or(cube.z == 1, cube.z == 2)
    mine, theirs = cube.z // 2 * 2, 2 - cube.z // 2 * 2

    def along(r, hop):
        line = lax.rem(r, LINE)
        if hop == 0:
            source = line_ref.at[line, pl.ds(jnp.where(cube.z == 0, 1, 0), parts - 1)]
            target, z = zed_ref.at[r, pl.ds(0, parts - 1)], cube.z ^ 1
        elif hop == 1:
            source = line_ref.at[line, pl.ds(theirs, 2)]
            target, z = zed_ref.at[r, pl.ds(parts - 1, 2)], 3 - cube.z
        else:
            source = line_ref.at[line, cube.z ^ 1]
            target, z = zed_ref.at[r, 0], cube.z ^ 1
        return remote(source, target, zs.at[r, hop], zr.at[r, hop], {"dp": cube.place, "tensor": z})

    def add_line(r, block, place):
        line = lax.rem(r, LINE)
        value = line_ref[line, block].astype(F32) + zed_ref[r, place].astype(F32)
        line_ref[line, block] = value.astype(BF)

    def give(r, left, right):
        if r >= RING:
            stage(r - RING, top).wait_send()
        value = dot_tn(left[:, wide:], right[...]).astype(BF)
        for z in range(parts):
            send_ref[r % RING, :, z] = value[:, z * cols : (z + 1) * cols].reshape(half, depth, cols)
        if r >= RING:
            pl.semaphore_wait(free_sem, 1)
        stage(r, top).start()

    def hold(r, left, right):
        advances(r - HELD + top)
        value = dot_tn(left[:, :wide], right[...])
        stage(r, top).wait_recv()
        for z in range(parts):
            part = value[:, z * cols : (z + 1) * cols].reshape(half, depth, cols)
            part = part + staged_ref[r % RING, :, z].astype(F32)
            held_ref[r % HELD, :, z] = part.astype(BF)
        if r + RING < SUBS:
            pl.semaphore_signal(
                free_sem,
                1,
                device_id={"dp": cube.place ^ 1, "tensor": cube.z},
                device_id_type=pl.DeviceIdType.MESH,
            )
        stage(r, top - 1).start()

    def advance(k):
        for i in range(top):
            level = top - 1 - i
            r = k - i

            @pl.when(jnp.logical_and(r >= 0, r < SUBS))
            def _(r=r, level=level):
                stage(r, level).wait_recv()
                place = lax.rem(r, HELD)

                def fold(slot):
                    value = held_ref[place, slot].astype(F32)
                    value = value + small_ref[r, (1 << level) - 1 + slot].astype(F32)
                    if level > 0:
                        held_ref[place, slot] = value.astype(BF)
                    else:
                        line_ref[lax.rem(r, LINE)] = value.astype(BF)

                loop(1 << level, fold)
                if level > 0:
                    stage(r, level - 1).start()
                else:

                    @pl.when(jnp.logical_not(inner))
                    def _():
                        along(r, 0).start()

                    for other in range(top):
                        stage(r, other).wait_send()

        r = k - top

        @pl.when(jnp.logical_and(inner, jnp.logical_and(r >= 0, r < SUBS)))
        def _(r=r):
            along(r, 0).wait_recv()
            for i in range(parts - 1):
                add_line(r, jnp.where(cube.z == 1, 1, 0) + i, i)
            along(r, 1).start()

        r = k - top - 1

        @pl.when(jnp.logical_and(inner, jnp.logical_and(r >= 0, r < SUBS)))
        def _(r=r):
            along(r, 1).wait_recv()
            for i in range(2):
                add_line(r, mine + i, parts - 1 + i)
            along(r, 2).start()
            grads_ref[r] = line_ref[lax.rem(r, LINE), cube.z].astype(F32)

        r = k - top - 2

        @pl.when(jnp.logical_and(r >= 0, r < SUBS))
        def _(r=r):
            @pl.when(inner)
            def _():
                along(r, 1).wait_send()
                along(r, 2).wait_send()

            @pl.when(jnp.logical_not(inner))
            def _():
                along(r, 2).wait_recv()
                value = line_ref[lax.rem(r, LINE), cube.z].astype(F32)
                grads_ref[r] = value + zed_ref[r, 0].astype(F32)
                along(r, 0).wait_send()

    done = [0]

    def advances(last):
        if last > done[0]:
            first = done[0]
            loop(last - first, lambda i: advance(first + i))
            done[0] = last

    back_out = Rows(cube, row_send.at[0], row_recv.at[0], row_here.at[0])
    back_in = Rows(cube, row_send.at[1], row_recv.at[1], row_here.at[1])
    pieces = 8

    sums_ref[...] = jnp.zeros_like(sums_ref)
    sums_ref[3:6, :] = second_ref[0:3, :]

    b_load.start()
    gate_load[0].start()
    weight(8, 0).start()
    slope_load[0].start()
    gate_load[1].start()
    out_load.start()
    y_load.start()
    greet(cube.column() + cube.neighbours())
    b_load.wait()
    gate_load[0].wait()
    give(0, b_ref, pool.at[0])
    slope_load[1].start()
    weight(9, 1).start()
    dh_load.start()
    z_load.start()
    r_load.start()
    mixed_load.start()
    loop(2, lambda i: fetch(i).start())
    gate_load[1].wait()
    give(1, b_ref, pool.at[1])

    out_load.wait()
    near_ref[1] = dot_nt(near_ref[0], cube.shuffle(width)).astype(BF)

    def send_out(piece):
        back_out.back(near_ref, 1, outputs_ref, piece, pieces)

    loop(2, send_out)
    hold(0, b_ref, pool.at[0])
    gate_load[2].start()

    def gate_back(j):
        slope_load[j].wait()
        weight(8 + j, j % 2).wait()

        def part(z):
            lanes = chunk(z, cols)
            grad = dot_nn(b_ref[...], weight_tile(wbuf, j % 2, z))
            low = (grad * pool[2 + j % 2, :, lanes].astype(F32)).astype(BF)
            pool[4 + j, :, lanes] = low
            sums_ref[6 + j : 7 + j, lanes] = total_rows(low.astype(F32))

        loop(parts, part)

    gate_back(0)
    slope_load[2].start()
    weight(10, 0).start()
    loop(2, lambda i: send_out(2 + i))
    hold(1, b_ref, pool.at[1])
    gate_load[3].start()
    gate_load[2].wait()
    give(2, b_ref, pool.at[0])
    gate_back(1)
    slope_load[3].start()
    weight(11, 1).start()
    loop(2, lambda i: send_out(4 + i))
    gate_load[3].wait()
    give(3, b_ref, pool.at[1])
    hold(2, b_ref, pool.at[0])
    gate_back(2)
    weight(4, 0).start()
    loop(2, lambda i: send_out(6 + i))
    hold(3, b_ref, pool.at[1])
    advances(1)
    gate_back(3)
    weight(5, 1).start()
    qkv_load.start()
    other_load.start()

    def fold_up(j):
        weight(4 + j, j % 2).wait()

        def part(z):
            dh_ref[...] += dot_nt(pool[4 + j, :, chunk(z, cols)], weight_tile(wbuf, j % 2, z))

        loop(parts, part)

    dh_load.wait()
    fold_up(0)
    weight(6, 0).start()
    fold_up(1)
    weight(7, 1).start()
    fold_up(2)
    weight(3, 0).start()
    fold_up(3)

    z_load.wait()
    r_load.wait()

    def norm_first(i):
        at = chunk(i, size)
        grad = dh_ref[at, :]
        z = z1_ref[at, :]
        dh = norm_back(grad, z, r1_ref[at, 0:1], vector(vec_ref, FIRST_GAIN))
        dh_ref[at, :] = dh
        b_ref[at, :] = dh.astype(BF)
        sums_ref[0:1, :] += total_rows(grad * z)
        sums_ref[1:2, :] += total_rows(grad)
        sums_ref[2:3, :] += total_rows(dh)

    loop(rows // size, norm_first)
    mixed_load.wait()
    give(4, b_ref, mixed_ref)
    weight(3, 0).wait()
    dm = 3

    def mix_back(z):
        pool[dm, :, chunk(z, cols)] = dot_nn(b_ref[...], weight_tile(wbuf, 0, z)).astype(BF)

    loop(parts, mix_back)
    weight(0, 0).start()
    weight(1, 1).start()
    advances(2)
    hold(4, b_ref, mixed_ref)
    y_load.wait()

    qkv_load.wait()
    other_load.wait()

    def swap(pair):
        lanes = chunk(pair, 2 * HD)
        return remote(
            far_ref.at[lax.rem(pair, 4)],
            swap_ref.at[:, :, lanes],
            swap_send.at[pair],
            swap_recv.at[pair],
            {"dp": cube.place ^ 1, "tensor": cube.z},
        )

    def attend(pair):
        lanes = chunk(pair, 2 * HD)
        fetch(pair).wait()
        slot = lax.rem(pair, 2)
        q2, dm2 = pool[0, :, lanes], pool[dm, :, lanes]
        k2 = [pool[1, :, lanes], pool[8, :, lanes]]
        v2 = [pool[2, :, lanes], pool[9, :, lanes]]
        weighed = (dm2.astype(F32) * mixed_ref[:, lanes].astype(F32)).T
        dqs, dks, dvs = [], [[], []], [[], []]
        for head in range(2):
            part = slice(head * HD, head * HD + HD)
            q, dmix = q2[:, part], dm2[:, part]
            chance = [chance_ref[slot, head, i * rows : (i + 1) * rows, :] for i in range(2)]
            grads = [dot_nt(v[:, part], dmix) for v in v2]
            inner = total_rows(weighed[part, :])
            dq = None
            for i in range(2):
                ds = (chance[i].astype(F32) * (grads[i] - inner)).astype(BF)
                term = dot_tn(k2[i][:, part], ds)
                dq = term if dq is None else dq + term
                dks[i].append(dot_nn(ds, q))
                dvs[i].append(dot_nn(chance[i], dmix))
            dqs.append(dq)
        dq = jnp.concatenate(dqs, axis=0).T.astype(BF).astype(F32) * SCALE
        mixed_ref[:, lanes] = dq.astype(BF)
        sums_ref[10:11, lanes] = total_rows(dq)
        near_ref[0, :, lanes] = jnp.concatenate(dks[0], axis=1).astype(BF)
        near_ref[1, :, lanes] = jnp.concatenate(dvs[0], axis=1).astype(BF)

        @pl.when(pair >= 4)
        def _():
            swap(pair - 4).wait_send()

        far_ref[lax.rem(pair, 4), 0] = jnp.concatenate(dks[1], axis=1).astype(BF)
        far_ref[lax.rem(pair, 4), 1] = jnp.concatenate(dvs[1], axis=1).astype(BF)
        swap(pair).start()

        @pl.when(pair + 2 < pairs)
        def _():
            fetch(pair + 2).start()

    back_out.back_end(near_ref, 1, outputs_ref)
    loop(2, attend)
    give(5, y_ref, pool.at[4])
    advances(3)
    hold(5, y_ref, pool.at[4])
    loop(2, lambda i: attend(2 + i))
    give(6, y_ref, pool.at[5])
    advances(4)
    hold(6, y_ref, pool.at[5])
    loop(2, lambda i: attend(4 + i))
    give(7, y_ref, pool.at[6])
    advances(5)
    hold(7, y_ref, pool.at[6])
    loop(pairs - 6, lambda i: attend(6 + i))
    give(8, y_ref, pool.at[7])
    advances(6)
    hold(8, y_ref, pool.at[7])
    x_load.start()

    def both(pair):
        swap(pair).wait_recv()
        lanes = chunk(pair, 2 * HD)
        for i in range(2):
            total = near_ref[i, :, lanes].astype(F32) + swap_ref[i, :, lanes].astype(F32)
            low = total.astype(BF)
            near_ref[i, :, lanes] = low
            if i == 1:
                sums_ref[11:12, lanes] = total_rows(low.astype(F32))

    loop(pairs, both)
    x_load.wait()
    give(9, y_ref, mixed_ref)

    value = sums_ref[0:8, :]
    thirds = []
    for _ in range(3):
        thirds.append(value.astype(BF))
        value = value - thirds[-1].astype(F32)
    value = dot_nt(jnp.concatenate(thirds, axis=0), cube.shuffle(width))
    sums_ref[0:6, :] = (value[0:8] + value[8:16] + value[16:24])[0:6, :]

    rounds = [{"dp": p, "tensor": cube.z} for p in partners]
    rounds += [{"dp": cube.place, "tensor": cube.z ^ 1}, {"dp": cube.place, "tensor": cube.z ^ 2}]

    def pool_sums(i):
        return remote(sums_ref, sums_in.at[i], sum_send.at[i], sum_recv.at[i], rounds[i])

    def next_sum(i):
        if 0 < i <= len(rounds):
            pool_sums(i - 1).wait()
            sums_ref[...] += sums_in[i - 1]
        if i < len(rounds):
            pool_sums(i).start()

    next_sum(0)

    def fold_in(kind, slot, right):
        weight(kind, slot).wait()

        def part(z):
            value = dot_nt(right[:, chunk(z, cols)], weight_tile(wbuf, slot, z))
            dh_ref[...] += value

        loop(parts, part)

    fold_in(0, 0, mixed_ref)
    weight(2, 0).start()
    fold_in(1, 1, near_ref.at[0])
    next_sum(1)
    fold_in(2, 0, near_ref.at[1])
    loop(4, lambda i: swap(pairs - 4 + i).wait_send())
    pool[0] = dot_nt(dh_ref[...].astype(BF), cube.shuffle(width)).astype(BF)

    def send_in(piece):
        back_in.back(pool, 0, back_ref, piece, pieces)

    loop(2, send_in)
    next_sum(2)
    advances(7)
    give(10, y_ref, near_ref.at[1])
    hold(9, y_ref, mixed_ref)
    next_sum(3)
    loop(2, lambda i: send_in(2 + i))
    give(11, y_ref, near_ref.at[0])
    hold(10, y_ref, near_ref.at[1])
    next_sum(4)
    loop(2, lambda i: send_in(4 + i))
    advances(8)
    hold(11, y_ref, near_ref.at[0])
    loop(2, lambda i: send_in(6 + i))
    advances(9)
    for i in range(5, len(rounds) + 1):
        next_sum(i)
    advances(10)
    advances(11)
    advances(12)
    sums_out[...] = sums_ref[...]
    advances(SUBS + top + 2)

    for r in range(SUBS - RING, SUBS):
        stage(r, top).wait_send()
    back_in.back_end(pool, 0, back_ref)
    back_in.back_wait(pool, 0, back_ref)
    back_out.back_wait(near_ref, 1, outputs_ref)


def backward(second_sums, held, count, parts):
    (weights, vectors, x, qkv, other, mixed, chance, z1, r1, y1, gated, slope, normed_rows, dh2, b2) = held
    subs, _, _, depth, cols = weights.shape
    rows, width = x.shape
    levels = count.bit_length() - 1
    half = count // 2
    pairs = width // (2 * HD)
    dma = pltpu.SemaphoreType.DMA
    low = lambda *shape: (shape, BF)
    high = lambda *shape: (shape, F32)
    hbm = pl.BlockSpec(memory_space=pl.ANY)
    vmem = pl.BlockSpec(memory_space=pltpu.VMEM)
    results = [
        high(subs, depth, cols),
        high(16, width),
        low(2, rows // 2, width),
        low(2, rows // 2, width),
    ]
    scratch = [
        low(10, rows, width),
        low(2, 2, 2 * rows, rows),
        low(rows, width),
        high(rows, width),
        high(rows, width),
        high(rows, 128),
        low(rows, width),
        low(rows, width),
        low(2, rows, width),
        low(4, 2, rows, 2 * HD),
        low(2, rows, width),
        low(2, count, parts, depth, cols),
        low(RING, half, parts, depth, cols),
        low(RING, half, parts, depth, cols),
        low(HELD, half, parts, depth, cols),
        low(LINE, parts, depth, cols),
        low(subs, half - 1, parts, depth, cols),
        low(subs, parts + 1, depth, cols),
        high(16, width),
        high(levels + 2, 16, width),
    ]
    return pl.pallas_call(
        functools.partial(backward_kernel, count, parts),
        in_specs=[vmem, vmem] + [hbm] * 14,
        out_specs=[vmem, vmem, hbm, hbm],
        out_shape=[jax.ShapeDtypeStruct(*r) for r in results],
        scratch_shapes=[pltpu.VMEM(*s) for s in scratch]
        + [
            dma((15,)),
            dma((2,)),
            dma((2,)),
            pltpu.SemaphoreType.REGULAR,
            dma((subs, levels)),
            dma((subs, levels)),
            dma((subs, 3)),
            dma((subs, 3)),
            dma((pairs,)),
            dma((pairs,)),
            dma((2, 2)),
            dma((2, 2)),
            dma((2,)),
            dma((levels + 2,)),
            dma((levels + 2,)),
        ],
        compiler_params=pltpu.CompilerParams(
            collective_id=2, has_side_effects=True, vmem_limit_bytes=62 * MIB
        ),
    )(vectors, second_sums, weights, x, qkv, other, mixed, chance, z1, r1, y1, gated, slope, normed_rows, dh2, b2)


def result_kernel(
    rows_ref,
    back_ref,
    down_ref,
    up_ref,
    q_ref,
    k_ref,
    v_ref,
    o_ref,
    sums_ref,
    rows_out,
    input_out,
    down_out,
    up_out,
    q_out,
    k_out,
    v_out,
    o_out,
    *small,
):
    rows_out[...] = rows_ref[...]
    input_out[...] = back_ref[...].astype(F32)
    down_out[...] = down_ref[0].T
    up_out[...] = up_ref[0]

    @pl.when(pl.program_id(0) == 0)
    def _():
        for source, target in ((q_ref, q_out), (k_ref, k_out), (v_ref, v_out)):
            target[...] = source[0]
        o_out[...] = o_ref[0].T
        for i in range(6):
            small[i][...] = sums_ref[i : i + 1, :]
        cols = small[7].shape[1]
        mine = chunk(lax.axis_index("tensor"), cols)
        small[7][...] = sums_ref[10:11, mine]
        small[8][...] = sums_ref[11:12, mine]
        for i in range(4):
            small[6][:, i * cols : (i + 1) * cols] = sums_ref[6 + i : 7 + i, mine]


def results(grads, sums, outputs, back):
    _, depth, cols = grads.shape
    _, rows, width = outputs.shape
    steps = 4
    at = {sub: r for r, sub in enumerate(ORDER)}
    row_spec = pl.BlockSpec((2, rows // steps, width), lambda j: (0, j, 0))
    one = lambda r: pl.BlockSpec((1, depth, cols), lambda j: (r, 0, 0))
    run = lambda r: pl.BlockSpec((1, depth, cols), lambda j: (r + j, 0, 0))
    whole = lambda *shape: pl.BlockSpec(shape, lambda j: (0,) * len(shape))
    high = lambda *shape: jax.ShapeDtypeStruct(shape, F32)
    return pl.pallas_call(
        result_kernel,
        grid=(steps,),
        in_specs=[row_spec, row_spec, run(at[DOWN]), run(at[UP])]
        + [one(at[0]), one(at[1]), one(at[2]), one(at[3]), whole(*sums.shape)],
        out_specs=[
            row_spec,
            row_spec,
            pl.BlockSpec((cols, depth), lambda j: (j, 0)),
            pl.BlockSpec((depth, cols), lambda j: (0, j)),
        ]
        + [whole(depth, cols)] * 3
        + [whole(cols, depth)]
        + [whole(1, width)] * 6
        + [whole(1, 4 * cols), whole(1, cols), whole(1, cols)],
        out_shape=[
            jax.ShapeDtypeStruct(outputs.shape, BF),
            high(*outputs.shape),
            high(4 * cols, depth),
            high(depth, 4 * cols),
        ]
        + [high(depth, cols)] * 3
        + [high(cols, depth)]
        + [high(1, width)] * 6
        + [high(1, 4 * cols), high(1, cols), high(1, cols)],
        compiler_params=pltpu.CompilerParams(vmem_limit_bytes=60 * MIB),
    )(outputs, back, grads, grads, grads, grads, grads, grads, sums)


def shards(
    inputs,
    query_weight,
    query_bias,
    key_weight,
    value_weight,
    value_bias,
    out_weight,
    out_bias,
    first_gain,
    first_shift,
    up_weight,
    up_bias,
    down_weight,
    down_bias,
    second_gain,
    second_shift,
    cotangent,
):
    count, parts = lax.axis_size("dp"), lax.axis_size("tensor")
    flat = lambda *values: [value.reshape(1, -1) for value in values]
    *held, second_sums = forward(
        [query_weight, key_weight, value_weight, out_weight, up_weight, down_weight],
        flat(query_bias, value_bias, up_bias),
        flat(out_bias, first_gain, first_shift, down_bias, second_gain, second_shift),
        inputs,
        cotangent,
        count,
        parts,
    )
    grads, sums, outputs, back = backward(second_sums, held, count, parts)
    outputs, input_grad, down, up, query, key, value, out, *small = results(grads, sums, outputs, back)
    small = [row.reshape(-1) for row in small]
    return (
        outputs,
        input_grad,
        query,
        small[7],
        key,
        value,
        small[8],
        out,
        small[2],
        small[0],
        small[1],
        up,
        small[6],
        down,
        small[5],
        small[3],
        small[4],
    )


def solution(mesh):
    rows = P(None, ("dp", "tensor"), None)
    return jax.shard_map(
        shards,
        mesh=mesh,
        in_specs=(
            rows,
            P("dp", "tensor"),
            P("tensor"),
            P("dp", "tensor"),
            P("dp", "tensor"),
            P("tensor"),
            P("tensor", "dp"),
            P(),
            P(),
            P(),
            P("dp", "tensor"),
            P("tensor"),
            P("tensor", "dp"),
            P(),
            P(),
            P(),
            rows,
        ),
        out_specs=(
            rows,
            rows,
            P("dp", "tensor"),
            P("tensor"),
            P("dp", "tensor"),
            P("dp", "tensor"),
            P("tensor"),
            P("tensor", "dp"),
            P(),
            P(),
            P(),
            P("dp", "tensor"),
            P("tensor"),
            P("tensor", "dp"),
            P(),
            P(),
            P(),
        ),
        check_vma=False,
    )
```

```python
import functools
import math

import jax
import jax.numpy as jnp
from jax import lax
from jax.experimental import pallas as pl
from jax.experimental.pallas import tpu as pltpu
from jax.sharding import PartitionSpec as P

HD = 64
LEN = 1024
EPSILON = 1e-05
SCALE = HD ** (-0.5)
LOG2E = math.log2(math.e)
BF = jnp.bfloat16
F32 = jnp.float32
MIB = 1 << 20


def dot_nn(left, right):
    return jnp.dot(left, right, preferred_element_type=F32)


def dot_nt(left, right):
    return lax.dot_general(left, right, (((1,), (1,)), ((), ())), preferred_element_type=F32)


def dot_tn(left, right):
    return lax.dot_general(left, right, (((0,), (0,)), ((), ())), preferred_element_type=F32)


OUT_BIAS, FIRST_GAIN, FIRST_SHIFT, DOWN_BIAS, SECOND_GAIN, SECOND_SHIFT = range(6)


def vector(ref, place):
    return ref[place : place + 1, :]


def normed(hidden):
    average = jnp.mean(hidden, axis=-1, keepdims=True)
    center = hidden - average
    spread = jnp.mean(center * center, axis=-1, keepdims=True)
    inverse = lax.rsqrt(spread + EPSILON)
    return center * inverse, inverse


def norm_back(grad, z, inverse, gain):
    scaled = grad * gain
    average = jnp.mean(scaled, axis=-1, keepdims=True)
    along = jnp.mean(scaled * z, axis=-1, keepdims=True)
    return (scaled - average - z * along) * inverse


def total_rows(value):
    return jnp.sum(value, axis=0, keepdims=True)


def remote(source, target, send, receive, device):
    return pltpu.make_async_remote_copy(
        source, target, send, receive, device_id=device, device_id_type=pl.DeviceIdType.MESH
    )


def greet(devices):
    barrier = pltpu.get_barrier_semaphore()
    for device in devices:
        pl.semaphore_signal(barrier, 1, device_id=device, device_id_type=pl.DeviceIdType.MESH)
    pl.semaphore_wait(barrier, len(devices))


class Cube:
    def __init__(self, count, parts):
        self.count, self.parts, self.half = count, parts, parts // 2
        self.place, self.z = lax.axis_index("dp"), lax.axis_index("tensor")
        self.core = lax.rem(self.place, 2)
        self.levels = count.bit_length() - 1
        bits = [1 << i for i in range(1, self.levels)]
        self.orders = [bits, bits[::-1]]

    def stages(self):
        ups, downs = self.orders
        out = []
        for up, down in zip(ups, downs):
            out.append(self.place ^ jnp.where(self.core == 0, up, down))
        return out + [self.place ^ 1]

    def masks(self):
        table = []
        for order in self.orders:
            held = [0]
            for bit in order:
                held = held + [m ^ bit for m in held]
            table.append(held)
        return [a + [m ^ 1 for m in b] for a, b in (table, table[::-1])]

    def column(self):
        mine = [{"dp": self.place, "tensor": lax.rem(self.z + d, self.parts)} for d in range(1, self.parts)]
        others = [{"dp": self.place ^ 1, "tensor": lax.rem(self.z + d, self.parts)} for d in range(self.parts)]
        return mine + others

    def neighbours(self):
        return [{"dp": p, "tensor": self.z} for p in self.stages()[:-1]]

    def shuffle(self, width):
        depth = width // self.count
        column = lax.broadcasted_iota(jnp.int32, (1, width), 1)
        slot = column // depth
        far = slot // (self.count // 2)
        flips = far
        for level, (up, down) in enumerate(zip(*self.orders)):
            bit = jnp.where(self.core == 0, up, down)
            other = jnp.where(self.core == 0, down, up)
            held = lax.rem(slot // (1 << level), 2)
            flips = flips + held * jnp.where(far == 0, bit, other)
        owner = self.place ^ flips
        source = owner * depth + lax.rem(column, depth)
        row = lax.broadcasted_iota(jnp.int32, (width, width), 0)
        return (row == source).astype(F32).astype(BF)


class Rows:
    def __init__(self, cube, send, receive, here):
        self.cube, self.send, self.receive, self.here = cube, send, receive, here
        c = cube
        self.slot = lax.rem(c.z, c.half)
        self.targets = [(c.place - c.core + c.z // c.half, m * c.half + c.core) for m in range(2)]
        self.micro = c.z // c.half
        self.sources = [(c.place - c.core + lax.rem(c.z, c.half), c.half * c.core + p) for p in range(2)]

    def own(self, device):
        return jnp.logical_and(device[0] == self.cube.place, device[1] == self.cube.z)

    def at(self, device):
        return {"dp": device[0], "tensor": device[1]}

    def into(self, source, target, piece, pieces):
        size = source.shape[1] // pieces
        at = pl.ds(pl.multiple_of(piece * size, size), size)
        for m, device in enumerate(self.targets):
            own = self.own(device)

            @pl.when(own)
            def _(m=m):
                pltpu.make_async_copy(source.at[m, at], target.at[self.slot, at], self.here).start()

            @pl.when(jnp.logical_not(own))
            def _(m=m, device=device):
                remote(
                    source.at[m, at],
                    target.at[self.slot, at],
                    self.send.at[m],
                    self.receive.at[self.slot],
                    self.at(device),
                ).start()

    def into_wait(self, source, target):
        for p, device in enumerate(self.sources):
            own = self.own(device)

            @pl.when(own)
            def _(p=p):
                pltpu.make_async_copy(source.at[0], target.at[p], self.here).wait()

            @pl.when(jnp.logical_not(own))
            def _(p=p, device=device):
                remote(
                    source.at[0], target.at[p], self.send.at[0], self.receive.at[p], self.at(device)
                ).wait_recv()

    def into_end(self, source, target):
        for m, device in enumerate(self.targets):

            @pl.when(jnp.logical_not(self.own(device)))
            def _(m=m, device=device):
                remote(
                    source.at[m], target.at[self.slot], self.send.at[m], self.receive.at[0], self.at(device)
                ).wait_send()


    def back(self, source, lead, target, piece, pieces):
        size = target.shape[1] // pieces
        for p, device in enumerate(self.sources):
            own = self.own(device)
            here = pl.ds(pl.multiple_of(p * target.shape[1] + piece * size, size), size)
            there = pl.ds(pl.multiple_of(piece * size, size), size)

            @pl.when(own)
            def _(here=here, there=there):
                pltpu.make_async_copy(
                    source.at[lead, here], target.at[self.micro, there], self.here
                ).start()

            @pl.when(jnp.logical_not(own))
            def _(p=p, device=device, here=here, there=there):
                remote(
                    source.at[lead, here],
                    target.at[self.micro, there],
                    self.send.at[p],
                    self.receive.at[self.micro],
                    self.at(device),
                ).start()

    def back_wait(self, source, lead, target):
        rows = target.shape[1]
        for m, device in enumerate(self.targets):

            @pl.when(jnp.logical_not(self.own(device)))
            def _(m=m, device=device):
                remote(
                    source.at[lead, pl.ds(0, rows)],
                    target.at[m],
                    self.send.at[0],
                    self.receive.at[m],
                    self.at(device),
                ).wait_recv()

    def back_end(self, source, lead, target):
        rows = target.shape[1]
        for p, device in enumerate(self.sources):
            own = self.own(device)

            @pl.when(own)
            def _(p=p):
                pltpu.make_async_copy(
                    source.at[lead, pl.ds(p * rows, rows)], target.at[self.micro], self.here
                ).wait()

            @pl.when(jnp.logical_not(own))
            def _(p=p, device=device):
                remote(
                    source.at[lead, pl.ds(p * rows, rows)],
                    target.at[self.micro],
                    self.send.at[p],
                    self.receive.at[0],
                    self.at(device),
                ).wait_send()


SUBS, UP, DOWN = 12, 4, 8
XS, XP, CS, CP, LEAD = 0, 4, 4, 8, 0
PACE = [4, 5, 6, 7, 7, 8, 9, 10, 11, 12, 13, 13]


def loop(count, body):
    lax.fori_loop(0, count, lambda i, _: (body(i), None)[1], None)


def chunk(i, size):
    return pl.ds(pl.multiple_of(i * size, size), size)


def weight_tile(ref, slot, z):
    value = ref[slot, :, z]
    return value.reshape(-1, value.shape[-1])


def forward_kernel(
    count,
    parts,
    q_in,
    k_in,
    v_in,
    o_in,
    up_in,
    down_in,
    q_bias,
    v_bias,
    up_bias,
    vec0,
    vec1,
    vec2,
    vec3,
    vec4,
    vec5,
    in_ref,
    cot_ref,
    weights_ref,
    vec_out,
    x_out,
    qkv_out,
    other_out,
    mixed_out,
    chance_out,
    z1_out,
    r1_out,
    y1_out,
    gated_out,
    slope_out,
    normed_out,
    dh2_out,
    b2_out,
    sums_out,
    local_ref,
    o_raw,
    down_raw,
    bias_ref,
    vec_ref,
    raw_ref,
    cot_raw,
    shuffle_ref,
    x_ref,
    c_ref,
    bias_all,
    qkv_ref,
    other_ref,
    mixed_ref,
    chance_ref,
    z1_ref,
    r1_ref,
    y1_ref,
    gated_ref,
    slope_ref,
    acc_ref,
    normed_ref,
    dh2_ref,
    b2_ref,
    sums_ref,
    wbuf,
    prep_sem,
    local_sem,
    zs,
    zr,
    ss,
    sr,
    wsem,
    bias_send,
    bias_recv,
    row_send,
    row_recv,
    row_here,
    kv_send,
    kv_recv,
    out_sem,
    save_sem,
):
    cube = Cube(count, parts)
    partners, levels = cube.stages(), cube.levels
    shifts = [lax.rem(cube.z + d, parts) for d in range(1, parts)]
    ahead = 5
    rows = x_ref.shape[0]
    cols = weights_ref.shape[-1]
    depth = weights_ref.shape[-2]
    sources = [k_in, v_in, q_in] + [up_in.at[:, i * cols : (i + 1) * cols] for i in range(4)]
    places = [local_ref.at[i] for i in (0, 1, 2, 4, 5, 6, 7)]
    prep = [
        pltpu.make_async_copy(source, place, prep_sem.at[i])
        for i, (source, place) in enumerate(zip(sources + [o_in, down_in], places + [o_raw, down_raw]))
    ]
    for copy in prep:
        copy.start()
    bias_ref[...] = jnp.zeros_like(bias_ref)
    bias_ref[0:1, :] = q_bias[...]
    bias_ref[1:2, :] = v_bias[...]
    for i in range(4):
        bias_ref[2 + i : 3 + i, :] = up_bias[:, i * cols : (i + 1) * cols]
    same = lax.broadcasted_iota(jnp.int32, (depth, depth), 0) == lax.broadcasted_iota(
        jnp.int32, (depth, depth), 1
    )
    eye = same.astype(F32).astype(BF)
    greet(cube.column() + cube.neighbours())
    for i in range(3):
        prep[i].wait()

    def own(sub):
        return pltpu.make_async_copy(local_ref.at[sub], weights_ref.at[sub, 0, cube.z], local_sem.at[sub])

    inner = jnp.logical_or(cube.z == 1, cube.z == 2)
    mine, theirs = cube.z // 2 * 2, 2 - cube.z // 2 * 2

    def along(sub, hop):
        if hop == 0:
            source, target, z = local_ref.at[sub], weights_ref.at[sub, 0, cube.z], cube.z ^ 1
        else:
            source = weights_ref.at[sub, 0, pl.ds(mine if hop == 1 else theirs, 2)]
            target, z = source, (3 - cube.z if hop == 1 else cube.z ^ 1)
        return remote(
            source, target, zs.at[sub, hop], zr.at[sub, hop], {"dp": cube.place, "tensor": z}
        )

    def stage(sub, level):
        size = 1 << level
        return remote(
            weights_ref.at[sub, pl.ds(0, size)],
            weights_ref.at[sub, pl.ds(size, size)],
            ss.at[sub, level],
            sr.at[sub, level],
            {"dp": partners[level], "tensor": cube.z},
        )

    def begin(sub):
        own(sub).start()
        along(sub, 0).start()

    def pass_pair(sub):
        own(sub).wait()
        along(sub, 0).wait_recv()

        @pl.when(inner)
        def _():
            along(sub, 1).start()

    def pass_on(sub):
        @pl.when(inner)
        def _():
            along(sub, 1).wait_recv()
            along(sub, 2).start()

    def first_stage(sub):
        @pl.when(jnp.logical_not(inner))
        def _():
            along(sub, 2).wait_recv()

        stage(sub, 0).start()

    def prepare(sub):
        @pl.when(sub + 1 < SUBS)
        def _():
            pass_on(sub + 1)

        @pl.when(sub + 2 < SUBS)
        def _():
            pass_pair(sub + 2)

        @pl.when(sub + ahead < SUBS)
        def _():
            begin(sub + ahead)

    def relay(step):
        @pl.when(step < SUBS)
        def _():
            first_stage(step)

        for level in range(levels):
            sub = step - level - 1

            @pl.when(jnp.logical_and(sub >= 0, sub < SUBS))
            def _(sub=sub, level=level):
                stage(sub, level).wait_recv()
                if level + 1 < levels:
                    stage(sub, level + 1).start()

        @pl.when(jnp.logical_and(step >= XS, step < XS + XP))
        def _():
            rows_x.into(in_ref, raw_ref, step - XS, XP)

        @pl.when(jnp.logical_and(step >= CS, step < CS + CP))
        def _():
            rows_c.into(cot_ref, cot_raw, step - CS, CP)

        @pl.when(step < LEAD)
        def _():
            prepare(2 * step)
            prepare(2 * step + 1)

        @pl.when(step >= LEAD)
        def _():
            prepare(step + LEAD)

    done = [0]

    def relays(last):
        if last > done[0]:
            first = done[0]
            loop(last - first, lambda i: relay(first + i))
            done[0] = last

    def load(sub):
        return pltpu.make_async_copy(weights_ref.at[sub], wbuf.at[sub % 4], wsem.at[sub % 4])

    def share_bias(d):
        return remote(
            bias_ref,
            bias_all.at[cube.z],
            bias_send.at[d],
            bias_recv.at[d],
            {"dp": cube.place, "tensor": shifts[d]},
        )

    rows_x = Rows(cube, row_send.at[0], row_recv.at[0], row_here.at[0])
    rows_c = Rows(cube, row_send.at[1], row_recv.at[1], row_here.at[1])
    outs = []

    def keep(source, target):
        copy = pltpu.make_async_copy(source, target, out_sem.at[len(outs)])
        copy.start()
        outs.append(copy)

    loop(3, begin)
    for copy in prep[3:]:
        copy.wait()
    local_ref[3] = dot_nt(eye, o_raw[...]).astype(BF)
    loop(ahead - 3, lambda i: begin(3 + i))
    for i in range(4):
        local_ref[DOWN + i] = dot_nt(eye, down_raw[i * cols : (i + 1) * cols, :]).astype(BF)
    for d in range(parts - 1):
        share_bias(d).start()
    pass_pair(0)
    pass_pair(1)
    pass_on(0)
    shuffle_ref[...] = cube.shuffle(x_ref.shape[1])
    bias_all[cube.z] = bias_ref[...]
    value = jnp.concatenate([v[...] for v in (vec0, vec1, vec2, vec3, vec4, vec5)] + [vec0[...]] * 2, axis=0)
    thirds = []
    for _ in range(3):
        thirds.append(value.astype(BF))
        value = value - thirds[-1].astype(F32)
    value = dot_nn(jnp.concatenate(thirds, axis=0), shuffle_ref[...])
    vec_ref[...] = value[0:8] + value[8:16] + value[16:24]
    keep(vec_ref, vec_out)
    relays(levels + 1)
    load(0).start()
    rows_x.into_wait(in_ref, raw_ref)
    half_rows = raw_ref.shape[1]
    for p in range(2):
        x_ref[p * half_rows : (p + 1) * half_rows, :] = dot_nn(raw_ref[p], shuffle_ref[...]).astype(BF)
    for d in range(parts - 1):
        share_bias(d).wait_recv()
    relays(max(PACE[0], levels + 2))
    load(1).start()

    def swap(kind):
        return remote(
            qkv_ref.at[kind],
            other_ref.at[kind - 1],
            kv_send.at[kind - 1],
            kv_recv.at[kind - 1],
            {"dp": cube.place ^ 1, "tensor": cube.z},
        )

    for sub, kind in enumerate((1, 2, 0)):
        load(sub).wait()

        def project(z, sub=sub, kind=kind):
            acc = dot_nn(x_ref[...], weight_tile(wbuf, sub, z))
            if kind == 0:
                acc = (acc + bias_all[z, 0:1, :]) * SCALE
            elif kind == 2:
                acc = acc + bias_all[z, 1:2, :]
            qkv_ref[kind, :, chunk(z, cols)] = acc.astype(BF)

        loop(parts, project)
        if kind > 0:
            swap(kind).start()
        if sub == 0:
            relays(max(PACE[1], levels + 3))
            load(2).start()
        elif sub == 1:
            relays(PACE[2])

    keep(x_ref, x_out)
    keep(qkv_ref, qkv_out)
    relays(max(PACE[3], levels + 4))
    load(3).start()
    for kind in (1, 2):
        swap(kind).wait_recv()
    keep(other_ref, other_out)

    def save(pair):
        slot = lax.rem(pair, 2)
        return pltpu.make_async_copy(chance_ref.at[slot], chance_out.at[pair], save_sem.at[slot])

    def attend(pair):
        lanes = chunk(pair, 2 * HD)
        q2 = qkv_ref[0, :, lanes]
        k2 = [qkv_ref[1, :, lanes], other_ref[0, :, lanes]]
        v2 = [qkv_ref[2, :, lanes], other_ref[1, :, lanes]]
        mixed = []
        slot = lax.rem(pair, 2)

        @pl.when(pair >= 2)
        def _():
            save(pair - 2).wait()

        for head in range(2):
            part = slice(head * HD, head * HD + HD)
            scores = [dot_nt(k[:, part], q2[:, part]) for k in k2]
            top = functools.reduce(jnp.maximum, [jnp.max(s, axis=0, keepdims=True) for s in scores])
            base = top * LOG2E
            expo = [jnp.exp2(s * LOG2E - base) for s in scores]
            total = functools.reduce(jnp.add, [jnp.sum(e, axis=0, keepdims=True) for e in expo])
            inverse = 1.0 / total
            chance = [(e * inverse).astype(BF) for e in expo]
            mixed.append(functools.reduce(jnp.add, [dot_tn(v[:, part], c) for c, v in zip(chance, v2)]))
            for i in range(2):
                chance_ref[slot, head, i * rows : (i + 1) * rows, :] = chance[i]
        mixed_ref[:, lanes] = jnp.concatenate(mixed, axis=0).T.astype(BF)
        save(pair).start()

    pairs = mixed_ref.shape[1] // (2 * HD)
    loop(2, attend)
    relays(PACE[4])
    loop(2, lambda i: attend(2 + i))
    relays(PACE[5])
    loop(2, lambda i: attend(4 + i))
    relays(PACE[6])
    loop(pairs - 6, lambda i: attend(6 + i))
    relays(max(PACE[7], levels + 6))
    keep(mixed_ref, mixed_out)
    loop(2, lambda i: save(pairs - 2 + i).wait())

    load(4).start()
    load(5).start()
    load(3).wait()

    def mix(z):
        value = dot_nt(mixed_ref[:, chunk(z, cols)], weight_tile(wbuf, 3, z))

        @pl.when(z == 0)
        def _():
            acc_ref[...] = value

        @pl.when(z > 0)
        def _():
            acc_ref[...] += value

    loop(parts, mix)
    size = 128

    def norm_first(i):
        at = chunk(i, size)
        hidden = x_ref[at, :].astype(F32) + acc_ref[at, :] + vector(vec_ref, OUT_BIAS)
        z, inverse = normed(hidden)
        z1_ref[at, :] = z
        r1_ref[at, :] = jnp.broadcast_to(inverse, (size, 128))
        y = z * vector(vec_ref, FIRST_GAIN) + vector(vec_ref, FIRST_SHIFT)
        y1_ref[at, :] = y.astype(BF)
        acc_ref[at, :] = y + vector(vec_ref, DOWN_BIAS)

    loop(rows // size, norm_first)
    keep(z1_ref, z1_out)
    keep(r1_ref, r1_out)
    keep(y1_ref, y1_out)

    def gate(sub):
        load(sub).wait()

        def part(z):
            lanes = chunk(z, cols)
            upper = dot_nn(y1_ref[...], weight_tile(wbuf, sub % 4, z)) + bias_all[z, sub - UP + 2 : sub - UP + 3, :]
            half = 0.5 + 0.5 * lax.erf(upper * (0.5**0.5))
            gated_ref[sub - UP, :, lanes] = (upper * half).astype(BF)
            bell = jnp.exp(upper * upper * -0.5) * ((2 * math.pi) ** -0.5)
            slope_ref[sub - UP, :, lanes] = (half + upper * bell).astype(BF)

        loop(parts, part)
        keep(gated_ref.at[sub - UP], gated_out.at[sub - UP])
        keep(slope_ref.at[sub - UP], slope_out.at[sub - UP])

    for sub in range(UP, DOWN):
        gate(sub)
        relays(max(PACE[8 + sub - UP], sub + 2 + levels + 1))
        load(sub + 2).start()

    rows_c.into_wait(cot_ref, cot_raw)
    for p in range(2):
        c_ref[p * half_rows : (p + 1) * half_rows, :] = dot_nn(cot_raw[p], shuffle_ref[...]).astype(BF)

    for sub in range(DOWN, SUBS):
        if sub == DOWN:
            relays(DOWN + 2 + levels + 1)
            load(DOWN + 2).start()
        elif sub == SUBS - 1:
            relays(SUBS + levels)
            load(sub).start()
        load(sub).wait()

        def fold(z, sub=sub):
            acc_ref[...] += dot_nt(gated_ref[sub - DOWN, :, chunk(z, cols)], weight_tile(wbuf, sub % 4, z))

        loop(parts, fold)

    sums_ref[...] = jnp.zeros_like(sums_ref)

    def norm_second(i):
        at = chunk(i, size)
        z, inverse = normed(acc_ref[at, :])
        gain = vector(vec_ref, SECOND_GAIN)
        normed_ref[at, :] = (z * gain + vector(vec_ref, SECOND_SHIFT)).astype(BF)
        grad = c_ref[at, :].astype(F32)
        dh = norm_back(grad, z, inverse, gain)
        dh2_ref[at, :] = dh
        b2_ref[at, :] = dh.astype(BF)
        sums_ref[0:1, :] += total_rows(grad * z)
        sums_ref[1:2, :] += total_rows(grad)
        sums_ref[2:3, :] += total_rows(dh)

    loop(rows // size, norm_second)
    keep(normed_ref, normed_out)
    keep(dh2_ref, dh2_out)
    keep(b2_ref, b2_out)
    keep(sums_ref, sums_out)

    def sent(sub):
        along(sub, 0).wait_send()

        @pl.when(inner)
        def _():
            along(sub, 1).wait_send()
            along(sub, 2).wait_send()

        for level in range(levels):
            stage(sub, level).wait_send()

    loop(SUBS, sent)
    for d in range(parts - 1):
        share_bias(d).wait_send()
    for kind in (1, 2):
        swap(kind).wait_send()
    rows_x.into_end(in_ref, raw_ref)
    rows_c.into_end(cot_ref, cot_raw)
    for copy in outs:
        copy.wait()


def forward(weights, biases, vectors, inputs, cotangent, count, parts):
    subs = SUBS
    depth, cols = weights[0].shape
    _, half_rows, width = inputs.shape
    rows = 2 * half_rows
    levels = count.bit_length() - 1
    pairs = width // (2 * HD)
    dma = pltpu.SemaphoreType.DMA
    low = lambda *shape: (shape, BF)
    high = lambda *shape: (shape, F32)
    results = [
        low(subs, count, parts, depth, cols),
        high(8, width),
        low(rows, width),
        low(3, rows, width),
        low(2, rows, width),
        low(rows, width),
        low(pairs, 2, 2 * rows, rows),
        high(rows, width),
        high(rows, 128),
        low(rows, width),
        low(4, rows, parts * cols),
        low(4, rows, parts * cols),
        low(rows, width),
        high(rows, width),
        low(rows, width),
        high(8, width),
    ]
    scratch = [
        low(subs, depth, cols),
        low(cols, depth),
        low(4 * cols, depth),
        high(8, cols),
        high(8, width),
        low(2, half_rows, width),
        low(2, half_rows, width),
        low(width, width),
        low(rows, width),
        low(rows, width),
        high(parts, 8, cols),
        low(3, rows, width),
        low(2, rows, width),
        low(rows, width),
        low(2, 2, 2 * rows, rows),
        high(rows, width),
        high(rows, 128),
        low(rows, width),
        low(4, rows, parts * cols),
        low(4, rows, parts * cols),
        high(rows, width),
        low(rows, width),
        high(rows, width),
        low(rows, width),
        high(8, width),
        low(4, count, parts, depth, cols),
    ]
    hbm = pl.BlockSpec(memory_space=pl.ANY)
    vmem = pl.BlockSpec(memory_space=pltpu.VMEM)
    return pl.pallas_call(
        functools.partial(forward_kernel, count, parts),
        in_specs=[hbm] * 6 + [vmem] * 9 + [hbm, hbm],
        out_specs=[hbm] * len(results),
        out_shape=[jax.ShapeDtypeStruct(*r) for r in results],
        scratch_shapes=[pltpu.VMEM(*s) for s in scratch]
        + [
            dma((9,)),
            dma((subs,)),
            dma((subs, 3)),
            dma((subs, 3)),
            dma((subs, levels)),
            dma((subs, levels)),
            dma((4,)),
            dma((parts - 1,)),
            dma((parts - 1,)),
            dma((2, 2)),
            dma((2, 2)),
            dma((2,)),
            dma((2,)),
            dma((2,)),
            dma((24,)),
            dma((2,)),
        ],
        compiler_params=pltpu.CompilerParams(
            collective_id=1, has_side_effects=True, vmem_limit_bytes=62 * MIB
        ),
    )(*weights, *biases, *vectors, inputs, cotangent)


HELD, RING, LINE = 5, 2, 4
ORDER = [8, 9, 10, 11, 3, 4, 5, 6, 7, 2, 1, 0]


def backward_kernel(
    count,
    parts,
    vec_ref,
    second_ref,
    weights_ref,
    x_in,
    qkv_in,
    other_in,
    mixed_in,
    chance_in,
    z1_in,
    r1_in,
    y1_in,
    gated_in,
    slope_in,
    normed_in,
    dh2_in,
    b2_in,
    grads_ref,
    sums_out,
    outputs_ref,
    back_ref,
    pool,
    chance_ref,
    y_ref,
    dh_ref,
    z1_ref,
    r1_ref,
    b_ref,
    mixed_ref,
    near_ref,
    far_ref,
    swap_ref,
    wbuf,
    send_ref,
    staged_ref,
    held_ref,
    line_ref,
    small_ref,
    zed_ref,
    sums_ref,
    sums_in,
    load_sem,
    fetch_sem,
    wsem,
    free_sem,
    ss,
    sr,
    zs,
    zr,
    swap_send,
    swap_recv,
    row_send,
    row_recv,
    row_here,
    sum_send,
    sum_recv,
):
    cube = Cube(count, parts)
    partners, levels = cube.stages(), cube.levels
    top = levels - 1
    half = count // 2
    shifts = [lax.rem(cube.z + d, parts) for d in range(1, parts)]
    rows, width = b_ref.shape
    cols = weights_ref.shape[-1]
    depth = weights_ref.shape[-2]
    wide = half * depth
    size = 128

    pairs = width // (2 * HD)

    def fetch(pair):
        slot = lax.rem(pair, 2)
        return pltpu.make_async_copy(chance_in.at[pair], chance_ref.at[slot], fetch_sem.at[slot])

    def load(place, source, target):
        return pltpu.make_async_copy(source, target, load_sem.at[place])

    def weight(sub, slot):
        return pltpu.make_async_copy(weights_ref.at[sub], wbuf.at[slot], wsem.at[slot])

    gate_load = [load(j % 2, gated_in.at[j], pool.at[j % 2]) for j in range(4)]
    slope_load = [load(2 + j % 2, slope_in.at[j], pool.at[2 + j % 2]) for j in range(4)]
    b_load = load(4, b2_in, b_ref)
    out_load = load(5, normed_in, near_ref.at[0])
    y_load = load(6, y1_in, y_ref)
    dh_load = load(7, dh2_in, dh_ref)
    z_load = load(8, z1_in, z1_ref)
    r_load = load(9, r1_in, r1_ref)
    mixed_load = load(10, mixed_in, mixed_ref)
    qkv_load = load(12, qkv_in, pool.at[pl.ds(0, 3)])
    other_load = load(13, other_in, pool.at[pl.ds(8, 2)])
    x_load = load(14, x_in, y_ref)

    def stage(r, level):
        if level == top:
            source, target = send_ref.at[lax.rem(r, RING)], staged_ref.at[lax.rem(r, RING)]
        else:
            source = held_ref.at[lax.rem(r, HELD), pl.ds(1 << level, 1 << level)]
            target = small_ref.at[r, pl.ds((1 << level) - 1, 1 << level)]
        return remote(
            source, target, ss.at[r, level], sr.at[r, level], {"dp": partners[level], "tensor": cube.z}
        )

    inner = jnp.logical_or(cube.z == 1, cube.z == 2)
    mine, theirs = cube.z // 2 * 2, 2 - cube.z // 2 * 2

    def along(r, hop):
        line = lax.rem(r, LINE)
        if hop == 0:
            source = line_ref.at[line, pl.ds(jnp.where(cube.z == 0, 1, 0), parts - 1)]
            target, z = zed_ref.at[r, pl.ds(0, parts - 1)], cube.z ^ 1
        elif hop == 1:
            source = line_ref.at[line, pl.ds(theirs, 2)]
            target, z = zed_ref.at[r, pl.ds(parts - 1, 2)], 3 - cube.z
        else:
            source = line_ref.at[line, cube.z ^ 1]
            target, z = zed_ref.at[r, 0], cube.z ^ 1
        return remote(source, target, zs.at[r, hop], zr.at[r, hop], {"dp": cube.place, "tensor": z})

    def add_line(r, block, place):
        line = lax.rem(r, LINE)
        value = line_ref[line, block].astype(F32) + zed_ref[r, place].astype(F32)
        line_ref[line, block] = value.astype(BF)

    def give(r, left, right):
        if r >= RING:
            stage(r - RING, top).wait_send()
        value = dot_tn(left[:, wide:], right[...]).astype(BF)
        for z in range(parts):
            send_ref[r % RING, :, z] = value[:, z * cols : (z + 1) * cols].reshape(half, depth, cols)
        if r >= RING:
            pl.semaphore_wait(free_sem, 1)
        stage(r, top).start()

    def hold(r, left, right):
        advances(r - HELD + top)
        value = dot_tn(left[:, :wide], right[...])
        stage(r, top).wait_recv()
        for z in range(parts):
            part = value[:, z * cols : (z + 1) * cols].reshape(half, depth, cols)
            part = part + staged_ref[r % RING, :, z].astype(F32)
            held_ref[r % HELD, :, z] = part.astype(BF)
        if r + RING < SUBS:
            pl.semaphore_signal(
                free_sem,
                1,
                device_id={"dp": cube.place ^ 1, "tensor": cube.z},
                device_id_type=pl.DeviceIdType.MESH,
            )
        stage(r, top - 1).start()

    def advance(k):
        for i in range(top):
            level = top - 1 - i
            r = k - i

            @pl.when(jnp.logical_and(r >= 0, r < SUBS))
            def _(r=r, level=level):
                stage(r, level).wait_recv()
                place = lax.rem(r, HELD)

                def fold(slot):
                    value = held_ref[place, slot].astype(F32)
                    value = value + small_ref[r, (1 << level) - 1 + slot].astype(F32)
                    if level > 0:
                        held_ref[place, slot] = value.astype(BF)
                    else:
                        line_ref[lax.rem(r, LINE)] = value.astype(BF)

                loop(1 << level, fold)
                if level > 0:
                    stage(r, level - 1).start()
                else:

                    @pl.when(jnp.logical_not(inner))
                    def _():
                        along(r, 0).start()

                    for other in range(top):
                        stage(r, other).wait_send()

        r = k - top

        @pl.when(jnp.logical_and(inner, jnp.logical_and(r >= 0, r < SUBS)))
        def _(r=r):
            along(r, 0).wait_recv()
            for i in range(parts - 1):
                add_line(r, jnp.where(cube.z == 1, 1, 0) + i, i)
            along(r, 1).start()

        r = k - top - 1

        @pl.when(jnp.logical_and(inner, jnp.logical_and(r >= 0, r < SUBS)))
        def _(r=r):
            along(r, 1).wait_recv()
            for i in range(2):
                add_line(r, mine + i, parts - 1 + i)
            along(r, 2).start()
            grads_ref[r] = line_ref[lax.rem(r, LINE), cube.z].astype(F32)

        r = k - top - 2

        @pl.when(jnp.logical_and(r >= 0, r < SUBS))
        def _(r=r):
            @pl.when(inner)
            def _():
                along(r, 1).wait_send()
                along(r, 2).wait_send()

            @pl.when(jnp.logical_not(inner))
            def _():
                along(r, 2).wait_recv()
                value = line_ref[lax.rem(r, LINE), cube.z].astype(F32)
                grads_ref[r] = value + zed_ref[r, 0].astype(F32)
                along(r, 0).wait_send()

    done = [0]

    def advances(last):
        if last > done[0]:
            first = done[0]
            loop(last - first, lambda i: advance(first + i))
            done[0] = last

    back_out = Rows(cube, row_send.at[0], row_recv.at[0], row_here.at[0])
    back_in = Rows(cube, row_send.at[1], row_recv.at[1], row_here.at[1])
    pieces = 8

    sums_ref[...] = jnp.zeros_like(sums_ref)
    sums_ref[3:6, :] = second_ref[0:3, :]

    b_load.start()
    gate_load[0].start()
    weight(8, 0).start()
    slope_load[0].start()
    gate_load[1].start()
    out_load.start()
    y_load.start()
    greet(cube.column() + cube.neighbours())
    b_load.wait()
    gate_load[0].wait()
    give(0, b_ref, pool.at[0])
    slope_load[1].start()
    weight(9, 1).start()
    dh_load.start()
    z_load.start()
    r_load.start()
    mixed_load.start()
    loop(2, lambda i: fetch(i).start())
    gate_load[1].wait()
    give(1, b_ref, pool.at[1])

    out_load.wait()
    near_ref[1] = dot_nt(near_ref[0], cube.shuffle(width)).astype(BF)

    def send_out(piece):
        back_out.back(near_ref, 1, outputs_ref, piece, pieces)

    loop(2, send_out)
    hold(0, b_ref, pool.at[0])
    gate_load[2].start()

    def gate_back(j):
        slope_load[j].wait()
        weight(8 + j, j % 2).wait()

        def part(z):
            lanes = chunk(z, cols)
            grad = dot_nn(b_ref[...], weight_tile(wbuf, j % 2, z))
            low = (grad * pool[2 + j % 2, :, lanes].astype(F32)).astype(BF)
            pool[4 + j, :, lanes] = low
            sums_ref[6 + j : 7 + j, lanes] = total_rows(low.astype(F32))

        loop(parts, part)

    gate_back(0)
    slope_load[2].start()
    weight(10, 0).start()
    loop(2, lambda i: send_out(2 + i))
    hold(1, b_ref, pool.at[1])
    gate_load[3].start()
    gate_load[2].wait()
    give(2, b_ref, pool.at[0])
    gate_back(1)
    slope_load[3].start()
    weight(11, 1).start()
    loop(2, lambda i: send_out(4 + i))
    gate_load[3].wait()
    give(3, b_ref, pool.at[1])
    hold(2, b_ref, pool.at[0])
    gate_back(2)
    weight(4, 0).start()
    loop(2, lambda i: send_out(6 + i))
    hold(3, b_ref, pool.at[1])
    advances(1)
    gate_back(3)
    weight(5, 1).start()
    qkv_load.start()
    other_load.start()

    def fold_up(j):
        weight(4 + j, j % 2).wait()

        def part(z):
            dh_ref[...] += dot_nt(pool[4 + j, :, chunk(z, cols)], weight_tile(wbuf, j % 2, z))

        loop(parts, part)

    dh_load.wait()
    fold_up(0)
    weight(6, 0).start()
    fold_up(1)
    weight(7, 1).start()
    fold_up(2)
    weight(3, 0).start()
    fold_up(3)

    z_load.wait()
    r_load.wait()

    def norm_first(i):
        at = chunk(i, size)
        grad = dh_ref[at, :]
        z = z1_ref[at, :]
        dh = norm_back(grad, z, r1_ref[at, 0:1], vector(vec_ref, FIRST_GAIN))
        dh_ref[at, :] = dh
        b_ref[at, :] = dh.astype(BF)
        sums_ref[0:1, :] += total_rows(grad * z)
        sums_ref[1:2, :] += total_rows(grad)
        sums_ref[2:3, :] += total_rows(dh)

    loop(rows // size, norm_first)
    mixed_load.wait()
    give(4, b_ref, mixed_ref)
    weight(3, 0).wait()
    dm = 3

    def mix_back(z):
        pool[dm, :, chunk(z, cols)] = dot_nn(b_ref[...], weight_tile(wbuf, 0, z)).astype(BF)

    loop(parts, mix_back)
    weight(2, 0).start()
    weight(0, 1).start()
    advances(2)
    hold(4, b_ref, mixed_ref)
    y_load.wait()

    qkv_load.wait()
    other_load.wait()

    def swap(pair):
        lanes = chunk(pair, 2 * HD)
        return remote(
            far_ref.at[lax.rem(pair, 4)],
            swap_ref.at[:, :, lanes],
            swap_send.at[pair],
            swap_recv.at[pair],
            {"dp": cube.place ^ 1, "tensor": cube.z},
        )

    def attend(pair):
        lanes = chunk(pair, 2 * HD)
        fetch(pair).wait()
        slot = lax.rem(pair, 2)
        q2, dm2 = pool[0, :, lanes], pool[dm, :, lanes]
        k2 = [pool[1, :, lanes], pool[8, :, lanes]]
        v2 = [pool[2, :, lanes], pool[9, :, lanes]]
        weighed = (dm2.astype(F32) * mixed_ref[:, lanes].astype(F32)).T
        dqs, dks, dvs = [], [[], []], [[], []]
        for head in range(2):
            part = slice(head * HD, head * HD + HD)
            q, dmix = q2[:, part], dm2[:, part]
            chance = [chance_ref[slot, head, i * rows : (i + 1) * rows, :] for i in range(2)]
            grads = [dot_nt(v[:, part], dmix) for v in v2]
            inner = total_rows(weighed[part, :])
            dq = None
            for i in range(2):
                ds = (chance[i].astype(F32) * (grads[i] - inner)).astype(BF)
                term = dot_tn(k2[i][:, part], ds)
                dq = term if dq is None else dq + term
                dks[i].append(dot_nn(ds, q))
                dvs[i].append(dot_nn(chance[i], dmix))
            dqs.append(dq)
        dq = jnp.concatenate(dqs, axis=0).T.astype(BF).astype(F32) * SCALE
        mixed_ref[:, lanes] = dq.astype(BF)
        sums_ref[10:11, lanes] = total_rows(dq)
        near_ref[0, :, lanes] = jnp.concatenate(dks[0], axis=1).astype(BF)
        near_ref[1, :, lanes] = jnp.concatenate(dvs[0], axis=1).astype(BF)

        @pl.when(pair >= 4)
        def _():
            swap(pair - 4).wait_send()

        far_ref[lax.rem(pair, 4), 0] = jnp.concatenate(dks[1], axis=1).astype(BF)
        far_ref[lax.rem(pair, 4), 1] = jnp.concatenate(dvs[1], axis=1).astype(BF)
        swap(pair).start()

        @pl.when(pair + 2 < pairs)
        def _():
            fetch(pair + 2).start()

    back_out.back_end(near_ref, 1, outputs_ref)
    loop(2, attend)
    give(5, y_ref, pool.at[4])
    advances(3)
    hold(5, y_ref, pool.at[4])
    loop(2, lambda i: attend(2 + i))
    give(6, y_ref, pool.at[5])
    advances(4)
    hold(6, y_ref, pool.at[5])
    loop(2, lambda i: attend(4 + i))
    give(7, y_ref, pool.at[6])
    advances(5)
    hold(7, y_ref, pool.at[6])
    loop(pairs - 6, lambda i: attend(6 + i))
    give(8, y_ref, pool.at[7])
    advances(6)
    hold(8, y_ref, pool.at[7])
    x_load.start()

    def both(pair):
        swap(pair).wait_recv()
        lanes = chunk(pair, 2 * HD)
        for i in range(2):
            total = near_ref[i, :, lanes].astype(F32) + swap_ref[i, :, lanes].astype(F32)
            low = total.astype(BF)
            near_ref[i, :, lanes] = low
            if i == 1:
                sums_ref[11:12, lanes] = total_rows(low.astype(F32))

    loop(pairs, both)
    x_load.wait()
    give(9, y_ref, mixed_ref)

    value = sums_ref[0:8, :]
    thirds = []
    for _ in range(3):
        thirds.append(value.astype(BF))
        value = value - thirds[-1].astype(F32)
    value = dot_nt(jnp.concatenate(thirds, axis=0), cube.shuffle(width))
    sums_ref[0:6, :] = (value[0:8] + value[8:16] + value[16:24])[0:6, :]

    rounds = [{"dp": p, "tensor": cube.z} for p in partners]
    rounds += [{"dp": cube.place, "tensor": cube.z ^ 1}, {"dp": cube.place, "tensor": cube.z ^ 2}]

    def pool_sums(i):
        return remote(sums_ref, sums_in.at[i], sum_send.at[i], sum_recv.at[i], rounds[i])

    def next_sum(i):
        if 0 < i <= len(rounds):
            pool_sums(i - 1).wait()
            sums_ref[...] += sums_in[i - 1]
        if i < len(rounds):
            pool_sums(i).start()

    next_sum(0)

    def fold_in(kind, slot, right):
        weight(kind, slot).wait()

        def part(z):
            value = dot_nt(right[:, chunk(z, cols)], weight_tile(wbuf, slot, z))
            dh_ref[...] += value

        loop(parts, part)

    fold_in(2, 0, mixed_ref)
    weight(1, 0).start()
    fold_in(0, 1, near_ref.at[0])
    next_sum(1)
    fold_in(1, 0, near_ref.at[1])
    loop(4, lambda i: swap(pairs - 4 + i).wait_send())
    pool[0] = dot_nt(dh_ref[...].astype(BF), cube.shuffle(width)).astype(BF)

    def send_in(piece):
        back_in.back(pool, 0, back_ref, piece, pieces)

    loop(2, send_in)
    next_sum(2)
    advances(7)
    give(10, y_ref, near_ref.at[1])
    hold(9, y_ref, mixed_ref)
    next_sum(3)
    loop(2, lambda i: send_in(2 + i))
    give(11, y_ref, near_ref.at[0])
    hold(10, y_ref, near_ref.at[1])
    next_sum(4)
    loop(2, lambda i: send_in(4 + i))
    advances(8)
    hold(11, y_ref, near_ref.at[0])
    loop(2, lambda i: send_in(6 + i))
    advances(9)
    for i in range(5, len(rounds) + 1):
        next_sum(i)
    advances(10)
    advances(11)
    advances(12)
    sums_out[...] = sums_ref[...]
    advances(SUBS + top + 2)

    for r in range(SUBS - RING, SUBS):
        stage(r, top).wait_send()
    back_in.back_end(pool, 0, back_ref)
    back_in.back_wait(pool, 0, back_ref)
    back_out.back_wait(near_ref, 1, outputs_ref)


def backward(second_sums, held, count, parts):
    (weights, vectors, x, qkv, other, mixed, chance, z1, r1, y1, gated, slope, normed_rows, dh2, b2) = held
    subs, _, _, depth, cols = weights.shape
    rows, width = x.shape
    levels = count.bit_length() - 1
    half = count // 2
    pairs = width // (2 * HD)
    dma = pltpu.SemaphoreType.DMA
    low = lambda *shape: (shape, BF)
    high = lambda *shape: (shape, F32)
    hbm = pl.BlockSpec(memory_space=pl.ANY)
    vmem = pl.BlockSpec(memory_space=pltpu.VMEM)
    results = [
        high(subs, depth, cols),
        high(16, width),
        low(2, rows // 2, width),
        low(2, rows // 2, width),
    ]
    scratch = [
        low(10, rows, width),
        low(2, 2, 2 * rows, rows),
        low(rows, width),
        high(rows, width),
        high(rows, width),
        high(rows, 128),
        low(rows, width),
        low(rows, width),
        low(2, rows, width),
        low(4, 2, rows, 2 * HD),
        low(2, rows, width),
        low(2, count, parts, depth, cols),
        low(RING, half, parts, depth, cols),
        low(RING, half, parts, depth, cols),
        low(HELD, half, parts, depth, cols),
        low(LINE, parts, depth, cols),
        low(subs, half - 1, parts, depth, cols),
        low(subs, parts + 1, depth, cols),
        high(16, width),
        high(levels + 2, 16, width),
    ]
    return pl.pallas_call(
        functools.partial(backward_kernel, count, parts),
        in_specs=[vmem, vmem] + [hbm] * 14,
        out_specs=[vmem, vmem, hbm, hbm],
        out_shape=[jax.ShapeDtypeStruct(*r) for r in results],
        scratch_shapes=[pltpu.VMEM(*s) for s in scratch]
        + [
            dma((15,)),
            dma((2,)),
            dma((2,)),
            pltpu.SemaphoreType.REGULAR,
            dma((subs, levels)),
            dma((subs, levels)),
            dma((subs, 3)),
            dma((subs, 3)),
            dma((pairs,)),
            dma((pairs,)),
            dma((2, 2)),
            dma((2, 2)),
            dma((2,)),
            dma((levels + 2,)),
            dma((levels + 2,)),
        ],
        compiler_params=pltpu.CompilerParams(
            collective_id=2, has_side_effects=True, vmem_limit_bytes=62 * MIB
        ),
    )(vectors, second_sums, weights, x, qkv, other, mixed, chance, z1, r1, y1, gated, slope, normed_rows, dh2, b2)


def result_kernel(
    rows_ref,
    back_ref,
    down_ref,
    up_ref,
    q_ref,
    k_ref,
    v_ref,
    o_ref,
    sums_ref,
    rows_out,
    input_out,
    down_out,
    up_out,
    q_out,
    k_out,
    v_out,
    o_out,
    *small,
):
    rows_out[...] = rows_ref[...]
    input_out[...] = back_ref[...].astype(F32)
    down_out[...] = down_ref[0].T
    up_out[...] = up_ref[0]

    @pl.when(pl.program_id(0) == 0)
    def _():
        for source, target in ((q_ref, q_out), (k_ref, k_out), (v_ref, v_out)):
            target[...] = source[0]
        o_out[...] = o_ref[0].T
        for i in range(6):
            small[i][...] = sums_ref[i : i + 1, :]
        cols = small[7].shape[1]
        mine = chunk(lax.axis_index("tensor"), cols)
        small[7][...] = sums_ref[10:11, mine]
        small[8][...] = sums_ref[11:12, mine]
        for i in range(4):
            small[6][:, i * cols : (i + 1) * cols] = sums_ref[6 + i : 7 + i, mine]


def results(grads, sums, outputs, back):
    _, depth, cols = grads.shape
    _, rows, width = outputs.shape
    steps = 4
    at = {sub: r for r, sub in enumerate(ORDER)}
    row_spec = pl.BlockSpec((2, rows // steps, width), lambda j: (0, j, 0))
    one = lambda r: pl.BlockSpec((1, depth, cols), lambda j: (r, 0, 0))
    run = lambda r: pl.BlockSpec((1, depth, cols), lambda j: (r + j, 0, 0))
    whole = lambda *shape: pl.BlockSpec(shape, lambda j: (0,) * len(shape))
    high = lambda *shape: jax.ShapeDtypeStruct(shape, F32)
    return pl.pallas_call(
        result_kernel,
        grid=(steps,),
        in_specs=[row_spec, row_spec, run(at[DOWN]), run(at[UP])]
        + [one(at[2]), one(at[0]), one(at[1]), one(at[3]), whole(*sums.shape)],
        out_specs=[
            row_spec,
            row_spec,
            pl.BlockSpec((cols, depth), lambda j: (j, 0)),
            pl.BlockSpec((depth, cols), lambda j: (0, j)),
        ]
        + [whole(depth, cols)] * 3
        + [whole(cols, depth)]
        + [whole(1, width)] * 6
        + [whole(1, 4 * cols), whole(1, cols), whole(1, cols)],
        out_shape=[
            jax.ShapeDtypeStruct(outputs.shape, BF),
            high(*outputs.shape),
            high(4 * cols, depth),
            high(depth, 4 * cols),
        ]
        + [high(depth, cols)] * 3
        + [high(cols, depth)]
        + [high(1, width)] * 6
        + [high(1, 4 * cols), high(1, cols), high(1, cols)],
        compiler_params=pltpu.CompilerParams(vmem_limit_bytes=60 * MIB),
    )(outputs, back, grads, grads, grads, grads, grads, grads, sums)


def shards(
    inputs,
    query_weight,
    query_bias,
    key_weight,
    value_weight,
    value_bias,
    out_weight,
    out_bias,
    first_gain,
    first_shift,
    up_weight,
    up_bias,
    down_weight,
    down_bias,
    second_gain,
    second_shift,
    cotangent,
):
    count, parts = lax.axis_size("dp"), lax.axis_size("tensor")
    flat = lambda *values: [value.reshape(1, -1) for value in values]
    *held, second_sums = forward(
        [query_weight, key_weight, value_weight, out_weight, up_weight, down_weight],
        flat(query_bias, value_bias, up_bias),
        flat(out_bias, first_gain, first_shift, down_bias, second_gain, second_shift),
        inputs,
        cotangent,
        count,
        parts,
    )
    grads, sums, outputs, back = backward(second_sums, held, count, parts)
    outputs, input_grad, down, up, query, key, value, out, *small = results(grads, sums, outputs, back)
    small = [row.reshape(-1) for row in small]
    return (
        outputs,
        input_grad,
        query,
        small[7],
        key,
        value,
        small[8],
        out,
        small[2],
        small[0],
        small[1],
        up,
        small[6],
        down,
        small[5],
        small[3],
        small[4],
    )


def solution(mesh):
    rows = P(None, ("dp", "tensor"), None)
    return jax.shard_map(
        shards,
        mesh=mesh,
        in_specs=(
            rows,
            P("dp", "tensor"),
            P("tensor"),
            P("dp", "tensor"),
            P("dp", "tensor"),
            P("tensor"),
            P("tensor", "dp"),
            P(),
            P(),
            P(),
            P("dp", "tensor"),
            P("tensor"),
            P("tensor", "dp"),
            P(),
            P(),
            P(),
            rows,
        ),
        out_specs=(
            rows,
            rows,
            P("dp", "tensor"),
            P("tensor"),
            P("dp", "tensor"),
            P("dp", "tensor"),
            P("tensor"),
            P("tensor", "dp"),
            P(),
            P(),
            P(),
            P("dp", "tensor"),
            P("tensor"),
            P("tensor", "dp"),
            P(),
            P(),
            P(),
        ),
        check_vma=False,
    )
```

```python
import functools
import math

import jax
import jax.numpy as jnp
from jax import lax
from jax.experimental import pallas as pl
from jax.experimental.pallas import tpu as pltpu
from jax.sharding import PartitionSpec as P

HD = 64
LEN = 1024
EPSILON = 1e-05
SCALE = HD ** (-0.5)
LOG2E = math.log2(math.e)
BF = jnp.bfloat16
F32 = jnp.float32
MIB = 1 << 20


def dot_nn(left, right):
    return jnp.dot(left, right, preferred_element_type=F32)


def dot_nt(left, right):
    return lax.dot_general(left, right, (((1,), (1,)), ((), ())), preferred_element_type=F32)


def dot_tn(left, right):
    return lax.dot_general(left, right, (((0,), (0,)), ((), ())), preferred_element_type=F32)


OUT_BIAS, FIRST_GAIN, FIRST_SHIFT, DOWN_BIAS, SECOND_GAIN, SECOND_SHIFT = range(6)


def vector(ref, place):
    return ref[place : place + 1, :]


def normed(hidden):
    average = jnp.mean(hidden, axis=-1, keepdims=True)
    center = hidden - average
    spread = jnp.mean(center * center, axis=-1, keepdims=True)
    inverse = lax.rsqrt(spread + EPSILON)
    return center * inverse, inverse


def norm_back(grad, z, inverse, gain):
    scaled = grad * gain
    average = jnp.mean(scaled, axis=-1, keepdims=True)
    along = jnp.mean(scaled * z, axis=-1, keepdims=True)
    return (scaled - average - z * along) * inverse


def total_rows(value):
    return jnp.sum(value, axis=0, keepdims=True)


def remote(source, target, send, receive, device):
    return pltpu.make_async_remote_copy(
        source, target, send, receive, device_id=device, device_id_type=pl.DeviceIdType.MESH
    )


def greet(devices):
    barrier = pltpu.get_barrier_semaphore()
    for device in devices:
        pl.semaphore_signal(barrier, 1, device_id=device, device_id_type=pl.DeviceIdType.MESH)
    pl.semaphore_wait(barrier, len(devices))


class Cube:
    def __init__(self, count, parts):
        self.count, self.parts, self.half = count, parts, parts // 2
        self.place, self.z = lax.axis_index("dp"), lax.axis_index("tensor")
        self.core = lax.rem(self.place, 2)
        self.levels = count.bit_length() - 1
        bits = [1 << i for i in range(1, self.levels)]
        self.orders = [bits, bits[::-1]]

    def stages(self):
        ups, downs = self.orders
        out = []
        for up, down in zip(ups, downs):
            out.append(self.place ^ jnp.where(self.core == 0, up, down))
        return out + [self.place ^ 1]

    def masks(self):
        table = []
        for order in self.orders:
            held = [0]
            for bit in order:
                held = held + [m ^ bit for m in held]
            table.append(held)
        return [a + [m ^ 1 for m in b] for a, b in (table, table[::-1])]

    def column(self):
        mine = [{"dp": self.place, "tensor": lax.rem(self.z + d, self.parts)} for d in range(1, self.parts)]
        others = [{"dp": self.place ^ 1, "tensor": lax.rem(self.z + d, self.parts)} for d in range(self.parts)]
        return mine + others

    def neighbours(self):
        return [{"dp": p, "tensor": self.z} for p in self.stages()[:-1]]

    def shuffle(self, width):
        depth = width // self.count
        column = lax.broadcasted_iota(jnp.int32, (1, width), 1)
        slot = column // depth
        far = slot // (self.count // 2)
        flips = far
        for level, (up, down) in enumerate(zip(*self.orders)):
            bit = jnp.where(self.core == 0, up, down)
            other = jnp.where(self.core == 0, down, up)
            held = lax.rem(slot // (1 << level), 2)
            flips = flips + held * jnp.where(far == 0, bit, other)
        owner = self.place ^ flips
        source = owner * depth + lax.rem(column, depth)
        row = lax.broadcasted_iota(jnp.int32, (width, width), 0)
        return (row == source).astype(F32).astype(BF)


class Rows:
    def __init__(self, cube, send, receive, here):
        self.cube, self.send, self.receive, self.here = cube, send, receive, here
        c = cube
        self.slot = lax.rem(c.z, c.half)
        self.targets = [(c.place - c.core + c.z // c.half, m * c.half + c.core) for m in range(2)]
        self.micro = c.z // c.half
        self.sources = [(c.place - c.core + lax.rem(c.z, c.half), c.half * c.core + p) for p in range(2)]

    def own(self, device):
        return jnp.logical_and(device[0] == self.cube.place, device[1] == self.cube.z)

    def at(self, device):
        return {"dp": device[0], "tensor": device[1]}

    def into(self, source, target, piece, pieces):
        size = source.shape[1] // pieces
        at = pl.ds(pl.multiple_of(piece * size, size), size)
        for m, device in enumerate(self.targets):
            own = self.own(device)

            @pl.when(own)
            def _(m=m):
                pltpu.make_async_copy(source.at[m, at], target.at[self.slot, at], self.here).start()

            @pl.when(jnp.logical_not(own))
            def _(m=m, device=device):
                remote(
                    source.at[m, at],
                    target.at[self.slot, at],
                    self.send.at[m],
                    self.receive.at[self.slot],
                    self.at(device),
                ).start()

    def into_wait(self, source, target):
        for p, device in enumerate(self.sources):
            own = self.own(device)

            @pl.when(own)
            def _(p=p):
                pltpu.make_async_copy(source.at[0], target.at[p], self.here).wait()

            @pl.when(jnp.logical_not(own))
            def _(p=p, device=device):
                remote(
                    source.at[0], target.at[p], self.send.at[0], self.receive.at[p], self.at(device)
                ).wait_recv()

    def into_end(self, source, target):
        for m, device in enumerate(self.targets):

            @pl.when(jnp.logical_not(self.own(device)))
            def _(m=m, device=device):
                remote(
                    source.at[m], target.at[self.slot], self.send.at[m], self.receive.at[0], self.at(device)
                ).wait_send()


    def back(self, source, lead, target, piece, pieces):
        size = target.shape[1] // pieces
        for p, device in enumerate(self.sources):
            own = self.own(device)
            here = pl.ds(pl.multiple_of(p * target.shape[1] + piece * size, size), size)
            there = pl.ds(pl.multiple_of(piece * size, size), size)

            @pl.when(own)
            def _(here=here, there=there):
                pltpu.make_async_copy(
                    source.at[lead, here], target.at[self.micro, there], self.here
                ).start()

            @pl.when(jnp.logical_not(own))
            def _(p=p, device=device, here=here, there=there):
                remote(
                    source.at[lead, here],
                    target.at[self.micro, there],
                    self.send.at[p],
                    self.receive.at[self.micro],
                    self.at(device),
                ).start()

    def back_wait(self, source, lead, target):
        rows = target.shape[1]
        for m, device in enumerate(self.targets):

            @pl.when(jnp.logical_not(self.own(device)))
            def _(m=m, device=device):
                remote(
                    source.at[lead, pl.ds(0, rows)],
                    target.at[m],
                    self.send.at[0],
                    self.receive.at[m],
                    self.at(device),
                ).wait_recv()

    def back_end(self, source, lead, target):
        rows = target.shape[1]
        for p, device in enumerate(self.sources):
            own = self.own(device)

            @pl.when(own)
            def _(p=p):
                pltpu.make_async_copy(
                    source.at[lead, pl.ds(p * rows, rows)], target.at[self.micro], self.here
                ).wait()

            @pl.when(jnp.logical_not(own))
            def _(p=p, device=device):
                remote(
                    source.at[lead, pl.ds(p * rows, rows)],
                    target.at[self.micro],
                    self.send.at[p],
                    self.receive.at[0],
                    self.at(device),
                ).wait_send()


SUBS, UP, DOWN = 12, 4, 8
XS, XP, CS, CP, LEAD = 0, 4, 4, 8, 0
PACE = [4, 5, 6, 7, 7, 8, 9, 10, 11, 12, 13, 13]


def loop(count, body):
    lax.fori_loop(0, count, lambda i, _: (body(i), None)[1], None)


def chunk(i, size):
    return pl.ds(pl.multiple_of(i * size, size), size)


def weight_tile(ref, slot, z):
    value = ref[slot, :, z]
    return value.reshape(-1, value.shape[-1])


def forward_kernel(
    count,
    parts,
    q_in,
    k_in,
    v_in,
    o_in,
    up_in,
    down_in,
    q_bias,
    v_bias,
    up_bias,
    vec0,
    vec1,
    vec2,
    vec3,
    vec4,
    vec5,
    in_ref,
    cot_ref,
    weights_ref,
    vec_out,
    x_out,
    qkv_out,
    other_out,
    mixed_out,
    chance_out,
    z1_out,
    r1_out,
    y1_out,
    gated_out,
    slope_out,
    normed_out,
    dh2_out,
    b2_out,
    sums_out,
    local_ref,
    o_raw,
    down_raw,
    bias_ref,
    vec_ref,
    raw_ref,
    cot_raw,
    shuffle_ref,
    x_ref,
    c_ref,
    bias_all,
    qkv_ref,
    other_ref,
    mixed_ref,
    chance_ref,
    z1_ref,
    r1_ref,
    y1_ref,
    gated_ref,
    slope_ref,
    acc_ref,
    normed_ref,
    dh2_ref,
    b2_ref,
    sums_ref,
    wbuf,
    prep_sem,
    local_sem,
    zs,
    zr,
    ss,
    sr,
    wsem,
    bias_send,
    bias_recv,
    row_send,
    row_recv,
    row_here,
    kv_send,
    kv_recv,
    out_sem,
    save_sem,
    last_sem,
):
    cube = Cube(count, parts)
    partners, levels = cube.stages(), cube.levels
    shifts = [lax.rem(cube.z + d, parts) for d in range(1, parts)]
    ahead = 5
    rows = x_ref.shape[0]
    cols = weights_ref.shape[-1]
    depth = weights_ref.shape[-2]
    sources = [k_in, v_in, q_in] + [up_in.at[:, i * cols : (i + 1) * cols] for i in range(4)]
    places = [local_ref.at[i] for i in (0, 1, 2, 4, 5, 6, 7)]
    prep = [
        pltpu.make_async_copy(source, place, prep_sem.at[i])
        for i, (source, place) in enumerate(zip(sources + [o_in, down_in], places + [o_raw, down_raw]))
    ]
    for copy in prep:
        copy.start()
    bias_ref[...] = jnp.zeros_like(bias_ref)
    bias_ref[0:1, :] = q_bias[...]
    bias_ref[1:2, :] = v_bias[...]
    for i in range(4):
        bias_ref[2 + i : 3 + i, :] = up_bias[:, i * cols : (i + 1) * cols]
    same = lax.broadcasted_iota(jnp.int32, (depth, depth), 0) == lax.broadcasted_iota(
        jnp.int32, (depth, depth), 1
    )
    eye = same.astype(F32).astype(BF)
    greet(cube.column() + cube.neighbours())
    for i in range(3):
        prep[i].wait()

    def own(sub):
        return pltpu.make_async_copy(local_ref.at[sub], weights_ref.at[sub, 0, cube.z], local_sem.at[sub])

    inner = jnp.logical_or(cube.z == 1, cube.z == 2)
    mine, theirs = cube.z // 2 * 2, 2 - cube.z // 2 * 2

    def along(sub, hop):
        if hop == 0:
            source, target, z = local_ref.at[sub], weights_ref.at[sub, 0, cube.z], cube.z ^ 1
        else:
            source = weights_ref.at[sub, 0, pl.ds(mine if hop == 1 else theirs, 2)]
            target, z = source, (3 - cube.z if hop == 1 else cube.z ^ 1)
        return remote(
            source, target, zs.at[sub, hop], zr.at[sub, hop], {"dp": cube.place, "tensor": z}
        )

    def stage(sub, level):
        size = 1 << level
        return remote(
            weights_ref.at[sub, pl.ds(0, size)],
            weights_ref.at[sub, pl.ds(size, size)],
            ss.at[sub, level],
            sr.at[sub, level],
            {"dp": partners[level], "tensor": cube.z},
        )

    def begin(sub):
        own(sub).start()
        along(sub, 0).start()

    def pass_pair(sub):
        own(sub).wait()
        along(sub, 0).wait_recv()

        @pl.when(inner)
        def _():
            along(sub, 1).start()

    def pass_on(sub):
        @pl.when(inner)
        def _():
            along(sub, 1).wait_recv()
            along(sub, 2).start()

    def first_stage(sub):
        @pl.when(jnp.logical_not(inner))
        def _():
            along(sub, 2).wait_recv()

        stage(sub, 0).start()

    def prepare(sub):
        @pl.when(sub + 1 < SUBS)
        def _():
            pass_on(sub + 1)

        @pl.when(sub + 2 < SUBS)
        def _():
            pass_pair(sub + 2)

        @pl.when(sub + ahead < SUBS)
        def _():
            begin(sub + ahead)

    def relay(step):
        @pl.when(step < SUBS)
        def _():
            first_stage(step)

        for level in range(levels):
            sub = step - level - 1

            @pl.when(jnp.logical_and(sub >= 0, sub < SUBS))
            def _(sub=sub, level=level):
                stage(sub, level).wait_recv()
                if level + 1 < levels:
                    stage(sub, level + 1).start()

        @pl.when(jnp.logical_and(step >= XS, step < XS + XP))
        def _():
            rows_x.into(in_ref, raw_ref, step - XS, XP)

        @pl.when(jnp.logical_and(step >= CS, step < CS + CP))
        def _():
            rows_c.into(cot_ref, cot_raw, step - CS, CP)

        @pl.when(step < LEAD)
        def _():
            prepare(2 * step)
            prepare(2 * step + 1)

        @pl.when(step >= LEAD)
        def _():
            prepare(step + LEAD)

    done = [0]

    def relays(last):
        if last > done[0]:
            first = done[0]
            loop(last - first, lambda i: relay(first + i))
            done[0] = last

    def load(sub):
        return pltpu.make_async_copy(weights_ref.at[sub], wbuf.at[sub % 4], wsem.at[sub % 4])

    def share_bias(d):
        return remote(
            bias_ref,
            bias_all.at[cube.z],
            bias_send.at[d],
            bias_recv.at[d],
            {"dp": cube.place, "tensor": shifts[d]},
        )

    rows_x = Rows(cube, row_send.at[0], row_recv.at[0], row_here.at[0])
    rows_c = Rows(cube, row_send.at[1], row_recv.at[1], row_here.at[1])
    outs = []

    def keep(source, target):
        copy = pltpu.make_async_copy(source, target, out_sem.at[len(outs)])
        copy.start()
        outs.append(copy)

    loop(3, begin)
    for copy in prep[3:]:
        copy.wait()
    local_ref[3] = dot_nt(eye, o_raw[...]).astype(BF)
    loop(ahead - 3, lambda i: begin(3 + i))
    for i in range(4):
        local_ref[DOWN + i] = dot_nt(eye, down_raw[i * cols : (i + 1) * cols, :]).astype(BF)
    for d in range(parts - 1):
        share_bias(d).start()
    pass_pair(0)
    pass_pair(1)
    pass_on(0)
    shuffle_ref[...] = cube.shuffle(x_ref.shape[1])
    bias_all[cube.z] = bias_ref[...]
    value = jnp.concatenate([v[...] for v in (vec0, vec1, vec2, vec3, vec4, vec5)] + [vec0[...]] * 2, axis=0)
    thirds = []
    for _ in range(3):
        thirds.append(value.astype(BF))
        value = value - thirds[-1].astype(F32)
    value = dot_nn(jnp.concatenate(thirds, axis=0), shuffle_ref[...])
    vec_ref[...] = value[0:8] + value[8:16] + value[16:24]
    keep(vec_ref, vec_out)
    relays(levels + 1)
    load(0).start()
    rows_x.into_wait(in_ref, raw_ref)
    half_rows = raw_ref.shape[1]
    for p in range(2):
        x_ref[p * half_rows : (p + 1) * half_rows, :] = dot_nn(raw_ref[p], shuffle_ref[...]).astype(BF)
    for d in range(parts - 1):
        share_bias(d).wait_recv()
    relays(max(PACE[0], levels + 2))
    load(1).start()

    def swap(kind):
        return remote(
            qkv_ref.at[kind],
            other_ref.at[kind - 1],
            kv_send.at[kind - 1],
            kv_recv.at[kind - 1],
            {"dp": cube.place ^ 1, "tensor": cube.z},
        )

    for sub, kind in enumerate((1, 2, 0)):
        load(sub).wait()

        def project(z, sub=sub, kind=kind):
            acc = dot_nn(x_ref[...], weight_tile(wbuf, sub, z))
            if kind == 0:
                acc = (acc + bias_all[z, 0:1, :]) * SCALE
            elif kind == 2:
                acc = acc + bias_all[z, 1:2, :]
            qkv_ref[kind, :, chunk(z, cols)] = acc.astype(BF)

        loop(parts, project)
        if kind > 0:
            swap(kind).start()
        if sub == 0:
            relays(max(PACE[1], levels + 3))
            load(2).start()
        elif sub == 1:
            relays(PACE[2])

    keep(x_ref, x_out)
    keep(qkv_ref, qkv_out)
    relays(max(PACE[3], levels + 4))
    load(3).start()
    for kind in (1, 2):
        swap(kind).wait_recv()
    keep(other_ref, other_out)

    def save(pair):
        slot = lax.rem(pair, 2)
        return pltpu.make_async_copy(chance_ref.at[slot], chance_out.at[pair], save_sem.at[slot])

    def attend(pair):
        lanes = chunk(pair, 2 * HD)
        q2 = qkv_ref[0, :, lanes]
        k2 = [qkv_ref[1, :, lanes], other_ref[0, :, lanes]]
        v2 = [qkv_ref[2, :, lanes], other_ref[1, :, lanes]]
        mixed = []
        slot = lax.rem(pair, 2)

        @pl.when(pair >= 2)
        def _():
            save(pair - 2).wait()

        for head in range(2):
            part = slice(head * HD, head * HD + HD)
            scores = [dot_nt(k[:, part], q2[:, part]) for k in k2]
            top = functools.reduce(jnp.maximum, [jnp.max(s, axis=0, keepdims=True) for s in scores])
            base = top * LOG2E
            expo = [jnp.exp2(s * LOG2E - base) for s in scores]
            total = functools.reduce(jnp.add, [jnp.sum(e, axis=0, keepdims=True) for e in expo])
            inverse = 1.0 / total
            chance = [(e * inverse).astype(BF) for e in expo]
            mixed.append(functools.reduce(jnp.add, [dot_tn(v[:, part], c) for c, v in zip(chance, v2)]))
            for i in range(2):
                chance_ref[slot, head, i * rows : (i + 1) * rows, :] = chance[i]
        mixed_ref[:, lanes] = jnp.concatenate(mixed, axis=0).T.astype(BF)
        save(pair).start()

    pairs = mixed_ref.shape[1] // (2 * HD)
    loop(2, attend)
    relays(PACE[4])
    loop(2, lambda i: attend(2 + i))
    relays(PACE[5])
    loop(2, lambda i: attend(4 + i))
    relays(PACE[6])
    loop(pairs - 6, lambda i: attend(6 + i))
    relays(max(PACE[7], levels + 6))
    keep(mixed_ref, mixed_out)
    loop(2, lambda i: save(pairs - 2 + i).wait())

    load(4).start()
    load(5).start()
    load(3).wait()

    def mix(z):
        value = dot_nt(mixed_ref[:, chunk(z, cols)], weight_tile(wbuf, 3, z))

        @pl.when(z == 0)
        def _():
            acc_ref[...] = value

        @pl.when(z > 0)
        def _():
            acc_ref[...] += value

    loop(parts, mix)
    size = 128

    def norm_first(i):
        at = chunk(i, size)
        hidden = x_ref[at, :].astype(F32) + acc_ref[at, :] + vector(vec_ref, OUT_BIAS)
        z, inverse = normed(hidden)
        z1_ref[at, :] = z
        r1_ref[at, :] = jnp.broadcast_to(inverse, (size, 128))
        y = z * vector(vec_ref, FIRST_GAIN) + vector(vec_ref, FIRST_SHIFT)
        y1_ref[at, :] = y.astype(BF)
        acc_ref[at, :] = y + vector(vec_ref, DOWN_BIAS)

    loop(rows // size, norm_first)
    keep(z1_ref, z1_out)
    keep(r1_ref, r1_out)
    keep(y1_ref, y1_out)

    def gate(sub):
        load(sub).wait()

        def part(z):
            lanes = chunk(z, cols)
            upper = dot_nn(y1_ref[...], weight_tile(wbuf, sub % 4, z)) + bias_all[z, sub - UP + 2 : sub - UP + 3, :]
            half = 0.5 + 0.5 * lax.erf(upper * (0.5**0.5))
            gated_ref[sub - UP, :, lanes] = (upper * half).astype(BF)
            bell = jnp.exp(upper * upper * -0.5) * ((2 * math.pi) ** -0.5)
            slope_ref[sub - UP, :, lanes] = (half + upper * bell).astype(BF)

        loop(parts, part)
        keep(gated_ref.at[sub - UP], gated_out.at[sub - UP])
        keep(slope_ref.at[sub - UP], slope_out.at[sub - UP])

    for sub in range(UP, DOWN):
        gate(sub)
        relays(max(PACE[8 + sub - UP], sub + 2 + levels + 1))
        load(sub + 2).start()

    rows_c.into_wait(cot_ref, cot_raw)
    for p in range(2):
        c_ref[p * half_rows : (p + 1) * half_rows, :] = dot_nn(cot_raw[p], shuffle_ref[...]).astype(BF)

    for sub in range(DOWN, SUBS):
        if sub == DOWN:
            relays(DOWN + 2 + levels + 1)
            load(DOWN + 2).start()
        elif sub == SUBS - 1:
            relays(SUBS + levels)
            load(sub).start()
        load(sub).wait()

        def fold(z, sub=sub):
            acc_ref[...] += dot_nt(gated_ref[sub - DOWN, :, chunk(z, cols)], weight_tile(wbuf, sub % 4, z))

        loop(parts, fold)

    sums_ref[...] = jnp.zeros_like(sums_ref)
    last = [(normed_ref, normed_out), (dh2_ref, dh2_out), (b2_ref, b2_out)]

    def norm_second(i):
        at = chunk(i, size)
        z, inverse = normed(acc_ref[at, :])
        gain = vector(vec_ref, SECOND_GAIN)
        normed_ref[at, :] = (z * gain + vector(vec_ref, SECOND_SHIFT)).astype(BF)
        grad = c_ref[at, :].astype(F32)
        dh = norm_back(grad, z, inverse, gain)
        dh2_ref[at, :] = dh
        b2_ref[at, :] = dh.astype(BF)
        for n, (source, target) in enumerate(last):
            pltpu.make_async_copy(source.at[at], target.at[at], last_sem.at[n]).start()
        sums_ref[0:1, :] += total_rows(grad * z)
        sums_ref[1:2, :] += total_rows(grad)
        sums_ref[2:3, :] += total_rows(dh)

    loop(rows // size, norm_second)
    keep(sums_ref, sums_out)

    def sent(sub):
        along(sub, 0).wait_send()

        @pl.when(inner)
        def _():
            along(sub, 1).wait_send()
            along(sub, 2).wait_send()

        for level in range(levels):
            stage(sub, level).wait_send()

    loop(SUBS, sent)
    for d in range(parts - 1):
        share_bias(d).wait_send()
    for kind in (1, 2):
        swap(kind).wait_send()
    rows_x.into_end(in_ref, raw_ref)
    rows_c.into_end(cot_ref, cot_raw)
    for copy in outs:
        copy.wait()
    for n, (source, target) in enumerate(last):
        pltpu.make_async_copy(source, target, last_sem.at[n]).wait()


def forward(weights, biases, vectors, inputs, cotangent, count, parts):
    subs = SUBS
    depth, cols = weights[0].shape
    _, half_rows, width = inputs.shape
    rows = 2 * half_rows
    levels = count.bit_length() - 1
    pairs = width // (2 * HD)
    dma = pltpu.SemaphoreType.DMA
    low = lambda *shape: (shape, BF)
    high = lambda *shape: (shape, F32)
    results = [
        low(subs, count, parts, depth, cols),
        high(8, width),
        low(rows, width),
        low(3, rows, width),
        low(2, rows, width),
        low(rows, width),
        low(pairs, 2, 2 * rows, rows),
        high(rows, width),
        high(rows, 128),
        low(rows, width),
        low(4, rows, parts * cols),
        low(4, rows, parts * cols),
        low(rows, width),
        high(rows, width),
        low(rows, width),
        high(8, width),
    ]
    scratch = [
        low(subs, depth, cols),
        low(cols, depth),
        low(4 * cols, depth),
        high(8, cols),
        high(8, width),
        low(2, half_rows, width),
        low(2, half_rows, width),
        low(width, width),
        low(rows, width),
        low(rows, width),
        high(parts, 8, cols),
        low(3, rows, width),
        low(2, rows, width),
        low(rows, width),
        low(2, 2, 2 * rows, rows),
        high(rows, width),
        high(rows, 128),
        low(rows, width),
        low(4, rows, parts * cols),
        low(4, rows, parts * cols),
        high(rows, width),
        low(rows, width),
        high(rows, width),
        low(rows, width),
        high(8, width),
        low(4, count, parts, depth, cols),
    ]
    hbm = pl.BlockSpec(memory_space=pl.ANY)
    vmem = pl.BlockSpec(memory_space=pltpu.VMEM)
    return pl.pallas_call(
        functools.partial(forward_kernel, count, parts),
        in_specs=[hbm] * 6 + [vmem] * 9 + [hbm, hbm],
        out_specs=[hbm] * len(results),
        out_shape=[jax.ShapeDtypeStruct(*r) for r in results],
        scratch_shapes=[pltpu.VMEM(*s) for s in scratch]
        + [
            dma((9,)),
            dma((subs,)),
            dma((subs, 3)),
            dma((subs, 3)),
            dma((subs, levels)),
            dma((subs, levels)),
            dma((4,)),
            dma((parts - 1,)),
            dma((parts - 1,)),
            dma((2, 2)),
            dma((2, 2)),
            dma((2,)),
            dma((2,)),
            dma((2,)),
            dma((24,)),
            dma((2,)),
            dma((3,)),
        ],
        compiler_params=pltpu.CompilerParams(
            collective_id=1, has_side_effects=True, vmem_limit_bytes=62 * MIB
        ),
    )(*weights, *biases, *vectors, inputs, cotangent)


HELD, RING, LINE = 5, 2, 4
ORDER = [8, 9, 10, 11, 3, 4, 5, 6, 7, 2, 1, 0]


def backward_kernel(
    count,
    parts,
    vec_ref,
    second_ref,
    weights_ref,
    x_in,
    qkv_in,
    other_in,
    mixed_in,
    chance_in,
    z1_in,
    r1_in,
    y1_in,
    gated_in,
    slope_in,
    normed_in,
    dh2_in,
    b2_in,
    grads_ref,
    sums_out,
    outputs_ref,
    back_ref,
    pool,
    chance_ref,
    y_ref,
    dh_ref,
    z1_ref,
    r1_ref,
    b_ref,
    mixed_ref,
    near_ref,
    far_ref,
    swap_ref,
    wbuf,
    send_ref,
    staged_ref,
    held_ref,
    line_ref,
    small_ref,
    zed_ref,
    sums_ref,
    sums_in,
    load_sem,
    fetch_sem,
    wsem,
    free_sem,
    ss,
    sr,
    zs,
    zr,
    swap_send,
    swap_recv,
    row_send,
    row_recv,
    row_here,
    sum_send,
    sum_recv,
):
    cube = Cube(count, parts)
    partners, levels = cube.stages(), cube.levels
    top = levels - 1
    half = count // 2
    shifts = [lax.rem(cube.z + d, parts) for d in range(1, parts)]
    rows, width = b_ref.shape
    cols = weights_ref.shape[-1]
    depth = weights_ref.shape[-2]
    wide = half * depth
    size = 128

    pairs = width // (2 * HD)

    def fetch(pair):
        slot = lax.rem(pair, 2)
        return pltpu.make_async_copy(chance_in.at[pair], chance_ref.at[slot], fetch_sem.at[slot])

    def load(place, source, target):
        return pltpu.make_async_copy(source, target, load_sem.at[place])

    def weight(sub, slot):
        return pltpu.make_async_copy(weights_ref.at[sub], wbuf.at[slot], wsem.at[slot])

    gate_load = [load(j % 2, gated_in.at[j], pool.at[j % 2]) for j in range(4)]
    slope_load = [load(2 + j % 2, slope_in.at[j], pool.at[2 + j % 2]) for j in range(4)]
    b_load = load(4, b2_in, b_ref)
    out_load = load(5, normed_in, near_ref.at[0])
    y_load = load(6, y1_in, y_ref)
    dh_load = load(7, dh2_in, dh_ref)
    z_load = load(8, z1_in, z1_ref)
    r_load = load(9, r1_in, r1_ref)
    mixed_load = load(10, mixed_in, mixed_ref)
    qkv_load = load(12, qkv_in, pool.at[pl.ds(0, 3)])
    other_load = load(13, other_in, pool.at[pl.ds(8, 2)])
    x_load = load(14, x_in, y_ref)

    def stage(r, level):
        if level == top:
            source, target = send_ref.at[lax.rem(r, RING)], staged_ref.at[lax.rem(r, RING)]
        else:
            source = held_ref.at[lax.rem(r, HELD), pl.ds(1 << level, 1 << level)]
            target = small_ref.at[r, pl.ds((1 << level) - 1, 1 << level)]
        return remote(
            source, target, ss.at[r, level], sr.at[r, level], {"dp": partners[level], "tensor": cube.z}
        )

    inner = jnp.logical_or(cube.z == 1, cube.z == 2)
    mine, theirs = cube.z // 2 * 2, 2 - cube.z // 2 * 2

    def along(r, hop):
        line = lax.rem(r, LINE)
        if hop == 0:
            source = line_ref.at[line, pl.ds(jnp.where(cube.z == 0, 1, 0), parts - 1)]
            target, z = zed_ref.at[r, pl.ds(0, parts - 1)], cube.z ^ 1
        elif hop == 1:
            source = line_ref.at[line, pl.ds(theirs, 2)]
            target, z = zed_ref.at[r, pl.ds(parts - 1, 2)], 3 - cube.z
        else:
            source = line_ref.at[line, cube.z ^ 1]
            target, z = zed_ref.at[r, 0], cube.z ^ 1
        return remote(source, target, zs.at[r, hop], zr.at[r, hop], {"dp": cube.place, "tensor": z})

    def add_line(r, block, place):
        line = lax.rem(r, LINE)
        value = line_ref[line, block].astype(F32) + zed_ref[r, place].astype(F32)
        line_ref[line, block] = value.astype(BF)

    def give(r, left, right):
        if r >= RING:
            stage(r - RING, top).wait_send()
        value = dot_tn(left[:, wide:], right[...]).astype(BF)
        for z in range(parts):
            send_ref[r % RING, :, z] = value[:, z * cols : (z + 1) * cols].reshape(half, depth, cols)
        if r >= RING:
            pl.semaphore_wait(free_sem, 1)
        stage(r, top).start()

    def hold(r, left, right):
        advances(r - HELD + top)
        value = dot_tn(left[:, :wide], right[...])
        stage(r, top).wait_recv()
        for z in range(parts):
            part = value[:, z * cols : (z + 1) * cols].reshape(half, depth, cols)
            part = part + staged_ref[r % RING, :, z].astype(F32)
            held_ref[r % HELD, :, z] = part.astype(BF)
        if r + RING < SUBS:
            pl.semaphore_signal(
                free_sem,
                1,
                device_id={"dp": cube.place ^ 1, "tensor": cube.z},
                device_id_type=pl.DeviceIdType.MESH,
            )
        stage(r, top - 1).start()

    def advance(k):
        for i in range(top):
            level = top - 1 - i
            r = k - i

            @pl.when(jnp.logical_and(r >= 0, r < SUBS))
            def _(r=r, level=level):
                stage(r, level).wait_recv()
                place = lax.rem(r, HELD)

                def fold(slot):
                    value = held_ref[place, slot].astype(F32)
                    value = value + small_ref[r, (1 << level) - 1 + slot].astype(F32)
                    if level > 0:
                        held_ref[place, slot] = value.astype(BF)
                    else:
                        line_ref[lax.rem(r, LINE)] = value.astype(BF)

                loop(1 << level, fold)
                if level > 0:
                    stage(r, level - 1).start()
                else:

                    @pl.when(jnp.logical_not(inner))
                    def _():
                        along(r, 0).start()

                    for other in range(top):
                        stage(r, other).wait_send()

        r = k - top

        @pl.when(jnp.logical_and(inner, jnp.logical_and(r >= 0, r < SUBS)))
        def _(r=r):
            along(r, 0).wait_recv()
            for i in range(parts - 1):
                add_line(r, jnp.where(cube.z == 1, 1, 0) + i, i)
            along(r, 1).start()

        r = k - top - 1

        @pl.when(jnp.logical_and(inner, jnp.logical_and(r >= 0, r < SUBS)))
        def _(r=r):
            along(r, 1).wait_recv()
            for i in range(2):
                add_line(r, mine + i, parts - 1 + i)
            along(r, 2).start()
            grads_ref[r] = line_ref[lax.rem(r, LINE), cube.z].astype(F32)

        r = k - top - 2

        @pl.when(jnp.logical_and(r >= 0, r < SUBS))
        def _(r=r):
            @pl.when(inner)
            def _():
                along(r, 1).wait_send()
                along(r, 2).wait_send()

            @pl.when(jnp.logical_not(inner))
            def _():
                along(r, 2).wait_recv()
                value = line_ref[lax.rem(r, LINE), cube.z].astype(F32)
                grads_ref[r] = value + zed_ref[r, 0].astype(F32)
                along(r, 0).wait_send()

    done = [0]

    def advances(last):
        if last > done[0]:
            first = done[0]
            loop(last - first, lambda i: advance(first + i))
            done[0] = last

    back_out = Rows(cube, row_send.at[0], row_recv.at[0], row_here.at[0])
    back_in = Rows(cube, row_send.at[1], row_recv.at[1], row_here.at[1])
    pieces = 8

    sums_ref[...] = jnp.zeros_like(sums_ref)
    sums_ref[3:6, :] = second_ref[0:3, :]

    b_load.start()
    gate_load[0].start()
    weight(8, 0).start()
    slope_load[0].start()
    gate_load[1].start()
    out_load.start()
    y_load.start()
    greet(cube.column() + cube.neighbours())
    b_load.wait()
    gate_load[0].wait()
    give(0, b_ref, pool.at[0])
    slope_load[1].start()
    weight(9, 1).start()
    dh_load.start()
    z_load.start()
    r_load.start()
    mixed_load.start()
    loop(2, lambda i: fetch(i).start())
    gate_load[1].wait()
    give(1, b_ref, pool.at[1])

    def gate_back(j):
        slope_load[j].wait()
        weight(8 + j, j % 2).wait()

        def part(z):
            lanes = chunk(z, cols)
            grad = dot_nn(b_ref[...], weight_tile(wbuf, j % 2, z))
            low = (grad * pool[2 + j % 2, :, lanes].astype(F32)).astype(BF)
            pool[4 + j, :, lanes] = low
            sums_ref[6 + j : 7 + j, lanes] = total_rows(low.astype(F32))

        loop(parts, part)

    gate_back(0)
    slope_load[2].start()
    weight(10, 0).start()
    hold(0, b_ref, pool.at[0])
    gate_load[2].start()

    out_load.wait()
    near_ref[1] = dot_nt(near_ref[0], cube.shuffle(width)).astype(BF)

    def send_out(piece):
        back_out.back(near_ref, 1, outputs_ref, piece, pieces)

    loop(2, send_out)
    loop(2, lambda i: send_out(2 + i))
    hold(1, b_ref, pool.at[1])
    gate_load[3].start()
    gate_load[2].wait()
    give(2, b_ref, pool.at[0])
    gate_back(1)
    slope_load[3].start()
    weight(11, 1).start()
    loop(2, lambda i: send_out(4 + i))
    gate_load[3].wait()
    give(3, b_ref, pool.at[1])
    hold(2, b_ref, pool.at[0])
    gate_back(2)
    weight(4, 0).start()
    loop(2, lambda i: send_out(6 + i))
    hold(3, b_ref, pool.at[1])
    advances(1)
    gate_back(3)
    weight(5, 1).start()
    qkv_load.start()
    other_load.start()

    def fold_up(j):
        weight(4 + j, j % 2).wait()

        def part(z):
            dh_ref[...] += dot_nt(pool[4 + j, :, chunk(z, cols)], weight_tile(wbuf, j % 2, z))

        loop(parts, part)

    dh_load.wait()
    fold_up(0)
    weight(6, 0).start()
    fold_up(1)
    weight(7, 1).start()
    fold_up(2)
    weight(3, 0).start()
    fold_up(3)

    z_load.wait()
    r_load.wait()

    def norm_first(i):
        at = chunk(i, size)
        grad = dh_ref[at, :]
        z = z1_ref[at, :]
        dh = norm_back(grad, z, r1_ref[at, 0:1], vector(vec_ref, FIRST_GAIN))
        dh_ref[at, :] = dh
        b_ref[at, :] = dh.astype(BF)
        sums_ref[0:1, :] += total_rows(grad * z)
        sums_ref[1:2, :] += total_rows(grad)
        sums_ref[2:3, :] += total_rows(dh)

    loop(rows // size, norm_first)
    mixed_load.wait()
    give(4, b_ref, mixed_ref)
    weight(3, 0).wait()
    dm = 3

    def mix_back(z):
        pool[dm, :, chunk(z, cols)] = dot_nn(b_ref[...], weight_tile(wbuf, 0, z)).astype(BF)

    loop(parts, mix_back)
    weight(2, 0).start()
    weight(0, 1).start()
    advances(2)
    hold(4, b_ref, mixed_ref)
    y_load.wait()

    qkv_load.wait()
    other_load.wait()

    def swap(pair):
        lanes = chunk(pair, 2 * HD)
        return remote(
            far_ref.at[lax.rem(pair, 4)],
            swap_ref.at[:, :, lanes],
            swap_send.at[pair],
            swap_recv.at[pair],
            {"dp": cube.place ^ 1, "tensor": cube.z},
        )

    def attend(pair):
        lanes = chunk(pair, 2 * HD)
        fetch(pair).wait()
        slot = lax.rem(pair, 2)
        q2, dm2 = pool[0, :, lanes], pool[dm, :, lanes]
        k2 = [pool[1, :, lanes], pool[8, :, lanes]]
        v2 = [pool[2, :, lanes], pool[9, :, lanes]]
        weighed = (dm2.astype(F32) * mixed_ref[:, lanes].astype(F32)).T
        dqs, dks, dvs = [], [[], []], [[], []]
        for head in range(2):
            part = slice(head * HD, head * HD + HD)
            q, dmix = q2[:, part], dm2[:, part]
            chance = [chance_ref[slot, head, i * rows : (i + 1) * rows, :] for i in range(2)]
            grads = [dot_nt(v[:, part], dmix) for v in v2]
            inner = total_rows(weighed[part, :])
            dq = None
            for i in range(2):
                ds = (chance[i].astype(F32) * (grads[i] - inner)).astype(BF)
                term = dot_tn(k2[i][:, part], ds)
                dq = term if dq is None else dq + term
                dks[i].append(dot_nn(ds, q))
                dvs[i].append(dot_nn(chance[i], dmix))
            dqs.append(dq)
        dq = jnp.concatenate(dqs, axis=0).T.astype(BF).astype(F32) * SCALE
        mixed_ref[:, lanes] = dq.astype(BF)
        sums_ref[10:11, lanes] = total_rows(dq)
        near_ref[0, :, lanes] = jnp.concatenate(dks[0], axis=1).astype(BF)
        near_ref[1, :, lanes] = jnp.concatenate(dvs[0], axis=1).astype(BF)

        @pl.when(pair >= 4)
        def _():
            swap(pair - 4).wait_send()

        far_ref[lax.rem(pair, 4), 0] = jnp.concatenate(dks[1], axis=1).astype(BF)
        far_ref[lax.rem(pair, 4), 1] = jnp.concatenate(dvs[1], axis=1).astype(BF)
        swap(pair).start()

        @pl.when(pair + 2 < pairs)
        def _():
            fetch(pair + 2).start()

    back_out.back_end(near_ref, 1, outputs_ref)
    loop(2, attend)
    give(5, y_ref, pool.at[4])
    advances(3)
    hold(5, y_ref, pool.at[4])
    loop(2, lambda i: attend(2 + i))
    give(6, y_ref, pool.at[5])
    advances(4)
    hold(6, y_ref, pool.at[5])
    loop(2, lambda i: attend(4 + i))
    give(7, y_ref, pool.at[6])
    advances(5)
    hold(7, y_ref, pool.at[6])
    loop(pairs - 6, lambda i: attend(6 + i))
    give(8, y_ref, pool.at[7])
    advances(6)
    hold(8, y_ref, pool.at[7])
    x_load.start()

    def both(pair):
        swap(pair).wait_recv()
        lanes = chunk(pair, 2 * HD)
        for i in range(2):
            total = near_ref[i, :, lanes].astype(F32) + swap_ref[i, :, lanes].astype(F32)
            low = total.astype(BF)
            near_ref[i, :, lanes] = low
            if i == 1:
                sums_ref[11:12, lanes] = total_rows(low.astype(F32))

    loop(pairs, both)
    x_load.wait()
    give(9, y_ref, mixed_ref)

    value = sums_ref[0:8, :]
    thirds = []
    for _ in range(3):
        thirds.append(value.astype(BF))
        value = value - thirds[-1].astype(F32)
    value = dot_nt(jnp.concatenate(thirds, axis=0), cube.shuffle(width))
    sums_ref[0:6, :] = (value[0:8] + value[8:16] + value[16:24])[0:6, :]

    rounds = [{"dp": p, "tensor": cube.z} for p in partners]
    rounds += [{"dp": cube.place, "tensor": cube.z ^ 1}, {"dp": cube.place, "tensor": cube.z ^ 2}]

    def pool_sums(i):
        return remote(sums_ref, sums_in.at[i], sum_send.at[i], sum_recv.at[i], rounds[i])

    def next_sum(i):
        if 0 < i <= len(rounds):
            pool_sums(i - 1).wait()
            sums_ref[...] += sums_in[i - 1]
        if i < len(rounds):
            pool_sums(i).start()

    next_sum(0)

    def fold_in(kind, slot, right):
        weight(kind, slot).wait()

        def part(z):
            value = dot_nt(right[:, chunk(z, cols)], weight_tile(wbuf, slot, z))
            dh_ref[...] += value

        loop(parts, part)

    fold_in(2, 0, mixed_ref)
    weight(1, 0).start()
    fold_in(0, 1, near_ref.at[0])
    next_sum(1)
    fold_in(1, 0, near_ref.at[1])
    loop(4, lambda i: swap(pairs - 4 + i).wait_send())
    pool[0] = dot_nt(dh_ref[...].astype(BF), cube.shuffle(width)).astype(BF)

    def send_in(piece):
        back_in.back(pool, 0, back_ref, piece, pieces)

    loop(2, send_in)
    next_sum(2)
    advances(7)
    give(10, y_ref, near_ref.at[1])
    hold(9, y_ref, mixed_ref)
    next_sum(3)
    loop(2, lambda i: send_in(2 + i))
    give(11, y_ref, near_ref.at[0])
    hold(10, y_ref, near_ref.at[1])
    next_sum(4)
    loop(2, lambda i: send_in(4 + i))
    advances(8)
    hold(11, y_ref, near_ref.at[0])
    loop(2, lambda i: send_in(6 + i))
    advances(9)
    for i in range(5, len(rounds) + 1):
        next_sum(i)
    advances(10)
    advances(11)
    advances(12)
    sums_out[...] = sums_ref[...]
    advances(SUBS + top + 2)

    for r in range(SUBS - RING, SUBS):
        stage(r, top).wait_send()
    back_in.back_end(pool, 0, back_ref)
    back_in.back_wait(pool, 0, back_ref)
    back_out.back_wait(near_ref, 1, outputs_ref)


def backward(second_sums, held, count, parts):
    (weights, vectors, x, qkv, other, mixed, chance, z1, r1, y1, gated, slope, normed_rows, dh2, b2) = held
    subs, _, _, depth, cols = weights.shape
    rows, width = x.shape
    levels = count.bit_length() - 1
    half = count // 2
    pairs = width // (2 * HD)
    dma = pltpu.SemaphoreType.DMA
    low = lambda *shape: (shape, BF)
    high = lambda *shape: (shape, F32)
    hbm = pl.BlockSpec(memory_space=pl.ANY)
    vmem = pl.BlockSpec(memory_space=pltpu.VMEM)
    results = [
        high(subs, depth, cols),
        high(16, width),
        low(2, rows // 2, width),
        low(2, rows // 2, width),
    ]
    scratch = [
        low(10, rows, width),
        low(2, 2, 2 * rows, rows),
        low(rows, width),
        high(rows, width),
        high(rows, width),
        high(rows, 128),
        low(rows, width),
        low(rows, width),
        low(2, rows, width),
        low(4, 2, rows, 2 * HD),
        low(2, rows, width),
        low(2, count, parts, depth, cols),
        low(RING, half, parts, depth, cols),
        low(RING, half, parts, depth, cols),
        low(HELD, half, parts, depth, cols),
        low(LINE, parts, depth, cols),
        low(subs, half - 1, parts, depth, cols),
        low(subs, parts + 1, depth, cols),
        high(16, width),
        high(levels + 2, 16, width),
    ]
    return pl.pallas_call(
        functools.partial(backward_kernel, count, parts),
        in_specs=[vmem, vmem] + [hbm] * 14,
        out_specs=[vmem, vmem, hbm, hbm],
        out_shape=[jax.ShapeDtypeStruct(*r) for r in results],
        scratch_shapes=[pltpu.VMEM(*s) for s in scratch]
        + [
            dma((15,)),
            dma((2,)),
            dma((2,)),
            pltpu.SemaphoreType.REGULAR,
            dma((subs, levels)),
            dma((subs, levels)),
            dma((subs, 3)),
            dma((subs, 3)),
            dma((pairs,)),
            dma((pairs,)),
            dma((2, 2)),
            dma((2, 2)),
            dma((2,)),
            dma((levels + 2,)),
            dma((levels + 2,)),
        ],
        compiler_params=pltpu.CompilerParams(
            collective_id=2, has_side_effects=True, vmem_limit_bytes=62 * MIB
        ),
    )(vectors, second_sums, weights, x, qkv, other, mixed, chance, z1, r1, y1, gated, slope, normed_rows, dh2, b2)


def result_kernel(
    rows_ref,
    back_ref,
    down_a,
    down_b,
    up_a,
    up_b,
    q_ref,
    k_ref,
    v_ref,
    o_ref,
    sums_ref,
    rows_out,
    input_out,
    down_out,
    up_out,
    q_out,
    k_out,
    v_out,
    o_out,
    *small,
):
    rows_out[...] = rows_ref[...]
    input_out[...] = back_ref[...].astype(F32)
    cols = up_a.shape[-1]
    for i, (down, up) in enumerate(((down_a, up_a), (down_b, up_b))):
        down_out[i * cols : (i + 1) * cols, :] = down[0].T
        up_out[:, i * cols : (i + 1) * cols] = up[0]

    @pl.when(pl.program_id(0) == 0)
    def _():
        for source, target in ((q_ref, q_out), (k_ref, k_out), (v_ref, v_out)):
            target[...] = source[0]
        o_out[...] = o_ref[0].T
        for i in range(6):
            small[i][...] = sums_ref[i : i + 1, :]
        mine = chunk(lax.axis_index("tensor"), cols)
        small[7][...] = sums_ref[10:11, mine]
        small[8][...] = sums_ref[11:12, mine]
        for i in range(4):
            small[6][:, i * cols : (i + 1) * cols] = sums_ref[6 + i : 7 + i, mine]


def results(grads, sums, outputs, back):
    _, depth, cols = grads.shape
    _, rows, width = outputs.shape
    steps = 2
    at = {sub: r for r, sub in enumerate(ORDER)}
    row_spec = pl.BlockSpec((2, rows // steps, width), lambda j: (0, j, 0))
    one = lambda r: pl.BlockSpec((1, depth, cols), lambda j: (r, 0, 0))
    run = lambda r: pl.BlockSpec((1, depth, cols), lambda j: (r + 2 * j, 0, 0))
    whole = lambda *shape: pl.BlockSpec(shape, lambda j: (0,) * len(shape))
    high = lambda *shape: jax.ShapeDtypeStruct(shape, F32)
    return pl.pallas_call(
        result_kernel,
        grid=(steps,),
        in_specs=[row_spec, row_spec]
        + [run(at[DOWN]), run(at[DOWN + 1]), run(at[UP]), run(at[UP + 1])]
        + [one(at[2]), one(at[0]), one(at[1]), one(at[3]), whole(*sums.shape)],
        out_specs=[
            row_spec,
            row_spec,
            pl.BlockSpec((2 * cols, depth), lambda j: (j, 0)),
            pl.BlockSpec((depth, 2 * cols), lambda j: (0, j)),
        ]
        + [whole(depth, cols)] * 3
        + [whole(cols, depth)]
        + [whole(1, width)] * 6
        + [whole(1, 4 * cols), whole(1, cols), whole(1, cols)],
        out_shape=[
            jax.ShapeDtypeStruct(outputs.shape, BF),
            high(*outputs.shape),
            high(4 * cols, depth),
            high(depth, 4 * cols),
        ]
        + [high(depth, cols)] * 3
        + [high(cols, depth)]
        + [high(1, width)] * 6
        + [high(1, 4 * cols), high(1, cols), high(1, cols)],
        compiler_params=pltpu.CompilerParams(vmem_limit_bytes=60 * MIB),
    )(outputs, back, *[grads] * 8, sums)


def shards(
    inputs,
    query_weight,
    query_bias,
    key_weight,
    value_weight,
    value_bias,
    out_weight,
    out_bias,
    first_gain,
    first_shift,
    up_weight,
    up_bias,
    down_weight,
    down_bias,
    second_gain,
    second_shift,
    cotangent,
):
    count, parts = lax.axis_size("dp"), lax.axis_size("tensor")
    flat = lambda *values: [value.reshape(1, -1) for value in values]
    *held, second_sums = forward(
        [query_weight, key_weight, value_weight, out_weight, up_weight, down_weight],
        flat(query_bias, value_bias, up_bias),
        flat(out_bias, first_gain, first_shift, down_bias, second_gain, second_shift),
        inputs,
        cotangent,
        count,
        parts,
    )
    grads, sums, outputs, back = backward(second_sums, held, count, parts)
    outputs, input_grad, down, up, query, key, value, out, *small = results(grads, sums, outputs, back)
    small = [row.reshape(-1) for row in small]
    return (
        outputs,
        input_grad,
        query,
        small[7],
        key,
        value,
        small[8],
        out,
        small[2],
        small[0],
        small[1],
        up,
        small[6],
        down,
        small[5],
        small[3],
        small[4],
    )


def solution(mesh):
    rows = P(None, ("dp", "tensor"), None)
    return jax.shard_map(
        shards,
        mesh=mesh,
        in_specs=(
            rows,
            P("dp", "tensor"),
            P("tensor"),
            P("dp", "tensor"),
            P("dp", "tensor"),
            P("tensor"),
            P("tensor", "dp"),
            P(),
            P(),
            P(),
            P("dp", "tensor"),
            P("tensor"),
            P("tensor", "dp"),
            P(),
            P(),
            P(),
            rows,
        ),
        out_specs=(
            rows,
            rows,
            P("dp", "tensor"),
            P("tensor"),
            P("dp", "tensor"),
            P("dp", "tensor"),
            P("tensor"),
            P("tensor", "dp"),
            P(),
            P(),
            P(),
            P("dp", "tensor"),
            P("tensor"),
            P("tensor", "dp"),
            P(),
            P(),
            P(),
        ),
        check_vma=False,
    )
```
